32 devices in a mesh: dp: 4 (over y, x), expert: 8 (over z, core).
Axes of the slice: x: 2, y: 2, z: 4, core: 2. Of those that a mesh axis runs over, the one named last changes fastest.
Arguments:
- tokens: bfloat16 [768, 7168], P(('dp', 'expert')), may hold values from -6 to 6
- grad_out: bfloat16 [768, 7168], P(('dp', 'expert')), may hold values from -6 to 6
- route_ids: int32 [768, 8], P(('dp', 'expert')), may hold values from 0 to 31, all different within a row; in each aligned block of 24 rows (0 to 23, 24 to 47, ...) at most 7 rows name the same one
- route_weight: bfloat16 [768, 8], P(('dp', 'expert')), may hold values from 0.049804688 to 1
- cluster_of: int32 [32], replicated, may hold values from 0 to 3, as said below
- gate_basis: bfloat16 [4, 512, 7168], P(None, 'expert', 'dp'), may hold values from -0.0625 to 0.0625
- up_basis: bfloat16 [4, 512, 7168], P(None, 'expert', 'dp'), may hold values from -0.0625 to 0.0625
- down_basis: bfloat16 [4, 512, 7168], P(None, 'expert', 'dp'), may hold values from -0.25 to 0.25
- gate_factor: bfloat16 [32, 512, 2048], P('expert', None, 'dp'), may hold values from -0.25 to 0.25
- up_factor: bfloat16 [32, 512, 2048], P('expert', None, 'dp'), may hold values from -0.25 to 0.25
- down_factor: bfloat16 [32, 2048, 512], P('expert', 'dp'), may hold values from -0.125 to 0.125
Outputs:
- grad_tokens: bfloat16 [768, 7168], P(('dp', 'expert'))
- grad_route: float32 [768, 8], P(('dp', 'expert'))
- grad_gate_basis: float32 [4, 512, 7168], P(None, 'expert', 'dp')
- grad_up_basis: float32 [4, 512, 7168], P(None, 'expert', 'dp')
- grad_down_basis: float32 [4, 512, 7168], P(None, 'expert', 'dp')
- grad_gate_factor: float32 [32, 512, 2048], P('expert', None, 'dp')
- grad_up_factor: float32 [32, 512, 2048], P('expert', None, 'dp')
- grad_down_factor: float32 [32, 2048, 512], P('expert', 'dp')
The draws below stay inside these ranges and needn't reach their ends.
Inputs may be any that keep to these rules, and one draw needn't show every extreme that they name: `route_ids`: each token names 8 different experts. Among the 24 tokens of one block no expert is named more than 7 times, and in every draw some expert is named exactly 7 times in some block. `cluster_of`: never falls from one expert to the next; all 4 experts of each group of 4 consecutive experts share one cluster; every cluster holds 1 to 3 such groups, and one holds exactly 3.
All inputs are finite; a program needn't handle non-finite values.
Results may differ from the reference program's by a relative error of at most 0.013.
Values may be sent and summed in bfloat16 or wider, within the bound.
No kernel may reach another device: no remote copies, remote signals or barrier semaphores. Data moves between devices by JAX's collectives and lax.ppermute only.
A program may use at most 128 MiB of HBM per device.

```python
import math
import jax
import jax.numpy as jnp
import numpy as np
from jax import lax

D = 7168
F = 2048
K = 8
R = 512
EXP_DEV = 4
TOK_DEV = 24
EXPERTS = 32
CLUSTERS = 4
CLUSTER_MOST = 3
CAP = 7
TOKENS = 768


def draw_cluster_of(key, part):
    key = jax.random.fold_in(key, 7)
    first_key, second_key = jax.random.split(key)
    groups = EXPERTS // EXP_DEV
    largest = jax.random.randint(first_key, (), 0, CLUSTERS)
    spare = groups - CLUSTER_MOST - (CLUSTERS - 1)
    picks = jax.random.randint(second_key, (spare,), 0, CLUSTERS - 1)
    picks = picks + (picks >= largest).astype(jnp.int32)
    counts = 1 + jnp.sum((picks[:, None] == jnp.arange(CLUSTERS, dtype=jnp.int32)[None, :]).astype(jnp.int32), axis=0)
    counts = jnp.where(jnp.arange(CLUSTERS, dtype=jnp.int32) == largest, CLUSTER_MOST, counts)
    ends = jnp.cumsum(counts)
    group_cluster = jnp.sum((jnp.arange(groups, dtype=jnp.int32)[:, None] >= ends[None, :]).astype(jnp.int32), axis=1)
    return jnp.repeat(group_cluster, EXP_DEV).astype(jnp.int32)


def levels(stream_key, dims, cuts, low, high):
    def one(axis_at, blocks):
        heights = jax.random.uniform(jax.random.fold_in(jax.random.fold_in(stream_key, 6), axis_at), (blocks,), jnp.float32, low / len(cuts), high / len(cuts))
        return jnp.repeat(jnp.exp(heights), dims[axis_at] // blocks).reshape((-1,) + (1,) * (len(dims) - axis_at - 1))

    gain = one(*cuts[0])
    for cut in cuts[1:]:
        gain = gain * one(*cut)
    return gain


def routed_block(key, own, number, rows, number_of, top, most, skew):
    ranking = jax.random.permutation(key, number_of)
    heavy_load, common = portions_of(number_of, rows * top, most, skew, True), portions_of(number_of, rows * top, most, skew, False)
    places = jnp.arange(number_of)

    def named(tallies, offset_by):
        used = int((tallies > 0).sum())
        fixed = max(1, used // 4)
        shifted = fixed + (places - fixed + offset_by * (used - fixed)) % max(1, number_of - fixed)
        return jnp.zeros((number_of,), jnp.int32).at[ranking[jnp.where(places < fixed, places, shifted)]].set(jnp.asarray(tallies, jnp.int32))

    tallies = jnp.where(number % 4 == 0, named(heavy_load, number // 4), named(common, number - number // 4 - 1))
    mixed = jax.random.permutation(jax.random.fold_in(own, 3), number_of)
    giver, receiver = mixed[0:number_of // 2 * 2:2], mixed[1:number_of // 2 * 2:2]
    room = jnp.minimum(tallies[giver] - 1, most - tallies[receiver]) // 2
    room = jnp.where((giver == ranking[0]) | (receiver == ranking[0]) | (tallies[receiver] == 0), 0, jnp.maximum(room, 0))
    shifted = jax.random.randint(jax.random.fold_in(own, 4), (number_of // 2,), 0, 1 << 20) % (room + 1)
    tallies = tallies.at[giver].add(-shifted).at[receiver].add(shifted)
    labels = jnp.searchsorted(jnp.cumsum(tallies), jnp.arange(rows * top), side="right").astype(jnp.int32)
    grid = labels.reshape(top, rows).T
    grid = grid[jax.random.permutation(jax.random.fold_in(own, 1), rows)]
    offset_by = jax.random.randint(jax.random.fold_in(own, 2), (rows, 1), 0, top)
    return jnp.take_along_axis(grid, (jnp.arange(top)[None, :] + offset_by) % top, axis=1)


def portions_of(amount, total, reach, lean, full):
    loads = [(1 << 20) // math.isqrt(standing ** lean) + 1 for standing in range(1, amount + 1)]
    largest = reach if full else min(reach, max(-(-total // amount), total * loads[0] // sum(loads)))
    least = 1 if total - largest >= amount - 1 else 0
    given, surplus = [largest] + [least] * (amount - 1), total - largest - least * (amount - 1)
    while surplus > 0:
        candidates = [i for i in range(1, amount) if given[i] < largest] or [i for i in range(1, amount) if given[i] < reach]
        pool, left = sum([loads[i] for i in candidates]), surplus
        for i in candidates:
            more = min(reach - given[i], max(1, left * loads[i] // pool), surplus)
            given[i] = given[i] + more
            surplus = surplus - more
    return np.array(given)


def noise(rng, shape, width, reach, shards=(), held_as=jnp.bfloat16):
    array = width * jax.random.normal(rng, shape, jnp.float32)
    if shards:
        array = array * levels(rng, shape, shards, -0.22, 0.18)
    return jnp.clip(array, -reach, reach).astype(held_as)


def setup_inputs(seed: int = 0) -> dict:
    keys = jax.random.split(jax.random.key(seed), 12)
    tokens = noise(keys[0], (TOKENS, D), 1.0, 6.0, ((0, 32),))
    grad_out = noise(keys[1], (TOKENS, D), 1.0, 6.0, ((0, 32),))
    route_ids_keys = jax.random.split(jax.random.fold_in(keys[2], 1), TOKENS // TOK_DEV)
    route_ids_turns = jax.random.permutation(jax.random.fold_in(keys[2], 3), TOKENS // TOK_DEV)
    route_ids = jax.vmap(lambda own, number: routed_block(jax.random.fold_in(keys[2], 2), own, number, TOK_DEV, EXPERTS, K, CAP, 2))(route_ids_keys, route_ids_turns).reshape((TOKENS, K))
    route_weight = jnp.clip(jnp.exp(math.log(1.0) - 2.9996462 * jax.random.uniform(keys[3], (TOKENS, K), jnp.float32) ** levels(keys[3], (TOKENS, K), ((0, 32),), -0.2, 0.2)), 0.049804688, 1.0).astype(jnp.bfloat16)
    cluster_of = draw_cluster_of(jax.random.fold_in(keys[11], 71), 0)
    gate_basis = noise(keys[5], (CLUSTERS, R, D), D ** -0.5, 0.0625, ((1, 8), (2, 4)))
    up_basis = noise(keys[6], (CLUSTERS, R, D), D ** -0.5, 0.0625, ((1, 8), (2, 4)))
    down_basis = noise(keys[7], (CLUSTERS, R, D), R ** -0.5, 0.25, ((1, 8), (2, 4)))
    gate_factor = noise(keys[8], (EXPERTS, R, F), R ** -0.5, 0.25, ((0, 8), (2, 4)))
    up_factor = noise(keys[9], (EXPERTS, R, F), R ** -0.5, 0.25, ((0, 8), (2, 4)))
    down_factor = noise(keys[10], (EXPERTS, F, R), F ** -0.5, 0.125, ((0, 8), (1, 4)))
    return {"tokens": tokens, "grad_out": grad_out, "route_ids": route_ids, "route_weight": route_weight, "cluster_of": cluster_of, "gate_basis": gate_basis, "up_basis": up_basis, "down_basis": down_basis, "gate_factor": gate_factor, "up_factor": up_factor, "down_factor": down_factor}


def rounded(value):
    return lax.optimization_barrier(value.astype(jnp.bfloat16))


def silu_pair(pre):
    sig = jax.nn.sigmoid(pre)
    return pre * sig, sig * (1.0 + pre * (1.0 - sig))


def reference(tokens, grad_out, route_ids, route_weight, cluster_of, gate_basis, up_basis, down_basis, gate_factor, up_factor, down_factor):
    blocks = TOKENS // TOK_DEV
    pairs = TOK_DEV * K
    block_ids = route_ids.reshape(blocks, pairs).astype(jnp.int32)
    matches = (block_ids[:, :, None] == jnp.arange(EXPERTS, dtype=jnp.int32)[None, None, :]).astype(jnp.int32)
    slot_rank = (jnp.sum(matches * jnp.cumsum(matches, axis=1), axis=2) - 1).astype(jnp.int32)
    block_index = jnp.broadcast_to(jnp.arange(blocks, dtype=jnp.int32)[:, None], (blocks, pairs))
    pair_index = jnp.arange(pairs, dtype=jnp.int32)[None, :]
    token_of = (block_index * TOK_DEV + pair_index // K).astype(jnp.int32)
    choice_of = jnp.broadcast_to(pair_index % K, (blocks, pairs)).astype(jnp.int32)
    table = jnp.full((EXPERTS, blocks, CAP), TOKENS, jnp.int32).at[block_ids, block_index, slot_rank].set(token_of)
    which = jnp.zeros((EXPERTS, blocks, CAP), jnp.int32).at[block_ids, block_index, slot_rank].set(choice_of)
    weights = jnp.zeros((EXPERTS, blocks, CAP), jnp.float32).at[block_ids, block_index, slot_rank].set(
        route_weight.reshape(blocks, pairs).astype(jnp.float32))
    tokens_pad = jnp.concatenate([tokens, jnp.zeros((1, D), tokens.dtype)], axis=0)
    grads_pad = jnp.concatenate([grad_out, jnp.zeros((1, D), grad_out.dtype)], axis=0)
    groups = EXPERTS // EXP_DEV
    fl = jnp.float32

    def group_step(carry, device):
        grad_tok, grad_rt, grad_bases = carry
        first = (device * EXP_DEV).astype(jnp.int32)
        token_index = lax.dynamic_slice_in_dim(table, first, EXP_DEV, 0).reshape(EXP_DEV, blocks * CAP)
        k_index = lax.dynamic_slice_in_dim(which, first, EXP_DEV, 0).reshape(EXP_DEV, blocks * CAP)
        slot_weight = lax.dynamic_slice_in_dim(weights, first, EXP_DEV, 0).reshape(EXP_DEV, blocks * CAP)
        cluster = cluster_of[first]
        x_rows = tokens_pad[token_index].astype(fl)
        dy_rows = grads_pad[token_index].astype(fl)
        gate_rows = gate_basis[cluster].astype(fl)
        up_rows = up_basis[cluster].astype(fl)
        down_rows = down_basis[cluster].astype(fl)
        gate_own = lax.dynamic_slice_in_dim(gate_factor, first, EXP_DEV, 0).astype(fl)
        up_own = lax.dynamic_slice_in_dim(up_factor, first, EXP_DEV, 0).astype(fl)
        down_own = lax.dynamic_slice_in_dim(down_factor, first, EXP_DEV, 0).astype(fl)
        rank_gate = rounded(jnp.einsum('emd,rd->emr', x_rows, gate_rows)).astype(fl)
        rank_up = rounded(jnp.einsum('emd,rd->emr', x_rows, up_rows)).astype(fl)
        gate_pre = jnp.einsum('emr,erf->emf', rank_gate, gate_own)
        up_pre = jnp.einsum('emr,erf->emf', rank_up, up_own)
        act, slope = silu_pair(gate_pre)
        hidden = rounded(act * up_pre).astype(fl)
        mixed = rounded(jnp.einsum('emf,efr->emr', hidden, down_own)).astype(fl)
        y_rows = jnp.einsum('emr,rd->emd', mixed, down_rows)
        dots = jnp.sum(y_rows * dy_rows, axis=2)
        upstream = rounded(slot_weight[:, :, None] * dy_rows).astype(fl)
        term_down = jnp.einsum('emr,emd->rd', mixed, upstream)
        grad_mixed = rounded(jnp.einsum('emd,rd->emr', upstream, down_rows)).astype(fl)
        grad_down_own = jnp.einsum('emf,emr->efr', hidden, grad_mixed)
        grad_hidden = jnp.einsum('emr,efr->emf', grad_mixed, down_own)
        grad_gate_pre = rounded(grad_hidden * up_pre * slope).astype(fl)
        grad_up_pre = rounded(grad_hidden * act).astype(fl)
        grad_gate_own = jnp.einsum('emr,emf->erf', rank_gate, grad_gate_pre)
        grad_up_own = jnp.einsum('emr,emf->erf', rank_up, grad_up_pre)
        grad_hg = rounded(jnp.einsum('emf,erf->emr', grad_gate_pre, gate_own)).astype(fl)
        grad_hu = rounded(jnp.einsum('emf,erf->emr', grad_up_pre, up_own)).astype(fl)
        term_gate = jnp.einsum('emr,emd->rd', grad_hg, x_rows)
        term_up = jnp.einsum('emr,emd->rd', grad_hu, x_rows)
        grad_x = rounded(jnp.einsum('emr,rd->emd', grad_hg, gate_rows) + jnp.einsum('emr,rd->emd', grad_hu, up_rows)).astype(fl)
        terms = rounded(jnp.stack([term_gate, term_up, term_down])).astype(fl)
        grad_bases = grad_bases.at[cluster].add(terms)
        flat_index = token_index.reshape(-1)
        grad_tok = grad_tok.at[flat_index].add(grad_x.reshape(-1, D))
        grad_rt = grad_rt.at[flat_index, k_index.reshape(-1)].add(dots.reshape(-1))
        return (grad_tok, grad_rt, grad_bases), (grad_gate_own, grad_up_own, grad_down_own)

    start = (jnp.zeros((TOKENS + 1, D), jnp.float32), jnp.zeros((TOKENS + 1, K), jnp.float32),
             jnp.zeros((CLUSTERS, 3, R, D), jnp.float32))
    carry, owned = lax.scan(group_step, start, jnp.arange(groups, dtype=jnp.int32))
    grad_tok, grad_rt, grad_bases = carry
    grad_gate_factor = owned[0].reshape(EXPERTS, R, F)
    grad_up_factor = owned[1].reshape(EXPERTS, R, F)
    grad_down_factor = owned[2].reshape(EXPERTS, F, R)
    return (grad_tok[:TOKENS].astype(jnp.bfloat16), grad_rt[:TOKENS], grad_bases[:, 0], grad_bases[:, 1],
            grad_bases[:, 2], grad_gate_factor, grad_up_factor, grad_down_factor)
```

```python
import jax
import jax.numpy as jnp
from jax import lax
from jax.sharding import Mesh
from jax.sharding import PartitionSpec as P

FL = jnp.float32
BF = jnp.bfloat16


def silu_pair(pre):
    sig = jax.nn.sigmoid(pre)
    return (pre * sig, sig * (1.0 + pre * (1.0 - sig)))


def mm(spec, a, b):
    return jnp.einsum(spec, a, b, preferred_element_type=FL)


def core_swap(value):
    return lax.ppermute(value, "core", [(0, 1), (1, 0)])


def core_join(value):
    other = core_swap(value)
    first = lax.axis_index("core") == 0
    return jnp.stack([jnp.where(first, value, other), jnp.where(first, other, value)])


def gather_columns(rows, n_dp):
    tok_rows, width = rows.shape
    part = width // n_dp
    pieces = jnp.concatenate([rows[:, i * part : (i + 1) * part] for i in range(n_dp)], axis=0)
    pieces = lax.all_to_all(pieces, "dp", split_axis=0, concat_axis=0, tiled=True)
    along = lax.all_gather(pieces, "ez", axis=0, tiled=True)
    return core_join(along).reshape(-1, part)


def dp_scatter_sum(value):
    got = lax.all_to_all(value.astype(BF), "dp", split_axis=0, concat_axis=0, tiled=True)
    return jnp.sum(got.astype(FL), axis=0)


def body(
    tokens,
    grad_out,
    route_ids,
    route_weight,
    cluster_of,
    gate_basis,
    up_basis,
    down_basis,
    gate_factor,
    up_factor,
    down_factor,
):
    n_dp = lax.axis_size("dp")
    n_z = lax.axis_size("ez")
    n_ex = n_z * 2
    me_e = lax.axis_index("ez") * 2 + lax.axis_index("core")
    tok_rows, model_width = tokens.shape
    top = route_ids.shape[1]
    local = gate_factor.shape[0]
    experts = local * n_ex
    capacity = max(2, 5 * tok_rows * top // (4 * experts))
    blocks = n_dp * n_ex
    total = blocks * tok_rows
    slots = blocks * capacity
    clusters, rank_own, width = gate_basis.shape
    rank = gate_factor.shape[1]
    rank_part = rank_own // n_dp

    def everywhere(value):
        got = lax.all_gather(value, ("dp", "ez", "core"), axis=0, tiled=False)
        got = got.reshape(n_dp, n_z, 2, tok_rows, top)
        return got.transpose(2, 1, 0, 3, 4).reshape(blocks, tok_rows, top)

    ids = everywhere(route_ids)
    weights = everywhere(route_weight).astype(FL)
    own_ids = me_e * local + jnp.arange(local, dtype=jnp.int32)
    hit = ids[None] == own_ids[:, None, None, None]
    named = jnp.any(hit, axis=3)
    weight_of = jnp.sum(jnp.where(hit, weights[None], 0.0), axis=3)
    order = jnp.cumsum(named.astype(jnp.int32), axis=2) - 1
    cell = jnp.arange(blocks, dtype=jnp.int32)[None, :, None] * capacity + order
    cell = jnp.where(named, cell, -1).reshape(local, 1, total)
    placed = cell == jnp.arange(slots, dtype=jnp.int32)[None, :, None]
    weight_of = weight_of.reshape(local, 1, total)
    pick = placed.astype(BF).reshape(local * slots, total)
    pick_weighted = jnp.where(placed, weight_of, 0.0).astype(BF).reshape(local * slots, total)
    slot_weight = jnp.sum(jnp.where(placed, weight_of, 0.0), axis=2, keepdims=True)

    group_cluster = cluster_of.reshape(n_ex, local)[:, 0]

    def to_groups(rows, bases):
        count = len(bases)
        parts = [
            mm("rf,tf->rt", basis.reshape(clusters * rank_own, width), rows).reshape(
                clusters, n_dp, rank_part, total
            )
            for basis in bases
        ]
        terms = jnp.stack(parts)
        mine = dp_scatter_sum(terms.transpose(2, 0, 1, 3, 4)).astype(BF)
        send = jnp.take(mine, group_cluster, axis=1)
        send = send.transpose(1, 0, 2, 3)
        got = lax.all_to_all(send, ("ez", "core"), split_axis=0, concat_axis=0, tiled=True)
        full = lax.all_gather(got, "dp", axis=0, tiled=False)
        full = full.transpose(2, 1, 0, 3, 4).reshape(count, rank, total)
        return [full[i] for i in range(count)]

    x_cols = gather_columns(tokens, n_dp)
    dy_cols = gather_columns(grad_out, n_dp)
    hg_rows, hu_rows = to_groups(x_cols, [gate_basis, up_basis])
    (hd_rows,) = to_groups(dy_cols, [down_basis])

    def to_slots(rows):
        return mm("nt,rt->nr", pick, rows).astype(BF).reshape(local, slots, rank)

    hg = to_slots(hg_rows)
    hu = to_slots(hu_rows)
    hd = to_slots(hd_rows)
    gate_pre = mm("jnr,jrf->jnf", hg, gate_factor)
    up_pre = mm("jnr,jrf->jnf", hu, up_factor)
    act, slope = silu_pair(gate_pre)
    hidden = (act * up_pre).astype(BF)
    mixed = mm("jnf,jfr->jnr", hidden, down_factor)
    dots = jnp.sum(mixed * hd.astype(FL), axis=2, keepdims=True)
    grad_mixed = (slot_weight * hd.astype(FL)).astype(BF)
    grad_hidden = mm("jnr,jfr->jnf", grad_mixed, down_factor)
    grad_gate_pre = (grad_hidden * up_pre * slope).astype(BF)
    grad_up_pre = (grad_hidden * act).astype(BF)
    grad_down_factor = mm("jnf,jnr->jfr", hidden, grad_mixed)
    grad_gate_factor = mm("jnr,jnf->jrf", hg, grad_gate_pre)
    grad_up_factor = mm("jnr,jnf->jrf", hu, grad_up_pre)
    grad_hg = mm("jnf,jrf->jnr", grad_gate_pre, gate_factor).astype(BF)
    grad_hu = mm("jnf,jrf->jnr", grad_up_pre, up_factor).astype(BF)

    def from_groups(terms):
        count = len(terms)
        value = jnp.stack(terms).reshape(count, n_ex, n_dp, rank_part, total)
        mine = dp_scatter_sum(value.transpose(2, 1, 0, 3, 4)).astype(BF)
        got = lax.all_to_all(mine, ("ez", "core"), split_axis=0, concat_axis=0, tiled=True)
        owner = group_cluster[None, :] == jnp.arange(clusters, dtype=jnp.int32)[:, None]
        summed = jnp.sum(
            jnp.where(owner[:, :, None, None, None], got.astype(FL)[None], 0.0), axis=1
        ).astype(BF)
        full = lax.all_gather(summed, "dp", axis=0, tiled=False)
        full = full.transpose(2, 1, 0, 3, 4).reshape(count, clusters * rank_own, total)
        return [full[i] for i in range(count)]

    flat = lambda value: value.reshape(local * slots, rank)
    (sum_mixed,) = from_groups([mm("nr,nt->rt", flat(mixed.astype(BF)), pick_weighted)])
    sum_gate, sum_up = from_groups(
        [mm("nr,nt->rt", flat(grad_hg), pick), mm("nr,nt->rt", flat(grad_hu), pick)]
    )
    shape = (clusters, rank_own, width)
    grad_down_basis = mm("rt,tf->rf", sum_mixed, dy_cols).reshape(shape)
    grad_gate_basis = mm("rt,tf->rf", sum_gate, x_cols).reshape(shape)
    grad_up_basis = mm("rt,tf->rf", sum_up, x_cols).reshape(shape)

    grad_x = mm("rt,rf->tf", sum_gate, gate_basis.reshape(-1, width)) + mm(
        "rt,rf->tf", sum_up, up_basis.reshape(-1, width)
    )
    halves = grad_x.reshape(2, total // 2, width)
    core = lax.axis_index("core")
    keep = jnp.where(core == 0, halves[0], halves[1])
    give = jnp.where(core == 0, halves[1], halves[0]).astype(BF)
    half = (keep + core_swap(give).astype(FL)).astype(BF)
    got = lax.all_to_all(half, "ez", split_axis=0, concat_axis=0, tiled=True)
    mine = jnp.sum(got.reshape(n_z, n_dp * tok_rows, width).astype(FL), axis=0).astype(BF)
    mine = lax.all_to_all(mine, "dp", split_axis=0, concat_axis=0, tiled=True)
    grad_tokens = jnp.concatenate(
        [mine[i * tok_rows : (i + 1) * tok_rows] for i in range(n_dp)], axis=1
    )

    scores = jnp.sum(jnp.where(placed, dots, 0.0), axis=1)
    scores = scores.reshape(local, 2, n_z, n_dp, tok_rows).transpose(3, 2, 1, 0, 4)
    scores = scores.reshape(blocks, local, tok_rows)
    back = lax.all_to_all(scores, ("dp", "ez", "core"), split_axis=0, concat_axis=0, tiled=True)
    by_expert = jnp.sum(back.reshape(n_dp, experts, tok_rows), axis=0)
    chosen = route_ids[:, :, None] == jnp.arange(experts, dtype=jnp.int32)[None, None, :]
    grad_route = jnp.sum(jnp.where(chosen, by_expert.T[:, None, :], 0.0), axis=2)
    return (
        grad_tokens,
        grad_route,
        grad_gate_basis,
        grad_up_basis,
        grad_down_basis,
        grad_gate_factor,
        grad_up_factor,
        grad_down_factor,
    )


def solution(mesh):
    n_dp, n_ex = mesh.shape["dp"], mesh.shape["expert"]
    split = Mesh(mesh.devices.reshape(n_dp, n_ex // 2, 2), ("dp", "ez", "core"))
    ex = ("ez", "core")
    rows = P(("dp", "ez", "core"), None)
    basis = P(None, ex, "dp")
    in_specs = (
        rows,
        rows,
        rows,
        rows,
        P(),
        basis,
        basis,
        basis,
        P(ex, None, "dp"),
        P(ex, None, "dp"),
        P(ex, "dp", None),
    )
    out_specs = (
        rows,
        rows,
        basis,
        basis,
        basis,
        P(ex, None, "dp"),
        P(ex, None, "dp"),
        P(ex, "dp", None),
    )
    return jax.shard_map(body, mesh=split, in_specs=in_specs, out_specs=out_specs, check_vma=False)
```

```python
import jax
import jax.numpy as jnp
from jax import lax
from jax.sharding import Mesh
from jax.sharding import PartitionSpec as P

FL = jnp.float32
BF = jnp.bfloat16


def silu_pair(pre):
    sig = jax.nn.sigmoid(pre)
    return (pre * sig, sig * (1.0 + pre * (1.0 - sig)))


def mm(spec, a, b):
    return jnp.einsum(spec, a, b, preferred_element_type=FL)


def core_swap(value):
    return lax.ppermute(value, "core", [(0, 1), (1, 0)])


def in_order(pieces, me):
    bit = 1
    while bit < len(pieces):
        odd = (me & bit) != 0
        pieces = [
            jnp.where(odd, pieces[j ^ bit], pieces[j]) for j in range(len(pieces))
        ]
        bit *= 2
    return pieces


def trade(chunk_for, axis):
    n = lax.axis_size(axis)
    sent = [lax.ppermute(chunk_for(k), axis, [(i, i ^ k) for i in range(n)]) for k in range(1, n)]
    return [chunk_for(0)] + sent


def gather_z(share):
    n = lax.axis_size("ez")
    if n != 4:
        got = trade(lambda k: share, "ez")
        return got, got[-1]
    near = lax.ppermute(share, "ez", [(0, 1), (1, 0), (2, 3), (3, 2)])
    far = lax.ppermute(share, "ez", [(0, 2), (2, 0), (1, 3), (3, 1)])
    inner = lax.ppermute(share, "ez", [(1, 2), (2, 1)])
    ends = lax.ppermute(far, "ez", [(2, 3), (1, 0)])
    z = lax.axis_index("ez")
    last = jnp.where((z == 1) | (z == 2), inner, ends)
    return [share, near, far, last], (near, far, inner)


def scatter_z(share_of):
    n = lax.axis_size("ez")
    if n != 4:
        got = trade(lambda k: share_of(k).astype(BF), "ez")
        return share_of(0) + sum(piece.astype(FL) for piece in got[1:])
    third = share_of(3).astype(BF)
    ends = lax.ppermute(third, "ez", [(0, 1), (3, 2)])
    near = lax.ppermute(share_of(1).astype(BF), "ez", [(0, 1), (1, 0), (2, 3), (3, 2)])
    inner = lax.ppermute(third, "ez", [(1, 2), (2, 1)])
    second = (share_of(2) + ends.astype(FL)).astype(BF)
    far = lax.ppermute(second, "ez", [(0, 2), (2, 0), (1, 3), (3, 1)])
    return share_of(0) + near.astype(FL) + inner.astype(FL) + far.astype(FL)


def body(
    tokens,
    grad_out,
    route_ids,
    route_weight,
    cluster_of,
    gate_basis,
    up_basis,
    down_basis,
    gate_factor,
    up_factor,
    down_factor,
):
    n_dp = lax.axis_size("dp")
    n_z = lax.axis_size("ez")
    n_ex = n_z * 2
    dp = lax.axis_index("dp")
    z = lax.axis_index("ez")
    core = lax.axis_index("core")
    me_e = z * 2 + core
    tok_rows, model_width = tokens.shape
    top = route_ids.shape[1]
    local = gate_factor.shape[0]
    experts = local * n_ex
    capacity = max(2, 5 * tok_rows * top // (4 * experts))
    blocks = n_dp * n_ex
    total = blocks * tok_rows
    half = total // 2
    share = n_dp * tok_rows
    slots = blocks * capacity
    clusters, rank_own, width = gate_basis.shape
    rank = gate_factor.shape[1]
    parts_core = n_dp // 2
    rank_part = rank_own // parts_core

    def own_columns(rows):
        pieces = trade(
            lambda k: lax.dynamic_slice_in_dim(rows, (dp ^ k) * width, width, 1), "dp"
        )
        return jnp.concatenate(in_order(pieces, dp), axis=0)

    def join_z(pieces):
        whole = jnp.zeros((n_z, share, width), BF)
        for k, piece in enumerate(pieces):
            whole = lax.dynamic_update_index_in_dim(whole, piece, z ^ k, 0)
        return whole.reshape(half, width)

    x_share = own_columns(tokens)
    dy_share = own_columns(grad_out)
    x_pieces, x_most = gather_z(x_share)
    dy_share, _ = lax.optimization_barrier((dy_share, x_most))
    dy_pieces, _ = gather_z(dy_share)
    x_half = join_z(x_pieces)
    dy_half = join_z(dy_pieces)

    def chip_rows(bases):
        own = jnp.stack(bases, axis=1)
        other = core_swap(own)
        count = len(bases)
        own = own.reshape(clusters, count, parts_core, rank_part, width)
        other = other.reshape(clusters, count, parts_core, rank_part, width)
        result = []
        for k in range(n_dp):
            part = dp ^ k
            at = part % parts_core
            mine = lax.dynamic_index_in_dim(own, at, 2, False)
            theirs = lax.dynamic_index_in_dim(other, at, 2, False)
            rows = jnp.where(part // parts_core == core, mine, theirs)
            result.append(rows.reshape(clusters * count * rank_part, width))
        return result

    rows_in = chip_rows([gate_basis, up_basis])
    rows_out = chip_rows([down_basis])

    routing = jnp.concatenate([route_ids.astype(FL), route_weight.astype(FL)], axis=1)
    routing = jnp.broadcast_to(routing[None], (blocks, tok_rows, 2 * top))
    routing = lax.all_to_all(routing, ("dp", "ez", "core"), split_axis=0, concat_axis=0, tiled=True)
    routing = routing.reshape(n_dp, n_z, 2, tok_rows, 2 * top).transpose(2, 1, 0, 3, 4)
    routing = routing.reshape(blocks, tok_rows, 2 * top)
    ids = routing[:, :, :top].astype(jnp.int32)
    weights = routing[:, :, top:]
    own_ids = me_e * local + jnp.arange(local, dtype=jnp.int32)
    hit = ids[None] == own_ids[:, None, None, None]
    named = jnp.any(hit, axis=3)
    weight_of = jnp.sum(jnp.where(hit, weights[None], 0.0), axis=3)
    order = jnp.cumsum(named.astype(jnp.int32), axis=2) - 1
    cell = jnp.arange(blocks, dtype=jnp.int32)[None, :, None] * capacity + order
    cell = jnp.where(named, cell, -1).reshape(local, 1, total)
    placed = cell == jnp.arange(slots, dtype=jnp.int32)[None, :, None]
    weight_of = weight_of.reshape(local, 1, total)
    pick = placed.astype(BF).reshape(local * slots, total)
    pick_weighted = jnp.where(placed, weight_of, 0.0).astype(BF).reshape(local * slots, total)
    slot_weight = jnp.sum(jnp.where(placed, weight_of, 0.0), axis=2, keepdims=True)

    group_cluster = cluster_of.reshape(n_ex, local)[:, 0]

    def to_groups(cols, rows, count):
        terms = [mm("rf,tf->rt", part, cols) for part in rows]
        got = trade(lambda k: terms[k].astype(BF), "dp")
        mine = terms[0] + sum(piece.astype(FL) for piece in got[1:])
        mine = mine.astype(BF).reshape(clusters, count * rank_part, half)
        send = mine.at[group_cluster].get(mode="promise_in_bounds")
        got = lax.all_to_all(send, ("ez", "core"), split_axis=0, concat_axis=0, tiled=True)
        pieces = in_order(trade(lambda k: got, "dp"), dp)
        full = jnp.stack(pieces).reshape(n_dp, n_z, 2, count, rank_part, half)
        full = full.transpose(3, 1, 0, 4, 2, 5).reshape(count, rank, total)
        return [full[i] for i in range(count)]

    hg_rows, hu_rows = to_groups(x_half, rows_in, 2)
    (hd_rows,) = to_groups(dy_half, rows_out, 1)

    def to_slots(rows):
        return mm("nt,rt->nr", pick, rows).astype(BF).reshape(local, slots, rank)

    hg = to_slots(hg_rows)
    hu = to_slots(hu_rows)
    hd = to_slots(hd_rows)
    gate_pre = mm("jnr,jrf->jnf", hg, gate_factor)
    up_pre = mm("jnr,jrf->jnf", hu, up_factor)
    act, slope = silu_pair(gate_pre)
    hidden = (act * up_pre).astype(BF)
    mixed = mm("jnf,jfr->jnr", hidden, down_factor)
    dots = jnp.sum(mixed * hd.astype(FL), axis=2, keepdims=True)
    grad_mixed = (slot_weight * hd.astype(FL)).astype(BF)
    grad_hidden = mm("jnr,jfr->jnf", grad_mixed, down_factor)
    grad_gate_pre = (grad_hidden * up_pre * slope).astype(BF)
    grad_up_pre = (grad_hidden * act).astype(BF)
    grad_down_factor = mm("jnf,jnr->jfr", hidden, grad_mixed)
    grad_gate_factor = mm("jnr,jnf->jrf", hg, grad_gate_pre)
    grad_up_factor = mm("jnr,jnf->jrf", hu, grad_up_pre)
    grad_hg = mm("jnf,jrf->jnr", grad_gate_pre, gate_factor).astype(BF)
    grad_hu = mm("jnf,jrf->jnr", grad_up_pre, up_factor).astype(BF)

    def from_groups(terms):
        count = len(terms)
        value = jnp.stack(terms).reshape(count, n_z, n_dp, rank_part, 2, half)
        chunk = lambda k: lax.dynamic_index_in_dim(value, dp ^ k, 2, False)
        got = trade(lambda k: chunk(k).astype(BF), "dp")
        mine = chunk(0) + sum(piece.astype(FL) for piece in got[1:])
        mine = mine.astype(BF).transpose(1, 3, 0, 2, 4)
        mine = mine.reshape(n_ex, count, rank_part, half)
        got = lax.all_to_all(mine, ("ez", "core"), split_axis=0, concat_axis=0, tiled=True)
        owner = group_cluster[None, :] == jnp.arange(clusters, dtype=jnp.int32)[:, None]
        summed = jnp.sum(
            jnp.where(owner[:, :, None, None, None], got.astype(FL)[None], 0.0), axis=1
        ).astype(BF)
        summed = summed.reshape(clusters * count * rank_part, half)
        return trade(lambda k: summed, "dp")

    flat = lambda value: value.reshape(local * slots, rank)
    mixed_parts = from_groups([mm("nr,nt->rt", flat(mixed.astype(BF)), pick_weighted)])
    in_parts = from_groups(
        [mm("nr,nt->rt", flat(grad_hg), pick), mm("nr,nt->rt", flat(grad_hu), pick)]
    )

    grad_x = sum(mm("rt,rf->tf", part, rows) for part, rows in zip(in_parts, rows_in))
    shares = grad_x.reshape(n_z, share, width)
    mine = scatter_z(lambda k: lax.dynamic_index_in_dim(shares, z ^ k, 0, False)).astype(BF)
    pieces = trade(
        lambda k: lax.dynamic_slice_in_dim(mine, (dp ^ k) * tok_rows, tok_rows, 0), "dp"
    )
    grad_tokens = jnp.concatenate(in_order(pieces, dp), axis=1)

    def both_cores(value, axis):
        other = core_swap(value)
        first = core == 0
        return jnp.concatenate(
            [jnp.where(first, value, other), jnp.where(first, other, value)], axis=axis
        )

    x_all = both_cores(x_half, 0)
    dy_all = both_cores(dy_half, 0)

    def own_ranks(parts, count):
        whole = jnp.stack(in_order(parts, dp))
        whole = whole.reshape(2, parts_core, clusters, count, rank_part, half)
        keep = jnp.where(core == 0, whole[0], whole[1])
        give = jnp.where(core == 0, whole[1], whole[0])
        other = core_swap(give)
        first = core == 0
        rows = jnp.stack([jnp.where(first, keep, other), jnp.where(first, other, keep)])
        rows = rows.transpose(3, 2, 1, 4, 0, 5)
        return rows.reshape(count, clusters * rank_own, total)

    shape = (clusters, rank_own, width)
    (sum_mixed,) = own_ranks(mixed_parts, 1)
    sum_gate, sum_up = own_ranks(in_parts, 2)
    grad_down_basis = mm("rt,tf->rf", sum_mixed, dy_all).reshape(shape)
    grad_gate_basis = mm("rt,tf->rf", sum_gate, x_all).reshape(shape)
    grad_up_basis = mm("rt,tf->rf", sum_up, x_all).reshape(shape)

    scores = jnp.sum(jnp.where(placed, dots, 0.0), axis=1)
    scores = scores.reshape(local, 2, n_z, n_dp, tok_rows).transpose(3, 2, 1, 0, 4)
    scores = scores.reshape(blocks, local, tok_rows)
    back = lax.all_to_all(scores, ("dp", "ez", "core"), split_axis=0, concat_axis=0, tiled=True)
    by_expert = jnp.sum(back.reshape(n_dp, experts, tok_rows), axis=0)
    chosen = route_ids[:, :, None] == jnp.arange(experts, dtype=jnp.int32)[None, None, :]
    grad_route = jnp.sum(jnp.where(chosen, by_expert.T[:, None, :], 0.0), axis=2)
    return (
        grad_tokens,
        grad_route,
        grad_gate_basis,
        grad_up_basis,
        grad_down_basis,
        grad_gate_factor,
        grad_up_factor,
        grad_down_factor,
    )


def solution(mesh):
    n_dp, n_ex = mesh.shape["dp"], mesh.shape["expert"]
    split = Mesh(mesh.devices.reshape(n_dp, n_ex // 2, 2), ("dp", "ez", "core"))
    ex = ("ez", "core")
    rows = P(("dp", "ez", "core"), None)
    basis = P(None, ex, "dp")
    in_specs = (
        rows,
        rows,
        rows,
        rows,
        P(),
        basis,
        basis,
        basis,
        P(ex, None, "dp"),
        P(ex, None, "dp"),
        P(ex, "dp", None),
    )
    out_specs = (
        rows,
        rows,
        basis,
        basis,
        basis,
        P(ex, None, "dp"),
        P(ex, None, "dp"),
        P(ex, "dp", None),
    )
    return jax.shard_map(body, mesh=split, in_specs=in_specs, out_specs=out_specs, check_vma=False)
```

```python
import jax
import jax.numpy as jnp
from jax import lax
from jax.experimental import pallas as pl
from jax.experimental.pallas import tpu as pltpu
from jax.sharding import Mesh
from jax.sharding import PartitionSpec as P

FL = jnp.float32
BF = jnp.bfloat16
VMEM = pltpu.VMEM


def mm(spec, a, b):
    return jnp.einsum(spec, a, b, preferred_element_type=FL)


def dot(a, b, a_dim, b_dim):
    return lax.dot_general(a, b, (((a_dim,), (b_dim,)), ((), ())), preferred_element_type=FL)


def after(value, first):
    mark = lax.slice(first, (0,) * first.ndim, (1,) * first.ndim).reshape(()).astype(FL) * 0.0
    return value + mark.astype(value.dtype)


def core_swap(value):
    return lax.ppermute(value, "core", [(0, 1), (1, 0)])


def in_order(pieces, me):
    bit = 1
    while bit < len(pieces):
        odd = (me & bit) != 0
        pieces = [
            jnp.where(odd, pieces[j ^ bit], pieces[j]) for j in range(len(pieces))
        ]
        bit *= 2
    return pieces


def trade(chunk_for, axis):
    n = lax.axis_size(axis)
    sent = [lax.ppermute(chunk_for(k), axis, [(i, i ^ k) for i in range(n)]) for k in range(1, n)]
    return [chunk_for(0)] + sent


def gather_z(share):
    n = lax.axis_size("ez")
    if n != 4:
        return trade(lambda k: share, "ez")
    far = lax.ppermute(share, "ez", [(0, 2), (2, 0), (1, 3), (3, 1)])
    near = lax.ppermute(share, "ez", [(0, 1), (1, 0), (2, 3), (3, 2)])
    inner = lax.ppermute(share, "ez", [(1, 2), (2, 1)])
    ends = lax.ppermute(far, "ez", [(2, 3), (1, 0)])
    return [share, near, far, inner, ends]


def scatter_z(share_of):
    n = lax.axis_size("ez")
    if n != 4:
        got = trade(lambda k: share_of(k).astype(BF), "ez")
        return share_of(0) + sum(piece.astype(FL) for piece in got[1:])
    third = share_of(3).astype(BF)
    ends = lax.ppermute(third, "ez", [(0, 1), (3, 2)])
    near = lax.ppermute(share_of(1).astype(BF), "ez", [(0, 1), (1, 0), (2, 3), (3, 2)])
    inner = lax.ppermute(third, "ez", [(1, 2), (2, 1)])
    second = (share_of(2) + ends.astype(FL)).astype(BF)
    far = lax.ppermute(second, "ez", [(0, 2), (2, 0), (1, 3), (3, 1)])
    return share_of(0) + near.astype(FL) + inner.astype(FL) + far.astype(FL)


def whole(array):
    return pl.BlockSpec(array.shape, lambda *_: (0,) * array.ndim, memory_space=VMEM)


def each(array):
    shape = (1,) + array.shape[1:]
    return pl.BlockSpec(shape, lambda j: (j,) + (0,) * (array.ndim - 1), memory_space=VMEM)


SCALAR = pl.BlockSpec(memory_space=pltpu.SMEM)
ANYWHERE = pl.BlockSpec(memory_space=pl.ANY)


def params(total):
    return pltpu.CompilerParams(vmem_limit_bytes=(8 + total * 15 // 1024) << 20)


def shaped(shape, kind):
    return jax.ShapeDtypeStruct(shape, kind)


def project(pieces, parts, z, n_z, first):
    share, width = pieces[0].shape
    half = n_z * share

    def kernel(z_ref, *refs):
        got, rest = refs[: len(pieces)], refs[len(pieces) :]
        bases, rest = rest[: len(parts)], rest[len(parts) :]
        cols, products = rest[1], rest[2:]
        me = z_ref[0]
        for k in range(n_z):
            at = pl.multiple_of((me ^ k) * share, 16)
            piece = got[k][...]
            if k == 3 and len(pieces) > n_z:
                middle = jnp.logical_or(me == 1, me == 2)
                piece = jnp.where(middle, piece, got[4][...])
            cols[pl.ds(at, share), :] = piece
        for base, product in zip(bases, products):
            product[...] = dot(base[...], cols[...], 1, 1).astype(BF)

    outs = [shaped((half, width), BF)] + [shaped((part.shape[0], half), BF) for part in parts]
    return pl.pallas_call(
        kernel,
        out_shape=outs,
        in_specs=[SCALAR]
        + [whole(piece) for piece in pieces]
        + [whole(part) for part in parts]
        + [ANYWHERE],
        out_specs=[whole(out) for out in outs],
        compiler_params=params(2 * half),
        cost_estimate=pl.CostEstimate(
            flops=2 * half * width * sum(part.shape[0] for part in parts),
            bytes_accessed=8 << 20,
            transcendentals=0,
        ),
        name="project",
    )(z.reshape(1), *pieces, *parts, first)


def make_picks(cell, weight, slots):
    local, _, total = cell.shape

    def kernel(cell_ref, weight_ref, pick_ref, heavy_ref, slot_ref):
        hit = cell_ref[0] == lax.broadcasted_iota(jnp.int32, (slots, total), 0)
        heavy = jnp.where(hit, weight_ref[0], 0.0)
        pick_ref[0] = jnp.where(hit, 1.0, 0.0).astype(BF)
        heavy_ref[0] = heavy.astype(BF)
        slot_ref[0] = jnp.sum(heavy, axis=1, keepdims=True)

    outs = [
        shaped((local, slots, total), BF),
        shaped((local, slots, total), BF),
        shaped((local, slots, 1), FL),
    ]
    return pl.pallas_call(
        kernel,
        grid=(local,),
        out_shape=outs,
        in_specs=[each(cell), each(weight)],
        out_specs=[each(out) for out in outs],
        compiler_params=params(total),
        cost_estimate=pl.CostEstimate(
            flops=6 * local * slots * total,
            bytes_accessed=4 * local * slots * total,
            transcendentals=0,
        ),
        name="make_picks",
    )(cell, weight)


def lay_out(pieces, target, me, count):
    n_dp = len(pieces)
    n_ex, rows, half = pieces[0].shape
    part = rows // count
    for k in range(n_dp):
        for e in range(n_ex):
            at = pl.multiple_of(((e // 2) * n_dp + (me ^ k)) * part, part)
            for b in range(count):
                piece = pieces[k][e, b * part : (b + 1) * part, :]
                target[b, pl.ds(at, part), (e % 2) * half : (e % 2 + 1) * half] = piece.astype(
                    target.dtype
                )


def rows_kind(part):
    return BF if part % 16 == 0 else FL


def hand_out(source, pieces, me, count):
    n_dp = len(pieces)
    n_ex, rows, half = pieces[0].shape
    part = rows // count
    for k in range(n_dp):
        for e in range(n_ex):
            at = pl.multiple_of(((e // 2) * n_dp + (me ^ k)) * part, part)
            for b in range(count):
                pieces[k][e, b * part : (b + 1) * part, :] = source[
                    b, pl.ds(at, part), (e % 2) * half : (e % 2 + 1) * half
                ].astype(BF)


def forward(pieces, pick, heavy, gate_factor, up_factor, down_factor, dp):
    n_dp = len(pieces)
    n_ex, rows, half = pieces[0].shape
    local, slots, total = pick.shape
    rank, hid = gate_factor.shape[1:]

    def kernel(dp_ref, *refs):
        got, refs = refs[:n_dp], refs[n_dp:]
        pick_ref, heavy_ref, gate_ref, up_ref, down_ref = refs[:5]
        hg_ref, hu_ref, hidden_ref, mixed_ref, act_ref, lift_ref = refs[5:11]
        sent = refs[11 : 11 + n_dp]
        rows_ref, total_ref = refs[11 + n_dp :]
        j = pl.program_id(0)
        me = dp_ref[0]

        @pl.when(j == 0)
        def _():
            lay_out(got, rows_ref, me, 2)
            total_ref[...] = jnp.zeros_like(total_ref)

        take = pick_ref[0]
        hg = dot(take, rows_ref[0].astype(BF), 1, 1).astype(BF)
        hu = dot(take, rows_ref[1].astype(BF), 1, 1).astype(BF)
        hg_ref[0] = hg
        hu_ref[0] = hu
        gate_pre = dot(hg, gate_ref[0], 1, 0)
        up_pre = dot(hu, up_ref[0], 1, 0)
        sig = 1.0 / (1.0 + jnp.exp(-gate_pre))
        act = gate_pre * sig
        act_ref[0] = act
        lift_ref[0] = up_pre * (sig * (1.0 + gate_pre * (1.0 - sig)))
        hidden = (act * up_pre).astype(BF)
        hidden_ref[0] = hidden
        mixed = dot(hidden, down_ref[0], 1, 0).astype(BF)
        mixed_ref[0] = mixed
        total_ref[0] += dot(mixed, heavy_ref[0], 0, 0)

        @pl.when(j == local - 1)
        def _():
            hand_out(total_ref, sent, me, 1)

    slot_shape = (local, slots, rank)
    hid_shape = (local, slots, hid)
    outs = [
        shaped(slot_shape, BF),
        shaped(slot_shape, BF),
        shaped(hid_shape, BF),
        shaped(slot_shape, BF),
        shaped(hid_shape, FL),
        shaped(hid_shape, FL),
    ]
    chunks = [shaped((n_ex, rows // 2, half), BF)] * n_dp
    got = pl.pallas_call(
        kernel,
        grid=(local,),
        out_shape=outs + chunks,
        in_specs=[SCALAR]
        + [whole(piece) for piece in pieces]
        + [each(x) for x in (pick, heavy, gate_factor, up_factor, down_factor)],
        out_specs=[each(out) for out in outs] + [whole(chunk) for chunk in chunks],
        scratch_shapes=[pltpu.VMEM((2, rank, total), rows_kind(rows // 2)), pltpu.VMEM((1, rank, total), FL)],
        compiler_params=params(total),
        cost_estimate=pl.CostEstimate(
            flops=local * slots * rank * (6 * total + 6 * hid),
            bytes_accessed=16 << 20,
            transcendentals=local * slots * hid,
        ),
        name="forward",
    )(dp.reshape(1), *pieces, pick, heavy, gate_factor, up_factor, down_factor)
    return got[:6], got[6:]


def backward(pieces, pick, weight, mixed, act, lift, gate_factor, up_factor, down_factor, dp):
    n_dp = len(pieces)
    n_ex, rows, half = pieces[0].shape
    local, slots, total = pick.shape
    rank, hid = gate_factor.shape[1:]

    def kernel(dp_ref, *refs):
        got, refs = refs[:n_dp], refs[n_dp:]
        pick_ref, weight_ref, mixed_ref, act_ref, lift_ref = refs[:5]
        gate_ref, up_ref, down_ref = refs[5:8]
        back_ref, gate_out, up_out, dots_ref = refs[8:12]
        sent = refs[12 : 12 + n_dp]
        rows_ref, total_ref = refs[12 + n_dp :]
        j = pl.program_id(0)
        me = dp_ref[0]

        @pl.when(j == 0)
        def _():
            lay_out(got, rows_ref, me, 1)
            total_ref[...] = jnp.zeros_like(total_ref)

        take = pick_ref[0]
        hd = dot(take, rows_ref[0].astype(BF), 1, 1)
        dots_ref[0] = jnp.sum(mixed_ref[0].astype(FL) * hd, axis=1, keepdims=True)
        back = (weight_ref[0] * hd).astype(BF)
        back_ref[0] = back
        grad_hidden = dot(back, down_ref[0], 1, 1)
        grad_gate = (grad_hidden * lift_ref[0]).astype(BF)
        grad_up = (grad_hidden * act_ref[0]).astype(BF)
        gate_out[0] = grad_gate
        up_out[0] = grad_up
        total_ref[0] += dot(dot(grad_gate, gate_ref[0], 1, 1).astype(BF), take, 0, 0)
        total_ref[1] += dot(dot(grad_up, up_ref[0], 1, 1).astype(BF), take, 0, 0)

        @pl.when(j == local - 1)
        def _():
            hand_out(total_ref, sent, me, 2)

    outs = [
        shaped((local, slots, rank), BF),
        shaped((local, slots, hid), BF),
        shaped((local, slots, hid), BF),
        shaped((local, slots, 1), FL),
    ]
    chunks = [shaped((n_ex, 2 * rows, half), BF)] * n_dp
    ins = (pick, weight, mixed, act, lift, gate_factor, up_factor, down_factor)
    got = pl.pallas_call(
        kernel,
        grid=(local,),
        out_shape=outs + chunks,
        in_specs=[SCALAR] + [whole(piece) for piece in pieces] + [each(x) for x in ins],
        out_specs=[each(out) for out in outs] + [whole(chunk) for chunk in chunks],
        scratch_shapes=[pltpu.VMEM((1, rank, total), rows_kind(rows)), pltpu.VMEM((2, rank, total), FL)],
        compiler_params=params(total),
        cost_estimate=pl.CostEstimate(
            flops=local * slots * rank * (6 * total + 6 * hid),
            bytes_accessed=16 << 20,
            transcendentals=0,
        ),
        name="backward",
    )(dp.reshape(1), *pieces, *ins)
    return got[:4], got[4:]


def factor_grads(hg, grad_gate, hu, grad_up, hidden, back, total):
    local, slots, rank = hg.shape
    hid = hidden.shape[2]

    def kernel(hg_ref, gate_ref, hu_ref, up_ref, hidden_ref, back_ref, out_g, out_u, out_d):
        out_g[0] = dot(hg_ref[0], gate_ref[0], 0, 0)
        out_u[0] = dot(hu_ref[0], up_ref[0], 0, 0)
        out_d[0] = dot(hidden_ref[0], back_ref[0], 0, 0)

    outs = [
        shaped((local, rank, hid), FL),
        shaped((local, rank, hid), FL),
        shaped((local, hid, rank), FL),
    ]
    ins = (hg, grad_gate, hu, grad_up, hidden, back)
    return pl.pallas_call(
        kernel,
        grid=(local,),
        out_shape=outs,
        in_specs=[each(x) for x in ins],
        out_specs=[each(out) for out in outs],
        compiler_params=params(total),
        cost_estimate=pl.CostEstimate(
            flops=6 * local * slots * rank * hid,
            bytes_accessed=18 << 20,
            transcendentals=0,
        ),
        name="factor_grads",
    )(*ins)


def body(
    tokens,
    grad_out,
    route_ids,
    route_weight,
    cluster_of,
    gate_basis,
    up_basis,
    down_basis,
    gate_factor,
    up_factor,
    down_factor,
):
    n_dp = lax.axis_size("dp")
    n_z = lax.axis_size("ez")
    n_ex = n_z * 2
    dp = lax.axis_index("dp")
    z = lax.axis_index("ez")
    core = lax.axis_index("core")
    me_e = z * 2 + core
    tok_rows = tokens.shape[0]
    top = route_ids.shape[1]
    local = gate_factor.shape[0]
    experts = local * n_ex
    capacity = max(2, 5 * tok_rows * top // (4 * experts))
    blocks = n_dp * n_ex
    total = blocks * tok_rows
    half = total // 2
    share = n_dp * tok_rows
    slots = blocks * capacity
    clusters, rank_own, width = gate_basis.shape
    parts_core = n_dp // 2
    rank_part = rank_own // parts_core

    def own_columns(rows):
        pieces = trade(
            lambda k: lax.dynamic_slice_in_dim(rows, (dp ^ k) * width, width, 1), "dp"
        )
        return jnp.concatenate(in_order(pieces, dp), axis=0)

    x_share = own_columns(tokens)
    x_pieces = gather_z(x_share)
    dy_share = own_columns(after(grad_out, x_share))
    dy_pieces = gather_z(after(dy_share, x_pieces[3]))

    def chip_rows(bases):
        own = after(jnp.stack(bases, axis=1), x_share)
        other = core_swap(own)
        count = len(bases)
        own = own.reshape(clusters, count, parts_core, rank_part, width)
        other = other.reshape(clusters, count, parts_core, rank_part, width)
        result = []
        for k in range(n_dp):
            part = dp ^ k
            at = part % parts_core
            mine = lax.dynamic_index_in_dim(own, at, 2, False)
            theirs = lax.dynamic_index_in_dim(other, at, 2, False)
            rows = jnp.where(part // parts_core == core, mine, theirs)
            result.append(rows.reshape(clusters * count * rank_part, width))
        return result

    rows_in = chip_rows([gate_basis, up_basis])
    rows_out = chip_rows([down_basis])

    routing = jnp.concatenate([route_ids.astype(FL), route_weight.astype(FL)], axis=1)
    routing = after(routing, x_share)
    routing = jnp.broadcast_to(routing[None], (blocks, tok_rows, 2 * top))
    routing = lax.all_to_all(routing, ("dp", "ez", "core"), split_axis=0, concat_axis=0, tiled=True)
    routing = after(routing, x_pieces[2])
    routing = routing.reshape(n_dp, n_z, 2, tok_rows, 2 * top).transpose(2, 1, 0, 3, 4)
    routing = routing.reshape(blocks, tok_rows, 2 * top)
    ids = routing[:, :, :top].astype(jnp.int32)
    weights = routing[:, :, top:]
    own_ids = me_e * local + jnp.arange(local, dtype=jnp.int32)
    hit = ids[None] == own_ids[:, None, None, None]
    named = jnp.any(hit, axis=3)
    weight_of = jnp.sum(jnp.where(hit, weights[None], 0.0), axis=3)
    order = jnp.cumsum(named.astype(jnp.int32), axis=2) - 1
    cell = jnp.arange(blocks, dtype=jnp.int32)[None, :, None] * capacity + order
    cell = jnp.where(named, cell, -1).reshape(local, 1, total)
    pick, heavy, slot_weight = make_picks(cell, weight_of.reshape(local, 1, total), slots)

    group_cluster = cluster_of.reshape(n_ex, local)[:, 0]

    def sum_parts(got):
        return sum(piece.astype(FL) for piece in got).astype(BF)

    def to_group(mine):
        mine = mine.reshape(clusters, -1, half)
        send = mine.at[group_cluster].get(mode="promise_in_bounds")
        return lax.all_to_all(send, ("ez", "core"), split_axis=0, concat_axis=0, tiled=True)

    x_half, *terms = project(x_pieces, rows_in, z, n_z, x_share)
    mine_in = sum_parts(trade(lambda k: terms[k], "dp"))
    got_in = to_group(mine_in)
    dy_half, *terms_out = project(dy_pieces, rows_out, z, n_z, mine_in)
    mine_out = sum_parts(trade(lambda k: terms_out[k], "dp"))
    got_out = to_group(after(mine_out, got_in))
    h_pieces = trade(lambda k: got_in, "dp")
    (hg, hu, hidden, mixed, act, lift), mixed_chunks = forward(
        h_pieces, pick, heavy, gate_factor, up_factor, down_factor, dp
    )
    d_pieces = trade(lambda k: got_out, "dp")
    (back, grad_gate, grad_up, dots), in_chunks = backward(
        d_pieces, pick, slot_weight, mixed, act, lift, gate_factor, up_factor, down_factor, dp
    )

    owner = group_cluster[None, :] == jnp.arange(clusters, dtype=jnp.int32)[:, None]

    def from_groups(mine):
        got = lax.all_to_all(mine, ("ez", "core"), split_axis=0, concat_axis=0, tiled=True)
        return jnp.sum(
            jnp.where(owner[:, :, None, None], got.astype(FL)[None], 0.0), axis=1
        ).astype(BF).reshape(-1, half)

    mixed_mine = sum_parts(trade(lambda k: mixed_chunks[k], "dp"))
    in_mine = sum_parts(trade(lambda k: in_chunks[k], "dp"))
    in_sum = from_groups(in_mine)
    mixed_sum = after(from_groups(mixed_mine), in_mine)
    in_parts = trade(lambda k: in_sum, "dp")
    mixed_parts = trade(lambda k: mixed_sum, "dp")
    grad_gate_factor, grad_up_factor, grad_down_factor = factor_grads(
        hg, grad_gate, hu, grad_up, hidden, back, total
    )

    grad_x = sum(mm("rt,rf->tf", part, rows) for part, rows in zip(in_parts, rows_in))
    shares = grad_x.reshape(n_z, share, width)
    mine = scatter_z(lambda k: lax.dynamic_index_in_dim(shares, z ^ k, 0, False)).astype(BF)
    pieces = trade(
        lambda k: lax.dynamic_slice_in_dim(mine, (dp ^ k) * tok_rows, tok_rows, 0), "dp"
    )
    grad_tokens = jnp.concatenate(in_order(pieces, dp), axis=1)

    def both_cores(value, axis):
        other = core_swap(value)
        first = core == 0
        return jnp.concatenate(
            [jnp.where(first, value, other), jnp.where(first, other, value)], axis=axis
        )

    x_all = both_cores(x_half, 0)
    dy_all = both_cores(dy_half, 0)

    def own_ranks(parts, count):
        stack = jnp.stack(in_order(parts, dp))
        stack = stack.reshape(2, parts_core, clusters, count, rank_part, half)
        keep = jnp.where(core == 0, stack[0], stack[1])
        give = jnp.where(core == 0, stack[1], stack[0])
        other = core_swap(give)
        first = core == 0
        rows = jnp.stack([jnp.where(first, keep, other), jnp.where(first, other, keep)])
        rows = rows.transpose(3, 2, 1, 4, 0, 5)
        return rows.reshape(count, clusters * rank_own, total)

    shape = (clusters, rank_own, width)
    (sum_mixed,) = own_ranks(mixed_parts, 1)
    sum_gate, sum_up = own_ranks(in_parts, 2)
    grad_down_basis = mm("rt,tf->rf", sum_mixed, dy_all).reshape(shape)
    grad_gate_basis = mm("rt,tf->rf", sum_gate, x_all).reshape(shape)
    grad_up_basis = mm("rt,tf->rf", sum_up, x_all).reshape(shape)

    placed = cell == jnp.arange(slots, dtype=jnp.int32)[None, :, None]
    scores = jnp.sum(jnp.where(placed, after(dots, in_mine), 0.0), axis=1)
    scores = scores.reshape(local, 2, n_z, n_dp, tok_rows).transpose(3, 2, 1, 0, 4)
    scores = scores.reshape(blocks, local, tok_rows)
    returned = lax.all_to_all(
        scores, ("dp", "ez", "core"), split_axis=0, concat_axis=0, tiled=True
    )
    by_expert = jnp.sum(returned.reshape(n_dp, experts, tok_rows), axis=0)
    chosen = route_ids[:, :, None] == jnp.arange(experts, dtype=jnp.int32)[None, None, :]
    grad_route = jnp.sum(jnp.where(chosen, by_expert.T[:, None, :], 0.0), axis=2)
    return (
        grad_tokens,
        grad_route,
        grad_gate_basis,
        grad_up_basis,
        grad_down_basis,
        grad_gate_factor,
        grad_up_factor,
        grad_down_factor,
    )


def solution(mesh):
    n_dp, n_ex = mesh.shape["dp"], mesh.shape["expert"]
    split = Mesh(mesh.devices.reshape(n_dp, n_ex // 2, 2), ("dp", "ez", "core"))
    ex = ("ez", "core")
    rows = P(("dp", "ez", "core"), None)
    basis = P(None, ex, "dp")
    in_specs = (
        rows,
        rows,
        rows,
        rows,
        P(),
        basis,
        basis,
        basis,
        P(ex, None, "dp"),
        P(ex, None, "dp"),
        P(ex, "dp", None),
    )
    out_specs = (
        rows,
        rows,
        basis,
        basis,
        basis,
        P(ex, None, "dp"),
        P(ex, None, "dp"),
        P(ex, "dp", None),
    )
    return jax.shard_map(body, mesh=split, in_specs=in_specs, out_specs=out_specs, check_vma=False)
```

```python
import functools

import jax
import jax.numpy as jnp
from jax import lax
from jax.experimental import pallas as pl
from jax.experimental.pallas import tpu as pltpu
from jax.sharding import Mesh
from jax.sharding import PartitionSpec as P

FL = jnp.float32
BF = jnp.bfloat16
VMEM = pltpu.VMEM


def mm(spec, a, b):
    return jnp.einsum(spec, a, b, preferred_element_type=FL)


def dot(a, b, a_dim, b_dim):
    return lax.dot_general(a, b, (((a_dim,), (b_dim,)), ((), ())), preferred_element_type=FL)


def after(value, first):
    mark = lax.slice(first, (0,) * first.ndim, (1,) * first.ndim).reshape(()).astype(FL) * 0.0
    return value + mark.astype(value.dtype)


def core_swap(value):
    return lax.ppermute(value, "core", [(0, 1), (1, 0)])


def in_order(pieces, me):
    bit = 1
    while bit < len(pieces):
        odd = (me & bit) != 0
        pieces = [
            jnp.where(odd, pieces[j ^ bit], pieces[j]) for j in range(len(pieces))
        ]
        bit *= 2
    return pieces


def trade(chunk_for, axis):
    n = lax.axis_size(axis)
    sent = [lax.ppermute(chunk_for(k), axis, [(i, i ^ k) for i in range(n)]) for k in range(1, n)]
    return [chunk_for(0)] + sent


def gather_z(share):
    n = lax.axis_size("ez")
    if n != 4:
        return trade(lambda k: share, "ez")
    far = lax.ppermute(share, "ez", [(0, 2), (2, 0), (1, 3), (3, 1)])
    near = lax.ppermute(share, "ez", [(0, 1), (1, 0), (2, 3), (3, 2)])
    inner = lax.ppermute(share, "ez", [(1, 2), (2, 1)])
    ends = lax.ppermute(far, "ez", [(2, 3), (1, 0)])
    return [share, near, far, inner, ends]


def scatter_z(share_of):
    n = lax.axis_size("ez")
    if n != 4:
        got = trade(lambda k: share_of(k).astype(BF), "ez")
        return share_of(0) + sum(piece.astype(FL) for piece in got[1:])
    third = share_of(3).astype(BF)
    ends = lax.ppermute(third, "ez", [(0, 1), (3, 2)])
    near = lax.ppermute(share_of(1).astype(BF), "ez", [(0, 1), (1, 0), (2, 3), (3, 2)])
    inner = lax.ppermute(third, "ez", [(1, 2), (2, 1)])
    second = (share_of(2) + ends.astype(FL)).astype(BF)
    far = lax.ppermute(second, "ez", [(0, 2), (2, 0), (1, 3), (3, 1)])
    return share_of(0) + near.astype(FL) + inner.astype(FL) + far.astype(FL)


def whole(array):
    return pl.BlockSpec(array.shape, lambda *_: (0,) * array.ndim, memory_space=VMEM)


def each(array):
    shape = (1,) + array.shape[1:]
    return pl.BlockSpec(shape, lambda j: (j,) + (0,) * (array.ndim - 1), memory_space=VMEM)


SCALAR = pl.BlockSpec(memory_space=pltpu.SMEM)
ANYWHERE = pl.BlockSpec(memory_space=pl.ANY)


def params():
    return pltpu.CompilerParams(vmem_limit_bytes=56 << 20)


def shaped(shape, kind):
    return jax.ShapeDtypeStruct(shape, kind)


def place_rows(own, other, target, part, at_core, low, same):
    count = len(own)

    def fill(source):
        for c in range(own[0].shape[0]):
            for b in range(count):
                to = (c * count + b) * part
                target[to : to + part, :] = source[b][c, pl.ds(low, part), :]

    pl.when(same == (at_core == 0))(functools.partial(fill, own))
    pl.when(same != (at_core == 0))(functools.partial(fill, other))


def project(pieces, rows, own, other, spot, n_dp, n_z, first):
    share, width = pieces[0].shape
    half = n_z * share
    bases = list(own) + list(other)
    count = len(own)
    clusters, rank_own, _ = own[0].shape
    parts_core = n_dp // 2
    part = rank_own // parts_core
    row_count = clusters * count * part
    built = rows is None

    def kernel(spot_ref, *refs):
        got, refs = refs[: len(pieces)], refs[len(pieces) :]
        z, dp, core = spot_ref[0], spot_ref[1], spot_ref[2]
        if built:
            ours, theirs = refs[:count], refs[count : 2 * count]
            cols, parts, products = refs[2 * count + 1], refs[2 * count + 2 :][:n_dp], refs[-n_dp:]
            for k in range(n_dp):
                low = pl.multiple_of((lax.rem(dp, parts_core) ^ (k % parts_core)) * part, part)
                same = core == dp // parts_core
                place_rows(ours, theirs, parts[k], part, k // parts_core, low, same)
        else:
            parts, cols, products = refs[:n_dp], refs[n_dp + 1], refs[-n_dp:]
        for k in range(n_z):
            at = pl.multiple_of((z ^ k) * share, 16)
            piece = got[k][...]
            if k == 3 and len(pieces) > n_z:
                middle = jnp.logical_or(z == 1, z == 2)
                piece = jnp.where(middle, piece, got[4][...])
            cols[pl.ds(at, share), :] = piece
        for base, product in zip(parts, products):
            product[...] = dot(base[...], cols[...], 1, 1).astype(BF)

    ins = list(pieces) + (bases if built else list(rows))
    outs = [shaped((half, width), BF)]
    if built:
        outs += [shaped((row_count, width), BF)] * n_dp
    outs += [shaped((row_count, half), BF)] * n_dp
    got = pl.pallas_call(
        kernel,
        out_shape=outs,
        in_specs=[SCALAR] + [whole(x) for x in ins] + [ANYWHERE],
        out_specs=[whole(out) for out in outs],
        compiler_params=params(),
        cost_estimate=pl.CostEstimate(
            flops=2 * half * width * n_dp * row_count,
            bytes_accessed=8 << 20,
            transcendentals=0,
        ),
        name="project",
    )(spot, *ins, first)
    return got[0], (got[1 : 1 + n_dp] if built else rows), got[-n_dp:]


def basis_grads(keep, other, cols, other_cols, spot, shape, n_dp):
    clusters, rank_own, width = shape
    parts_core = n_dp // 2
    part = rank_own // parts_core
    half = cols.shape[0]
    count = keep[0].shape[0] // (clusters * part)
    block = 256 if width % 256 == 0 else width

    def kernel(spot_ref, *refs):
        ours, theirs = refs[:parts_core], refs[parts_core : 2 * parts_core]
        cols_ref, other_ref = refs[2 * parts_core : 2 * parts_core + 2]
        outs, rows_ref = refs[-1 - count : -1], refs[-1]
        dp = spot_ref[1]

        @pl.when(pl.program_id(0) == 0)
        def _():
            for k in range(parts_core):
                low = (lax.rem(dp, parts_core) ^ k) * part
                for c in range(clusters):
                    at = pl.multiple_of(c * rank_own + low, part)
                    for b in range(count):
                        take = slice((c * count + b) * part, (c * count + b + 1) * part)
                        kind = rows_ref.dtype
                        rows_ref[0, b, pl.ds(at, part), :] = ours[k][take, :].astype(kind)
                        rows_ref[1, b, pl.ds(at, part), :] = theirs[k][take, :].astype(kind)

        for b in range(count):
            total = dot(rows_ref[0, b].astype(BF), cols_ref[...], 1, 0)
            total += dot(rows_ref[1, b].astype(BF), other_ref[...], 1, 0)
            outs[b][...] = total

    ins = list(keep) + list(other)
    out = shaped((clusters * rank_own, width), FL)
    strip = pl.BlockSpec((half, block), lambda j: (0, j), memory_space=VMEM)
    got = pl.pallas_call(
        kernel,
        grid=(width // block,),
        out_shape=[out] * count,
        in_specs=[SCALAR] + [whole(x) for x in ins] + [strip, strip],
        out_specs=[
            pl.BlockSpec((clusters * rank_own, block), lambda j: (0, j), memory_space=VMEM)
        ]
        * count,
        scratch_shapes=[pltpu.VMEM((2, count, clusters * rank_own, half), rows_kind(part))],
        compiler_params=params(),
        cost_estimate=pl.CostEstimate(
            flops=4 * count * clusters * rank_own * half * width,
            bytes_accessed=(3 + 2 * count) << 20,
            transcendentals=0,
        ),
        name="basis_grads",
    )(spot, *ins, cols, other_cols)
    return [grad.reshape(shape) for grad in got]


def make_picks(cell, weight, slots):
    local, _, total = cell.shape

    def kernel(cell_ref, weight_ref, pick_ref, heavy_ref, slot_ref):
        hit = cell_ref[0] == lax.broadcasted_iota(jnp.int32, (slots, total), 0)
        heavy = jnp.where(hit, weight_ref[0], 0.0)
        pick_ref[0] = jnp.where(hit, 1.0, 0.0).astype(BF)
        heavy_ref[0] = heavy.astype(BF)
        slot_ref[0] = jnp.sum(heavy, axis=1, keepdims=True)

    outs = [
        shaped((local, slots, total), BF),
        shaped((local, slots, total), BF),
        shaped((local, slots, 1), FL),
    ]
    return pl.pallas_call(
        kernel,
        grid=(local,),
        out_shape=outs,
        in_specs=[each(cell), each(weight)],
        out_specs=[each(out) for out in outs],
        compiler_params=params(),
        cost_estimate=pl.CostEstimate(
            flops=6 * local * slots * total,
            bytes_accessed=4 * local * slots * total,
            transcendentals=0,
        ),
        name="make_picks",
    )(cell, weight)


def lay_out(pieces, target, me, count):
    n_dp = len(pieces)
    n_ex, rows, half = pieces[0].shape
    part = rows // count
    for k in range(n_dp):
        for e in range(n_ex):
            at = pl.multiple_of(((e // 2) * n_dp + (me ^ k)) * part, part)
            for b in range(count):
                piece = pieces[k][e, b * part : (b + 1) * part, :]
                target[b, pl.ds(at, part), (e % 2) * half : (e % 2 + 1) * half] = piece.astype(
                    target.dtype
                )


def rows_kind(part):
    return BF if part % 16 == 0 else FL


def hand_out(source, pieces, me, count):
    n_dp = len(pieces)
    n_ex, rows, half = pieces[0].shape
    part = rows // count
    for k in range(n_dp):
        for e in range(n_ex):
            at = pl.multiple_of(((e // 2) * n_dp + (me ^ k)) * part, part)
            for b in range(count):
                pieces[k][e, b * part : (b + 1) * part, :] = source[
                    b, pl.ds(at, part), (e % 2) * half : (e % 2 + 1) * half
                ].astype(BF)


def forward(pieces, pick, heavy, gate_factor, up_factor, down_factor, dp):
    n_dp = len(pieces)
    n_ex, rows, half = pieces[0].shape
    local, slots, total = pick.shape
    rank, hid = gate_factor.shape[1:]

    def kernel(dp_ref, *refs):
        got, refs = refs[:n_dp], refs[n_dp:]
        pick_ref, heavy_ref, gate_ref, up_ref, down_ref = refs[:5]
        hg_ref, hu_ref, hidden_ref, mixed_ref, act_ref, lift_ref = refs[5:11]
        sent = refs[11 : 11 + n_dp]
        rows_ref, total_ref = refs[11 + n_dp :]
        j = pl.program_id(0)
        me = dp_ref[0]

        @pl.when(j == 0)
        def _():
            lay_out(got, rows_ref, me, 2)
            total_ref[...] = jnp.zeros_like(total_ref)

        take = pick_ref[0]
        hg = dot(take, rows_ref[0].astype(BF), 1, 1).astype(BF)
        hu = dot(take, rows_ref[1].astype(BF), 1, 1).astype(BF)
        hg_ref[0] = hg
        hu_ref[0] = hu
        gate_pre = dot(hg, gate_ref[0], 1, 0)
        up_pre = dot(hu, up_ref[0], 1, 0)
        sig = 1.0 / (1.0 + jnp.exp(-gate_pre))
        act = gate_pre * sig
        act_ref[0] = act
        lift_ref[0] = up_pre * (sig * (1.0 + gate_pre * (1.0 - sig)))
        hidden = (act * up_pre).astype(BF)
        hidden_ref[0] = hidden
        mixed = dot(hidden, down_ref[0], 1, 0).astype(BF)
        mixed_ref[0] = mixed
        total_ref[0] += dot(mixed, heavy_ref[0], 0, 0)

        @pl.when(j == local - 1)
        def _():
            hand_out(total_ref, sent, me, 1)

    slot_shape = (local, slots, rank)
    hid_shape = (local, slots, hid)
    outs = [
        shaped(slot_shape, BF),
        shaped(slot_shape, BF),
        shaped(hid_shape, BF),
        shaped(slot_shape, BF),
        shaped(hid_shape, FL),
        shaped(hid_shape, FL),
    ]
    chunks = [shaped((n_ex, rows // 2, half), BF)] * n_dp
    got = pl.pallas_call(
        kernel,
        grid=(local,),
        out_shape=outs + chunks,
        in_specs=[SCALAR]
        + [whole(piece) for piece in pieces]
        + [each(x) for x in (pick, heavy, gate_factor, up_factor, down_factor)],
        out_specs=[each(out) for out in outs] + [whole(chunk) for chunk in chunks],
        scratch_shapes=[pltpu.VMEM((2, rank, total), rows_kind(rows // 2)), pltpu.VMEM((1, rank, total), FL)],
        compiler_params=params(),
        cost_estimate=pl.CostEstimate(
            flops=local * slots * rank * (6 * total + 6 * hid),
            bytes_accessed=16 << 20,
            transcendentals=local * slots * hid,
        ),
        name="forward",
    )(dp.reshape(1), *pieces, pick, heavy, gate_factor, up_factor, down_factor)
    return got[:6], got[6:]


def backward(pieces, pick, weight, mixed, act, lift, gate_factor, up_factor, down_factor, dp):
    n_dp = len(pieces)
    n_ex, rows, half = pieces[0].shape
    local, slots, total = pick.shape
    rank, hid = gate_factor.shape[1:]

    def kernel(dp_ref, *refs):
        got, refs = refs[:n_dp], refs[n_dp:]
        pick_ref, weight_ref, mixed_ref, act_ref, lift_ref = refs[:5]
        gate_ref, up_ref, down_ref = refs[5:8]
        back_ref, gate_out, up_out, dots_ref = refs[8:12]
        sent = refs[12 : 12 + n_dp]
        rows_ref, total_ref = refs[12 + n_dp :]
        j = pl.program_id(0)
        me = dp_ref[0]

        @pl.when(j == 0)
        def _():
            lay_out(got, rows_ref, me, 1)
            total_ref[...] = jnp.zeros_like(total_ref)

        take = pick_ref[0]
        hd = dot(take, rows_ref[0].astype(BF), 1, 1)
        dots_ref[0] = jnp.sum(mixed_ref[0].astype(FL) * hd, axis=1, keepdims=True)
        back = (weight_ref[0] * hd).astype(BF)
        back_ref[0] = back
        grad_hidden = dot(back, down_ref[0], 1, 1)
        grad_gate = (grad_hidden * lift_ref[0]).astype(BF)
        grad_up = (grad_hidden * act_ref[0]).astype(BF)
        gate_out[0] = grad_gate
        up_out[0] = grad_up
        total_ref[0] += dot(dot(grad_gate, gate_ref[0], 1, 1).astype(BF), take, 0, 0)
        total_ref[1] += dot(dot(grad_up, up_ref[0], 1, 1).astype(BF), take, 0, 0)

        @pl.when(j == local - 1)
        def _():
            hand_out(total_ref, sent, me, 2)

    outs = [
        shaped((local, slots, rank), BF),
        shaped((local, slots, hid), BF),
        shaped((local, slots, hid), BF),
        shaped((local, slots, 1), FL),
    ]
    chunks = [shaped((n_ex, 2 * rows, half), BF)] * n_dp
    ins = (pick, weight, mixed, act, lift, gate_factor, up_factor, down_factor)
    got = pl.pallas_call(
        kernel,
        grid=(local,),
        out_shape=outs + chunks,
        in_specs=[SCALAR] + [whole(piece) for piece in pieces] + [each(x) for x in ins],
        out_specs=[each(out) for out in outs] + [whole(chunk) for chunk in chunks],
        scratch_shapes=[pltpu.VMEM((1, rank, total), rows_kind(rows)), pltpu.VMEM((2, rank, total), FL)],
        compiler_params=params(),
        cost_estimate=pl.CostEstimate(
            flops=local * slots * rank * (6 * total + 6 * hid),
            bytes_accessed=16 << 20,
            transcendentals=0,
        ),
        name="backward",
    )(dp.reshape(1), *pieces, *ins)
    return got[:4], got[4:]


def factor_grads(hg, grad_gate, hu, grad_up, hidden, back, first):
    local, slots, rank = hg.shape
    hid = hidden.shape[2]

    def kernel(hg_ref, gate_ref, hu_ref, up_ref, hidden_ref, back_ref, _, out_g, out_u, out_d):
        out_g[0] = dot(hg_ref[0], gate_ref[0], 0, 0)
        out_u[0] = dot(hu_ref[0], up_ref[0], 0, 0)
        out_d[0] = dot(hidden_ref[0], back_ref[0], 0, 0)

    outs = [
        shaped((local, rank, hid), FL),
        shaped((local, rank, hid), FL),
        shaped((local, hid, rank), FL),
    ]
    ins = (hg, grad_gate, hu, grad_up, hidden, back)
    return pl.pallas_call(
        kernel,
        grid=(local,),
        out_shape=outs,
        in_specs=[each(x) for x in ins] + [ANYWHERE],
        out_specs=[each(out) for out in outs],
        compiler_params=params(),
        cost_estimate=pl.CostEstimate(
            flops=6 * local * slots * rank * hid,
            bytes_accessed=18 << 20,
            transcendentals=0,
        ),
        name="factor_grads",
    )(*ins, first)


def body(
    tokens,
    grad_out,
    route_ids,
    route_weight,
    cluster_of,
    gate_basis,
    up_basis,
    down_basis,
    gate_factor,
    up_factor,
    down_factor,
):
    n_dp = lax.axis_size("dp")
    n_z = lax.axis_size("ez")
    n_ex = n_z * 2
    dp = lax.axis_index("dp")
    z = lax.axis_index("ez")
    core = lax.axis_index("core")
    me_e = z * 2 + core
    tok_rows = tokens.shape[0]
    top = route_ids.shape[1]
    local = gate_factor.shape[0]
    experts = local * n_ex
    capacity = max(2, 5 * tok_rows * top // (4 * experts))
    blocks = n_dp * n_ex
    total = blocks * tok_rows
    half = total // 2
    share = n_dp * tok_rows
    slots = blocks * capacity
    clusters, rank_own, width = gate_basis.shape
    parts_core = n_dp // 2
    rank_part = rank_own // parts_core

    def own_columns(rows):
        pieces = trade(
            lambda k: lax.dynamic_slice_in_dim(rows, (dp ^ k) * width, width, 1), "dp"
        )
        return jnp.concatenate(in_order(pieces, dp), axis=0)

    x_share = own_columns(tokens)
    x_pieces = gather_z(x_share)
    dy_share = own_columns(after(grad_out, x_pieces[1]))
    dy_pieces = gather_z(after(dy_share, x_pieces[2]))
    spot = jnp.stack([z, dp, core]).astype(jnp.int32)

    def chip_rows(own, other):
        if rank_part % 16 == 0:
            return None
        count = len(own)
        shape = (clusters, count, parts_core, rank_part, width)
        own = jnp.stack(own, axis=1).reshape(shape)
        other = jnp.stack(other, axis=1).reshape(shape)
        result = []
        for k in range(n_dp):
            part = dp ^ k
            at = part % parts_core
            mine = lax.dynamic_index_in_dim(own, at, 2, False)
            theirs = lax.dynamic_index_in_dim(other, at, 2, False)
            rows = jnp.where(part // parts_core == core, mine, theirs)
            result.append(rows.reshape(clusters * count * rank_part, width))
        return result

    own_in, own_out = [gate_basis, up_basis], [down_basis]
    other_in = [core_swap(basis) for basis in own_in]
    other_out = [core_swap(basis) for basis in own_out]

    routing = jnp.concatenate([route_ids.astype(FL), route_weight.astype(FL)], axis=1)
    routing = after(routing, x_pieces[-1])
    routing = jnp.broadcast_to(routing[None], (blocks, tok_rows, 2 * top))
    routing = lax.all_to_all(routing, ("dp", "ez", "core"), split_axis=0, concat_axis=0, tiled=True)
    routing = routing.reshape(n_dp, n_z, 2, tok_rows, 2 * top).transpose(2, 1, 0, 3, 4)
    routing = routing.reshape(blocks, tok_rows, 2 * top)
    ids = routing[:, :, :top].astype(jnp.int32)
    weights = routing[:, :, top:]
    own_ids = me_e * local + jnp.arange(local, dtype=jnp.int32)
    hit = ids[None] == own_ids[:, None, None, None]
    named = jnp.any(hit, axis=3)
    weight_of = jnp.sum(jnp.where(hit, weights[None], 0.0), axis=3)
    order = jnp.cumsum(named.astype(jnp.int32), axis=2) - 1
    cell = jnp.arange(blocks, dtype=jnp.int32)[None, :, None] * capacity + order
    cell = jnp.where(named, cell, -1).reshape(local, 1, total)
    pick, heavy, slot_weight = make_picks(cell, weight_of.reshape(local, 1, total), slots)

    group_cluster = cluster_of.reshape(n_ex, local)[:, 0]

    def sum_parts(got):
        return sum(piece.astype(FL) for piece in got).astype(BF)

    def to_group(mine):
        mine = mine.reshape(clusters, -1, half)
        send = mine.at[group_cluster].get(mode="promise_in_bounds")
        return lax.all_to_all(send, ("ez", "core"), split_axis=0, concat_axis=0, tiled=True)

    x_half, rows_in, terms = project(
        x_pieces, chip_rows(own_in, other_in), own_in, other_in, spot, n_dp, n_z, x_share
    )
    mine_in = sum_parts(trade(lambda k: terms[k], "dp"))
    got_in = to_group(mine_in)
    dy_half, _, terms_out = project(
        dy_pieces, chip_rows(own_out, other_out), own_out, other_out, spot, n_dp, n_z, mine_in
    )
    mine_out = sum_parts(trade(lambda k: terms_out[k], "dp"))
    got_out = to_group(mine_out)
    h_pieces = trade(lambda k: got_in, "dp")
    (hg, hu, hidden, mixed, act, lift), mixed_chunks = forward(
        h_pieces, pick, heavy, gate_factor, up_factor, down_factor, dp
    )
    d_pieces = trade(lambda k: got_out, "dp")
    (back, grad_gate, grad_up, dots), in_chunks = backward(
        d_pieces, pick, slot_weight, mixed, act, lift, gate_factor, up_factor, down_factor, dp
    )

    owner = group_cluster[None, :] == jnp.arange(clusters, dtype=jnp.int32)[:, None]

    def from_groups(mine):
        got = lax.all_to_all(mine, ("ez", "core"), split_axis=0, concat_axis=0, tiled=True)
        return jnp.sum(
            jnp.where(owner[:, :, None, None], got.astype(FL)[None], 0.0), axis=1
        ).astype(BF).reshape(-1, half)

    mixed_mine = sum_parts(trade(lambda k: mixed_chunks[k], "dp"))
    in_mine = sum_parts(trade(lambda k: in_chunks[k], "dp"))
    in_sum = from_groups(in_mine)
    in_parts = trade(lambda k: in_sum, "dp")
    mixed_sum = from_groups(after(mixed_mine, in_parts[1]))
    mixed_parts = trade(lambda k: mixed_sum, "dp")
    grad_gate_factor, grad_up_factor, grad_down_factor = factor_grads(
        hg, grad_gate, hu, grad_up, hidden, back, in_mine
    )

    grad_x = sum(mm("rt,rf->tf", part, rows) for part, rows in zip(in_parts, rows_in))
    shares = grad_x.reshape(n_z, share, width)
    mine = scatter_z(lambda k: lax.dynamic_index_in_dim(shares, z ^ k, 0, False)).astype(BF)
    pieces = trade(
        lambda k: lax.dynamic_slice_in_dim(mine, (dp ^ k) * tok_rows, tok_rows, 0), "dp"
    )
    grad_tokens = jnp.concatenate(in_order(pieces, dp), axis=1)

    x_other = core_swap(x_half)
    dy_other = core_swap(dy_half)
    same = core == dp // parts_core

    def own_ranks(parts):
        near, far = parts[:parts_core], parts[parts_core:]
        keep = [jnp.where(same, a, b) for a, b in zip(near, far)]
        other = [core_swap(jnp.where(same, b, a)) for a, b in zip(near, far)]
        return keep, other

    shape = (clusters, rank_own, width)
    grad_gate_basis, grad_up_basis = basis_grads(
        *own_ranks(in_parts), x_half, x_other, spot, shape, n_dp
    )
    (grad_down_basis,) = basis_grads(
        *own_ranks(mixed_parts), dy_half, dy_other, spot, shape, n_dp
    )

    placed = cell == jnp.arange(slots, dtype=jnp.int32)[None, :, None]
    scores = jnp.sum(jnp.where(placed, after(dots, in_parts[2]), 0.0), axis=1)
    scores = scores.reshape(local, 2, n_z, n_dp, tok_rows).transpose(3, 2, 1, 0, 4)
    scores = scores.reshape(blocks, local, tok_rows)
    returned = lax.all_to_all(
        scores, ("dp", "ez", "core"), split_axis=0, concat_axis=0, tiled=True
    )
    by_expert = jnp.sum(returned.reshape(n_dp, experts, tok_rows), axis=0)
    chosen = route_ids[:, :, None] == jnp.arange(experts, dtype=jnp.int32)[None, None, :]
    grad_route = jnp.sum(jnp.where(chosen, by_expert.T[:, None, :], 0.0), axis=2)
    return (
        grad_tokens,
        grad_route,
        grad_gate_basis,
        grad_up_basis,
        grad_down_basis,
        grad_gate_factor,
        grad_up_factor,
        grad_down_factor,
    )


def solution(mesh):
    n_dp, n_ex = mesh.shape["dp"], mesh.shape["expert"]
    split = Mesh(mesh.devices.reshape(n_dp, n_ex // 2, 2), ("dp", "ez", "core"))
    ex = ("ez", "core")
    rows = P(("dp", "ez", "core"), None)
    basis = P(None, ex, "dp")
    in_specs = (
        rows,
        rows,
        rows,
        rows,
        P(),
        basis,
        basis,
        basis,
        P(ex, None, "dp"),
        P(ex, None, "dp"),
        P(ex, "dp", None),
    )
    out_specs = (
        rows,
        rows,
        basis,
        basis,
        basis,
        P(ex, None, "dp"),
        P(ex, None, "dp"),
        P(ex, "dp", None),
    )
    return jax.shard_map(body, mesh=split, in_specs=in_specs, out_specs=out_specs, check_vma=False)
```

```python
import functools

import jax
import jax.numpy as jnp
from jax import lax
from jax.experimental import pallas as pl
from jax.experimental.pallas import tpu as pltpu
from jax.sharding import Mesh
from jax.sharding import PartitionSpec as P

FL = jnp.float32
BF = jnp.bfloat16
VMEM = pltpu.VMEM


def mm(spec, a, b):
    return jnp.einsum(spec, a, b, preferred_element_type=FL)


def dot(a, b, a_dim, b_dim):
    return lax.dot_general(a, b, (((a_dim,), (b_dim,)), ((), ())), preferred_element_type=FL)


def after(value, first):
    mark = lax.slice(first, (0,) * first.ndim, (1,) * first.ndim).reshape(()).astype(FL) * 0.0
    return value + mark.astype(value.dtype)


def core_swap(value):
    return lax.ppermute(value, "core", [(0, 1), (1, 0)])


def in_order(pieces, me):
    bit = 1
    while bit < len(pieces):
        odd = (me & bit) != 0
        pieces = [
            jnp.where(odd, pieces[j ^ bit], pieces[j]) for j in range(len(pieces))
        ]
        bit *= 2
    return pieces


def trade(chunk_for, axis):
    n = lax.axis_size(axis)
    sent = [lax.ppermute(chunk_for(k), axis, [(i, i ^ k) for i in range(n)]) for k in range(1, n)]
    return [chunk_for(0)] + sent


def gather_z(share):
    n = lax.axis_size("ez")
    if n != 4:
        return trade(lambda k: share, "ez")
    far = lax.ppermute(share, "ez", [(0, 2), (2, 0), (1, 3), (3, 1)])
    near = lax.ppermute(share, "ez", [(0, 1), (1, 0), (2, 3), (3, 2)])
    inner = lax.ppermute(share, "ez", [(1, 2), (2, 1)])
    ends = lax.ppermute(far, "ez", [(2, 3), (1, 0)])
    return [share, near, far, inner, ends]


def scatter_z(share_of):
    n = lax.axis_size("ez")
    if n != 4:
        got = trade(lambda k: share_of(k).astype(BF), "ez")
        return share_of(0) + sum(piece.astype(FL) for piece in got[1:]), got[1], got[1]
    third = share_of(3).astype(BF)
    ends = lax.ppermute(third, "ez", [(0, 1), (3, 2)])
    near = lax.ppermute(share_of(1).astype(BF), "ez", [(0, 1), (1, 0), (2, 3), (3, 2)])
    inner = lax.ppermute(third, "ez", [(1, 2), (2, 1)])
    second = (share_of(2) + ends.astype(FL)).astype(BF)
    far = lax.ppermute(second, "ez", [(0, 2), (2, 0), (1, 3), (3, 1)])
    return share_of(0) + near.astype(FL) + inner.astype(FL) + far.astype(FL), near, second


def whole(array):
    return pl.BlockSpec(array.shape, lambda *_: (0,) * array.ndim, memory_space=VMEM)


def each(array):
    shape = (1,) + array.shape[1:]
    return pl.BlockSpec(shape, lambda j: (j,) + (0,) * (array.ndim - 1), memory_space=VMEM)


SCALAR = pl.BlockSpec(memory_space=pltpu.SMEM)
ANYWHERE = pl.BlockSpec(memory_space=pl.ANY)


FREE = pl.CostEstimate(flops=0, bytes_accessed=0, transcendentals=0)


def params(total, big=False):
    return pltpu.CompilerParams(vmem_limit_bytes=(56 if big else 8 + total * 15 // 1024) << 20)


def shaped(shape, kind):
    return jax.ShapeDtypeStruct(shape, kind)


def project(pieces, rows, bases, spot, n_dp, n_z, first):
    gathered = len(pieces) == 1
    width = pieces[0].shape[1]
    half = pieces[0].shape[0] * (1 if gathered else n_z)
    share = half // n_z
    count = len(bases)
    clusters, rank_own = bases[0].shape[1:3]
    parts_core = n_dp // 2
    part = rank_own // parts_core
    row_count = clusters * count * part
    built = rows is None
    ins = list(pieces) + list(bases if built else rows)

    def kernel(spot_ref, *refs):
        got, sources = refs[: len(pieces)], refs[len(pieces) : len(ins)]
        outs = list(refs[len(ins) + 1 :])
        z, dp = spot_ref[0], spot_ref[1]
        cols = got[0] if gathered else outs.pop(0)
        products = outs[-n_dp:]
        parts = sources
        if built:
            parts = outs[:n_dp]
            for k in range(n_dp):
                own = dp ^ k
                low = pl.multiple_of(lax.rem(own, parts_core) * part, part)
                for c in range(clusters):
                    for b in range(count):
                        to = (c * count + b) * part
                        parts[k][to : to + part, :] = sources[b][
                            own // parts_core, c, pl.ds(low, part), :
                        ]
        if not gathered:
            for k in range(n_z):
                at = pl.multiple_of((z ^ k) * share, 16)
                piece = got[k][...]
                if k == 3 and len(pieces) > n_z:
                    middle = jnp.logical_or(z == 1, z == 2)
                    piece = jnp.where(middle, piece, got[4][...])
                cols[pl.ds(at, share), :] = piece
        for base, product in zip(parts, products):
            product[...] = dot(base[...], cols[...], 1, 1).astype(BF)

    outs = [] if gathered else [shaped((half, width), BF)]
    if built:
        outs += [shaped((row_count, width), BF)] * n_dp
    outs += [shaped((row_count, half), BF)] * n_dp
    got = pl.pallas_call(
        kernel,
        out_shape=outs,
        in_specs=[SCALAR] + [whole(x) for x in ins] + [ANYWHERE],
        out_specs=[whole(out) for out in outs],
        compiler_params=params(2 * half, True),
        cost_estimate=FREE,
        name="project",
    )(spot, *ins, first)
    cols = pieces[0] if gathered else got[0]
    return cols, (got[-2 * n_dp : -n_dp] if built else rows), got[-n_dp:]


def basis_grads(keep, other, cols, spot, shape, n_dp, first):
    clusters, rank_own, width = shape
    parts_core = n_dp // 2
    part = rank_own // parts_core
    half = cols.shape[1]
    count = keep[0].shape[0] // (clusters * part)
    block = width // 2 if width % 256 == 0 else width

    def kernel(spot_ref, *refs):
        ours, theirs = refs[:parts_core], refs[parts_core : 2 * parts_core]
        cols_ref, outs, rows_ref = refs[2 * parts_core], refs[-1 - count : -1], refs[-1]
        dp, core = spot_ref[1], spot_ref[2]

        @pl.when(pl.program_id(0) == 0)
        def _():
            for k in range(parts_core):
                low = (lax.rem(dp, parts_core) ^ k) * part
                for c in range(clusters):
                    at = pl.multiple_of(c * rank_own + low, part)
                    for b in range(count):
                        take = slice((c * count + b) * part, (c * count + b + 1) * part)
                        kind = rows_ref.dtype
                        rows_ref[core, b, pl.ds(at, part), :] = ours[k][take, :].astype(kind)
                        rows_ref[1 - core, b, pl.ds(at, part), :] = theirs[k][take, :].astype(kind)

        for b in range(count):
            total = dot(rows_ref[0, b].astype(BF), cols_ref[0], 1, 0)
            total += dot(rows_ref[1, b].astype(BF), cols_ref[1], 1, 0)
            outs[b][...] = total

    ins = list(keep) + list(other)
    out = shaped((clusters * rank_own, width), FL)
    got = pl.pallas_call(
        kernel,
        grid=(width // block,),
        out_shape=[out] * count,
        in_specs=[SCALAR]
        + [whole(x) for x in ins]
        + [pl.BlockSpec((2, half, block), lambda j: (0, 0, j), memory_space=VMEM), ANYWHERE],
        out_specs=[
            pl.BlockSpec((clusters * rank_own, block), lambda j: (0, j), memory_space=VMEM)
        ]
        * count,
        scratch_shapes=[pltpu.VMEM((2, count, clusters * rank_own, half), rows_kind(part))],
        compiler_params=params(2 * half),
        cost_estimate=FREE,
        name="basis_grads",
    )(spot, *ins, cols, first)
    return [grad.reshape(shape) for grad in got]


def make_picks(cell, weight, slots):
    local, _, total = cell.shape

    def kernel(cell_ref, weight_ref, pick_ref, slot_ref):
        hit = cell_ref[0] == lax.broadcasted_iota(jnp.int32, (slots, total), 0)
        pick_ref[0] = jnp.where(hit, 1.0, 0.0).astype(BF)
        slot_ref[0] = jnp.sum(jnp.where(hit, weight_ref[0], 0.0), axis=1, keepdims=True)

    outs = [shaped((local, slots, total), BF), shaped((local, slots, 1), FL)]
    return pl.pallas_call(
        kernel,
        grid=(local,),
        out_shape=outs,
        in_specs=[each(cell), each(weight)],
        out_specs=[each(out) for out in outs],
        compiler_params=params(total),
        cost_estimate=FREE,
        name="make_picks",
    )(cell, weight)


def lay_out(pieces, target, me, count):
    n_dp = len(pieces)
    n_ex, rows, half = pieces[0].shape
    part = rows // count
    for k in range(n_dp):
        for e in range(n_ex):
            at = pl.multiple_of(((e // 2) * n_dp + (me ^ k)) * part, part)
            for b in range(count):
                piece = pieces[k][e, b * part : (b + 1) * part, :]
                target[b, pl.ds(at, part), (e % 2) * half : (e % 2 + 1) * half] = piece.astype(
                    target.dtype
                )


def rows_kind(part):
    return BF if part % 16 == 0 else FL


def hand_out(source, pieces, me, count):
    n_dp = len(pieces)
    n_ex, rows, half = pieces[0].shape
    part = rows // count
    for k in range(n_dp):
        for e in range(n_ex):
            at = pl.multiple_of(((e // 2) * n_dp + (me ^ k)) * part, part)
            for b in range(count):
                pieces[k][e, b * part : (b + 1) * part, :] = source[
                    b, pl.ds(at, part), (e % 2) * half : (e % 2 + 1) * half
                ].astype(BF)


def forward(pieces, pick, gate_factor, up_factor, down_factor, dp):
    n_dp = len(pieces)
    n_ex, rows, half = pieces[0].shape
    local, slots, total = pick.shape
    rank, hid = gate_factor.shape[1:]

    def kernel(dp_ref, *refs):
        got, refs = refs[:n_dp], refs[n_dp:]
        pick_ref, gate_ref, up_ref, down_ref = refs[:4]
        hg_ref, hu_ref, hidden_ref, mixed_ref, act_ref, lift_ref, rows_ref = refs[4:]
        j = pl.program_id(0)
        me = dp_ref[0]

        @pl.when(j == 0)
        def _():
            lay_out(got, rows_ref, me, 2)

        take = pick_ref[0]
        hg = dot(take, rows_ref[0].astype(BF), 1, 1).astype(BF)
        hu = dot(take, rows_ref[1].astype(BF), 1, 1).astype(BF)
        hg_ref[0] = hg
        hu_ref[0] = hu
        gate_pre = dot(hg, gate_ref[0], 1, 0)
        up_pre = dot(hu, up_ref[0], 1, 0)
        sig = 1.0 / (1.0 + jnp.exp(-gate_pre))
        act = gate_pre * sig
        act_ref[0] = act
        lift_ref[0] = up_pre * (sig * (1.0 + gate_pre * (1.0 - sig)))
        hidden = (act * up_pre).astype(BF)
        hidden_ref[0] = hidden
        mixed_ref[0] = dot(hidden, down_ref[0], 1, 0).astype(BF)

    slot_shape = (local, slots, rank)
    hid_shape = (local, slots, hid)
    outs = [
        shaped(slot_shape, BF),
        shaped(slot_shape, BF),
        shaped(hid_shape, BF),
        shaped(slot_shape, BF),
        shaped(hid_shape, FL),
        shaped(hid_shape, FL),
    ]
    return pl.pallas_call(
        kernel,
        grid=(local,),
        out_shape=outs,
        in_specs=[SCALAR]
        + [whole(piece) for piece in pieces]
        + [each(x) for x in (pick, gate_factor, up_factor, down_factor)],
        out_specs=[each(out) for out in outs],
        scratch_shapes=[pltpu.VMEM((2, rank, total), rows_kind(rows // 2))],
        compiler_params=params(total, True),
        cost_estimate=FREE,
        name="forward",
    )(dp.reshape(1), *pieces, pick, gate_factor, up_factor, down_factor)


def backward(pieces, pick, weight, mixed, act, lift, gate_factor, up_factor, down_factor, dp):
    n_dp = len(pieces)
    n_ex, rows, half = pieces[0].shape
    local, slots, total = pick.shape
    rank, hid = gate_factor.shape[1:]

    def kernel(dp_ref, *refs):
        got, refs = refs[:n_dp], refs[n_dp:]
        pick_ref, weight_ref, mixed_ref, act_ref, lift_ref = refs[:5]
        gate_ref, up_ref, down_ref = refs[5:8]
        back_ref, gate_out, up_out, dots_ref = refs[8:12]
        sent = refs[12 : 12 + n_dp]
        rows_ref, total_ref = refs[12 + n_dp :]
        j = pl.program_id(0)
        me = dp_ref[0]

        @pl.when(j == 0)
        def _():
            lay_out(got, rows_ref, me, 1)
            total_ref[...] = jnp.zeros_like(total_ref)

        take = pick_ref[0]
        hd = dot(take, rows_ref[0].astype(BF), 1, 1)
        dots_ref[0] = jnp.sum(mixed_ref[0].astype(FL) * hd, axis=1, keepdims=True)
        back = (weight_ref[0] * hd).astype(BF)
        back_ref[0] = back
        grad_hidden = dot(back, down_ref[0], 1, 1)
        grad_gate = (grad_hidden * lift_ref[0]).astype(BF)
        grad_up = (grad_hidden * act_ref[0]).astype(BF)
        gate_out[0] = grad_gate
        up_out[0] = grad_up
        total_ref[0] += dot(dot(grad_gate, gate_ref[0], 1, 1).astype(BF), take, 0, 0)
        total_ref[1] += dot(dot(grad_up, up_ref[0], 1, 1).astype(BF), take, 0, 0)

        @pl.when(j == local - 1)
        def _():
            hand_out(total_ref, sent, me, 2)

    outs = [
        shaped((local, slots, rank), BF),
        shaped((local, slots, hid), BF),
        shaped((local, slots, hid), BF),
        shaped((local, slots, 1), FL),
    ]
    chunks = [shaped((n_ex, 2 * rows, half), BF)] * n_dp
    ins = (pick, weight, mixed, act, lift, gate_factor, up_factor, down_factor)
    got = pl.pallas_call(
        kernel,
        grid=(local,),
        out_shape=outs + chunks,
        in_specs=[SCALAR] + [whole(piece) for piece in pieces] + [each(x) for x in ins],
        out_specs=[each(out) for out in outs] + [whole(chunk) for chunk in chunks],
        scratch_shapes=[pltpu.VMEM((1, rank, total), rows_kind(rows)), pltpu.VMEM((2, rank, total), FL)],
        compiler_params=params(total),
        cost_estimate=FREE,
        name="backward",
    )(dp.reshape(1), *pieces, *ins)
    return got[:4], got[4:]


def mixed_sums(mixed, pick, weight, dp, chunk, n_dp, first):
    local, slots, rank = mixed.shape
    total = pick.shape[2]

    def kernel(dp_ref, mixed_ref, pick_ref, weight_ref, *refs):
        sent, total_ref = refs[1:-1], refs[-1]
        j = pl.program_id(0)
        heavy = (pick_ref[0] * weight_ref[0]).astype(BF)
        term = dot(mixed_ref[0], heavy, 0, 0)

        @pl.when(j == 0)
        def _():
            total_ref[0] = term

        @pl.when(j > 0)
        def _():
            total_ref[0] += term

        @pl.when(j == local - 1)
        def _():
            hand_out(total_ref, sent, dp_ref[0], 1)

    chunks = [shaped(chunk, BF)] * n_dp
    return pl.pallas_call(
        kernel,
        grid=(local,),
        out_shape=chunks,
        in_specs=[SCALAR, each(mixed), each(pick), each(weight), ANYWHERE],
        out_specs=[whole(out) for out in chunks],
        scratch_shapes=[pltpu.VMEM((1, rank, total), FL)],
        compiler_params=params(total),
        cost_estimate=FREE,
        name="mixed_sums",
    )(dp.reshape(1), mixed, pick, weight, first)


def factor_grads(hg, grad_gate, hu, grad_up, hidden, back, total, first):
    local, slots, rank = hg.shape
    hid = hidden.shape[2]

    def kernel(hg_ref, gate_ref, hu_ref, up_ref, hidden_ref, back_ref, _, out_g, out_u, out_d):
        out_g[0] = dot(hg_ref[0], gate_ref[0], 0, 0)
        out_u[0] = dot(hu_ref[0], up_ref[0], 0, 0)
        out_d[0] = dot(hidden_ref[0], back_ref[0], 0, 0)

    outs = [
        shaped((local, rank, hid), FL),
        shaped((local, rank, hid), FL),
        shaped((local, hid, rank), FL),
    ]
    ins = (hg, grad_gate, hu, grad_up, hidden, back)
    return pl.pallas_call(
        kernel,
        grid=(local,),
        out_shape=outs,
        in_specs=[each(x) for x in ins] + [ANYWHERE],
        out_specs=[each(out) for out in outs],
        compiler_params=params(total),
        cost_estimate=FREE,
        name="factor_grads",
    )(*ins, first)


def body(
    tokens,
    grad_out,
    route_ids,
    route_weight,
    cluster_of,
    gate_basis,
    up_basis,
    down_basis,
    gate_factor,
    up_factor,
    down_factor,
):
    n_dp = lax.axis_size("dp")
    n_z = lax.axis_size("ez")
    n_ex = n_z * 2
    dp = lax.axis_index("dp")
    z = lax.axis_index("ez")
    core = lax.axis_index("core")
    me_e = z * 2 + core
    tok_rows = tokens.shape[0]
    top = route_ids.shape[1]
    local = gate_factor.shape[0]
    experts = local * n_ex
    capacity = max(2, 5 * tok_rows * top // (4 * experts))
    blocks = n_dp * n_ex
    total = blocks * tok_rows
    half = total // 2
    share = n_dp * tok_rows
    slots = blocks * capacity
    clusters, rank_own, width = gate_basis.shape
    parts_core = n_dp // 2
    rank_part = rank_own // parts_core

    def own_columns(rows):
        pieces = trade(
            lambda k: lax.dynamic_slice_in_dim(rows, (dp ^ k) * width, width, 1), "dp"
        )
        return jnp.concatenate(in_order(pieces, dp), axis=0)

    x_share = own_columns(tokens)
    x_pieces = gather_z(x_share)
    dy_share = own_columns(after(grad_out, x_pieces[1]))
    dy_half = lax.all_gather(dy_share, "ez", axis=0, tiled=True)
    spot = jnp.stack([z, dp, core]).astype(jnp.int32)

    def chip_rows(bases):
        if rank_part % 16 == 0:
            return None
        both = jnp.stack(bases, axis=2)
        both = both.reshape(2, clusters, len(bases), parts_core, rank_part, width)
        result = []
        for k in range(n_dp):
            part = dp ^ k
            rows = lax.dynamic_index_in_dim(both, part // parts_core, 0, False)
            rows = lax.dynamic_index_in_dim(rows, part % parts_core, 2, False)
            result.append(rows.reshape(clusters * len(bases) * rank_part, width))
        return result

    bases = [
        lax.all_gather(basis, "core", axis=0) for basis in (gate_basis, up_basis, down_basis)
    ]
    bases_in, bases_out = bases[:2], bases[2:]

    routing = jnp.concatenate([route_ids.astype(FL), route_weight.astype(FL)], axis=1)
    routing = after(routing, x_pieces[1])
    routing = jnp.broadcast_to(routing[None], (blocks, tok_rows, 2 * top))
    routing = lax.all_to_all(routing, ("dp", "ez", "core"), split_axis=0, concat_axis=0, tiled=True)
    routing = routing.reshape(n_dp, n_z, 2, tok_rows, 2 * top).transpose(2, 1, 0, 3, 4)
    routing = routing.reshape(blocks, tok_rows, 2 * top)
    ids = routing[:, :, :top].astype(jnp.int32)
    weights = routing[:, :, top:]
    own_ids = me_e * local + jnp.arange(local, dtype=jnp.int32)
    hit = ids[None] == own_ids[:, None, None, None]
    named = jnp.any(hit, axis=3)
    weight_of = jnp.sum(jnp.where(hit, weights[None], 0.0), axis=3)
    order = jnp.cumsum(named.astype(jnp.int32), axis=2) - 1
    cell = jnp.arange(blocks, dtype=jnp.int32)[None, :, None] * capacity + order
    cell = jnp.where(named, cell, -1).reshape(local, 1, total)
    weight_of = weight_of.reshape(local, 1, total)
    pick, slot_weight = make_picks(cell, weight_of, slots)

    group_cluster = cluster_of.reshape(n_ex, local)[:, 0]

    def sum_parts(got):
        return sum(piece.astype(FL) for piece in got).astype(BF)

    def to_group(mine):
        mine = mine.reshape(clusters, -1, half)
        send = mine.at[group_cluster].get(mode="promise_in_bounds")
        return lax.all_to_all(send, ("ez", "core"), split_axis=0, concat_axis=0, tiled=True)

    x_half, rows_in, terms = project(
        x_pieces, chip_rows(bases_in), bases_in, spot, n_dp, n_z, x_share
    )
    mine_in = sum_parts(trade(lambda k: terms[k], "dp"))
    got_in = to_group(mine_in)
    _, _, terms_out = project(
        [dy_half], chip_rows(bases_out), bases_out, spot, n_dp, n_z, mine_in
    )
    mine_out = sum_parts(trade(lambda k: terms_out[k], "dp"))
    got_out = to_group(mine_out)
    h_pieces = trade(lambda k: got_in, "dp")
    hg, hu, hidden, mixed, act, lift = forward(
        h_pieces, pick, gate_factor, up_factor, down_factor, dp
    )
    d_pieces = trade(lambda k: got_out, "dp")
    mixed_chunks = mixed_sums(mixed, pick, weight_of, dp, got_out.shape, n_dp, d_pieces[1])
    (back, grad_gate, grad_up, dots), in_chunks = backward(
        d_pieces, pick, slot_weight, mixed, act, lift, gate_factor, up_factor, down_factor, dp
    )

    owner = group_cluster[None, :] == jnp.arange(clusters, dtype=jnp.int32)[:, None]

    def from_groups(mine):
        got = lax.all_to_all(mine, ("ez", "core"), split_axis=0, concat_axis=0, tiled=True)
        return jnp.sum(
            jnp.where(owner[:, :, None, None], got.astype(FL)[None], 0.0), axis=1
        ).astype(BF).reshape(-1, half)

    mixed_mine = sum_parts(trade(lambda k: mixed_chunks[k], "dp"))
    in_mine = sum_parts(trade(lambda k: in_chunks[k], "dp"))
    grad_gate_factor, grad_up_factor, grad_down_factor = factor_grads(
        hg, grad_gate, hu, grad_up, hidden, back, total, in_mine
    )
    mixed_sum = from_groups(mixed_mine)
    in_sum = after(from_groups(in_mine), grad_gate_factor)
    in_parts = trade(lambda k: in_sum, "dp")
    mixed_parts = trade(lambda k: mixed_sum, "dp")

    grad_x = sum(mm("rt,rf->tf", part, rows) for part, rows in zip(in_parts, rows_in))
    shares = grad_x.reshape(n_z, share, width)
    mine, near, second = scatter_z(lambda k: lax.dynamic_index_in_dim(shares, z ^ k, 0, False))

    x_both = lax.all_gather(x_half, "core", axis=0)
    dy_both = lax.all_gather(dy_half, "core", axis=0)
    same = core == dp // parts_core

    def own_ranks(parts):
        near, far = parts[:parts_core], parts[parts_core:]
        keep = [jnp.where(same, a, b) for a, b in zip(near, far)]
        other = [core_swap(jnp.where(same, b, a)) for a, b in zip(near, far)]
        return keep, other

    shape = (clusters, rank_own, width)
    grad_gate_basis, grad_up_basis = basis_grads(
        *own_ranks(in_parts), x_both, spot, shape, n_dp, second
    )
    (grad_down_basis,) = basis_grads(
        *own_ranks(mixed_parts), dy_both, spot, shape, n_dp, second
    )

    placed = cell == jnp.arange(slots, dtype=jnp.int32)[None, :, None]
    scores = jnp.sum(jnp.where(placed, after(dots, near), 0.0), axis=1)
    scores = scores.reshape(local, 2, n_z, n_dp, tok_rows).transpose(3, 2, 1, 0, 4)
    scores = scores.reshape(blocks, local, tok_rows)
    returned = lax.all_to_all(
        scores, ("dp", "ez", "core"), split_axis=0, concat_axis=0, tiled=True
    )
    by_expert = jnp.sum(returned.reshape(n_dp, experts, tok_rows), axis=0)
    chosen = route_ids[:, :, None] == jnp.arange(experts, dtype=jnp.int32)[None, None, :]
    grad_route = jnp.sum(jnp.where(chosen, by_expert.T[:, None, :], 0.0), axis=2)

    for part in (grad_gate_basis, grad_down_basis, returned):
        mine = after(mine, part)
    mine = mine.astype(BF)
    pieces = trade(
        lambda k: lax.dynamic_slice_in_dim(mine, (dp ^ k) * tok_rows, tok_rows, 0), "dp"
    )
    grad_tokens = jnp.concatenate(in_order(pieces, dp), axis=1)
    return (
        grad_tokens,
        grad_route,
        grad_gate_basis,
        grad_up_basis,
        grad_down_basis,
        grad_gate_factor,
        grad_up_factor,
        grad_down_factor,
    )


def solution(mesh):
    n_dp, n_ex = mesh.shape["dp"], mesh.shape["expert"]
    split = Mesh(mesh.devices.reshape(n_dp, n_ex // 2, 2), ("dp", "ez", "core"))
    ex = ("ez", "core")
    rows = P(("dp", "ez", "core"), None)
    basis = P(None, ex, "dp")
    in_specs = (
        rows,
        rows,
        rows,
        rows,
        P(),
        basis,
        basis,
        basis,
        P(ex, None, "dp"),
        P(ex, None, "dp"),
        P(ex, "dp", None),
    )
    out_specs = (
        rows,
        rows,
        basis,
        basis,
        basis,
        P(ex, None, "dp"),
        P(ex, None, "dp"),
        P(ex, "dp", None),
    )
    return jax.shard_map(body, mesh=split, in_specs=in_specs, out_specs=out_specs, check_vma=False)
```

```python
import functools

import jax
import jax.numpy as jnp
from jax import lax
from jax.experimental import pallas as pl
from jax.experimental.pallas import tpu as pltpu
from jax.sharding import Mesh
from jax.sharding import PartitionSpec as P

FL = jnp.float32
BF = jnp.bfloat16
VMEM = pltpu.VMEM


def mm(spec, a, b):
    return jnp.einsum(spec, a, b, preferred_element_type=FL)


def dot(a, b, a_dim, b_dim):
    return lax.dot_general(a, b, (((a_dim,), (b_dim,)), ((), ())), preferred_element_type=FL)


def after(value, first):
    mark = lax.slice(first, (0,) * first.ndim, (1,) * first.ndim).reshape(()).astype(FL) * 0.0
    return value + mark.astype(value.dtype)


def core_swap(value):
    return lax.ppermute(value, "core", [(0, 1), (1, 0)])


def in_order(pieces, me):
    bit = 1
    while bit < len(pieces):
        odd = (me & bit) != 0
        pieces = [
            jnp.where(odd, pieces[j ^ bit], pieces[j]) for j in range(len(pieces))
        ]
        bit *= 2
    return pieces


def trade(chunk_for, axis):
    n = lax.axis_size(axis)
    sent = [lax.ppermute(chunk_for(k), axis, [(i, i ^ k) for i in range(n)]) for k in range(1, n)]
    return [chunk_for(0)] + sent


def whole(array):
    return pl.BlockSpec(array.shape, lambda *_: (0,) * array.ndim, memory_space=VMEM)


def each(array):
    shape = (1,) + array.shape[1:]
    return pl.BlockSpec(shape, lambda j: (j,) + (0,) * (array.ndim - 1), memory_space=VMEM)


SCALAR = pl.BlockSpec(memory_space=pltpu.SMEM)
ANYWHERE = pl.BlockSpec(memory_space=pl.ANY)


FREE = pl.CostEstimate(flops=0, bytes_accessed=0, transcendentals=0)


def params(total, big=False):
    return pltpu.CompilerParams(vmem_limit_bytes=(56 if big else 8 + total * 15 // 1024) << 20)


def shaped(shape, kind):
    return jax.ShapeDtypeStruct(shape, kind)


def place_rows(own, other, target, part, from_own, low):
    count = len(own)

    def fill(source):
        for c in range(own[0].shape[0]):
            for b in range(count):
                to = (c * count + b) * part
                target[to : to + part, :] = source[b][c, pl.ds(low, part), :]

    pl.when(from_own)(functools.partial(fill, own))
    pl.when(jnp.logical_not(from_own))(functools.partial(fill, other))


def project(cols, rows, own, other, spot, n_dp):
    half = cols.shape[0]
    count = len(own)
    clusters, rank_own, width = own[0].shape
    parts_core = n_dp // 2
    part = rank_own // parts_core
    row_count = clusters * count * part
    built = rows is None
    ins = [cols] + (list(own) + list(other) if built else list(rows))

    def kernel(spot_ref, cols_ref, *refs):
        sources, outs = refs[: len(ins) - 1], refs[len(ins) - 1 :]
        dp, core = spot_ref[0], spot_ref[1]
        parts, products = sources, outs[-n_dp:]
        if built:
            parts = outs[:n_dp]
            for k in range(n_dp):
                low = pl.multiple_of(lax.rem(dp ^ k, parts_core) * part, part)
                from_own = core == (dp ^ k) // parts_core
                place_rows(sources[:count], sources[count:], parts[k], part, from_own, low)
        for base, product in zip(parts, products):
            product[...] = dot(base[...], cols_ref[:, :width], 1, 1).astype(BF)

    outs = [shaped((row_count, width), BF)] * n_dp if built else []
    outs += [shaped((row_count, half), BF)] * n_dp
    got = pl.pallas_call(
        kernel,
        out_shape=outs,
        in_specs=[SCALAR] + [whole(x) for x in ins],
        out_specs=[whole(out) for out in outs],
        compiler_params=params(2 * half, True),
        cost_estimate=FREE,
        name="project",
    )(spot, *ins)
    return (got[:n_dp] if built else rows), got[-n_dp:]


def basis_grads(keep, other, cols, spot, shape, n_dp):
    clusters, rank_own, width = shape
    parts_core = n_dp // 2
    part = rank_own // parts_core
    half = cols.shape[1]
    count = keep[0].shape[0] // (clusters * part)
    block = width // 2 if width % 256 == 0 else width

    def kernel(spot_ref, *refs):
        ours, theirs = refs[:parts_core], refs[parts_core : 2 * parts_core]
        cols_ref, outs, rows_ref = refs[2 * parts_core], refs[-1 - count : -1], refs[-1]
        dp, core = spot_ref[0], spot_ref[1]

        @pl.when(pl.program_id(0) == 0)
        def _():
            for k in range(parts_core):
                low = (lax.rem(dp, parts_core) ^ k) * part
                for c in range(clusters):
                    at = pl.multiple_of(c * rank_own + low, part)
                    for b in range(count):
                        take = slice((c * count + b) * part, (c * count + b + 1) * part)
                        kind = rows_ref.dtype
                        rows_ref[core, b, pl.ds(at, part), :] = ours[k][take, :].astype(kind)
                        rows_ref[1 - core, b, pl.ds(at, part), :] = theirs[k][take, :].astype(kind)

        for b in range(count):
            total = dot(rows_ref[0, b].astype(BF), cols_ref[0], 1, 0)
            total += dot(rows_ref[1, b].astype(BF), cols_ref[1], 1, 0)
            outs[b][...] = total

    ins = list(keep) + list(other)
    out = shaped((clusters * rank_own, width), FL)
    got = pl.pallas_call(
        kernel,
        grid=(width // block,),
        out_shape=[out] * count,
        in_specs=[SCALAR]
        + [whole(x) for x in ins]
        + [pl.BlockSpec((2, half, block), lambda j: (0, 0, j), memory_space=VMEM)],
        out_specs=[
            pl.BlockSpec((clusters * rank_own, block), lambda j: (0, j), memory_space=VMEM)
        ]
        * count,
        scratch_shapes=[pltpu.VMEM((2, count, clusters * rank_own, half), rows_kind(part))],
        compiler_params=params(2 * half),
        cost_estimate=FREE,
        name="basis_grads",
    )(spot, *ins, cols)
    return [grad.reshape(shape) for grad in got]


def make_picks(cell, weight, slots):
    local, _, total = cell.shape

    def kernel(cell_ref, weight_ref, pick_ref, slot_ref):
        hit = cell_ref[0] == lax.broadcasted_iota(jnp.int32, (slots, total), 0)
        pick_ref[0] = jnp.where(hit, 1.0, 0.0).astype(BF)
        slot_ref[0] = jnp.sum(jnp.where(hit, weight_ref[0], 0.0), axis=1, keepdims=True)

    outs = [shaped((local, slots, total), BF), shaped((local, slots, 1), FL)]
    return pl.pallas_call(
        kernel,
        grid=(local,),
        out_shape=outs,
        in_specs=[each(cell), each(weight)],
        out_specs=[each(out) for out in outs],
        compiler_params=params(total),
        cost_estimate=FREE,
        name="make_picks",
    )(cell, weight)


def lay_out(pieces, target, me, count):
    n_dp = len(pieces)
    n_ex, rows, half = pieces[0].shape
    part = rows // count
    for k in range(n_dp):
        for e in range(n_ex):
            at = pl.multiple_of(((e // 2) * n_dp + (me ^ k)) * part, part)
            for b in range(count):
                piece = pieces[k][e, b * part : (b + 1) * part, :]
                target[b, pl.ds(at, part), (e % 2) * half : (e % 2 + 1) * half] = piece.astype(
                    target.dtype
                )


def rows_kind(part):
    return BF if part % 16 == 0 else FL


def hand_out(source, pieces, me, count):
    n_dp = len(pieces)
    n_ex, rows, half = pieces[0].shape
    part = rows // count
    for k in range(n_dp):
        for e in range(n_ex):
            at = pl.multiple_of(((e // 2) * n_dp + (me ^ k)) * part, part)
            for b in range(count):
                pieces[k][e, b * part : (b + 1) * part, :] = source[
                    b, pl.ds(at, part), (e % 2) * half : (e % 2 + 1) * half
                ].astype(BF)


def forward(pieces, pick, weight, gate_factor, up_factor, down_factor, dp):
    n_dp = len(pieces)
    n_ex, rows, half = pieces[0].shape
    local, slots, total = pick.shape
    rank, hid = gate_factor.shape[1:]

    def kernel(dp_ref, *refs):
        got, refs = refs[:n_dp], refs[n_dp:]
        pick_ref, weight_ref, gate_ref, up_ref, down_ref = refs[:5]
        hg_ref, hu_ref, hidden_ref, mixed_ref, act_ref, lift_ref = refs[5:11]
        sent = refs[11 : 11 + n_dp]
        rows_ref, total_ref = refs[11 + n_dp :]
        j = pl.program_id(0)
        me = dp_ref[0]

        @pl.when(j == 0)
        def _():
            lay_out(got, rows_ref, me, 2)
            total_ref[...] = jnp.zeros_like(total_ref)

        take = pick_ref[0]
        hg = dot(take, rows_ref[0].astype(BF), 1, 1).astype(BF)
        hu = dot(take, rows_ref[1].astype(BF), 1, 1).astype(BF)
        hg_ref[0] = hg
        hu_ref[0] = hu
        gate_pre = dot(hg, gate_ref[0], 1, 0)
        up_pre = dot(hu, up_ref[0], 1, 0)
        sig = 1.0 / (1.0 + jnp.exp(-gate_pre))
        act = gate_pre * sig
        act_ref[0] = act
        lift_ref[0] = up_pre * (sig * (1.0 + gate_pre * (1.0 - sig)))
        hidden = (act * up_pre).astype(BF)
        hidden_ref[0] = hidden
        mixed = dot(hidden, down_ref[0], 1, 0).astype(BF)
        mixed_ref[0] = mixed
        total_ref[0] += dot(mixed, (take * weight_ref[0]).astype(BF), 0, 0)

        @pl.when(j == local - 1)
        def _():
            hand_out(total_ref, sent, me, 1)

    slot_shape = (local, slots, rank)
    hid_shape = (local, slots, hid)
    outs = [
        shaped(slot_shape, BF),
        shaped(slot_shape, BF),
        shaped(hid_shape, BF),
        shaped(slot_shape, BF),
        shaped(hid_shape, FL),
        shaped(hid_shape, FL),
    ]
    chunks = [shaped((n_ex, rows // 2, half), BF)] * n_dp
    got = pl.pallas_call(
        kernel,
        grid=(local,),
        out_shape=outs + chunks,
        in_specs=[SCALAR]
        + [whole(piece) for piece in pieces]
        + [each(x) for x in (pick, weight, gate_factor, up_factor, down_factor)],
        out_specs=[each(out) for out in outs] + [whole(chunk) for chunk in chunks],
        scratch_shapes=[pltpu.VMEM((2, rank, total), rows_kind(rows // 2)), pltpu.VMEM((1, rank, total), FL)],
        compiler_params=params(total, True),
        cost_estimate=FREE,
        name="forward",
    )(dp.reshape(1), *pieces, pick, weight, gate_factor, up_factor, down_factor)
    return got[:6], got[6:]


def backward(pieces, pick, weight, mixed, act, lift, gate_factor, up_factor, down_factor, dp):
    n_dp = len(pieces)
    n_ex, rows, half = pieces[0].shape
    local, slots, total = pick.shape
    rank, hid = gate_factor.shape[1:]

    def kernel(dp_ref, *refs):
        got, refs = refs[:n_dp], refs[n_dp:]
        pick_ref, weight_ref, mixed_ref, act_ref, lift_ref = refs[:5]
        gate_ref, up_ref, down_ref = refs[5:8]
        back_ref, gate_out, up_out, dots_ref = refs[8:12]
        sent = refs[12 : 12 + n_dp]
        rows_ref, total_ref = refs[12 + n_dp :]
        j = pl.program_id(0)
        me = dp_ref[0]

        @pl.when(j == 0)
        def _():
            lay_out(got, rows_ref, me, 1)
            total_ref[...] = jnp.zeros_like(total_ref)

        take = pick_ref[0]
        hd = dot(take, rows_ref[0].astype(BF), 1, 1)
        dots_ref[0] = jnp.sum(mixed_ref[0].astype(FL) * hd, axis=1, keepdims=True)
        back = (weight_ref[0] * hd).astype(BF)
        back_ref[0] = back
        grad_hidden = dot(back, down_ref[0], 1, 1)
        grad_gate = (grad_hidden * lift_ref[0]).astype(BF)
        grad_up = (grad_hidden * act_ref[0]).astype(BF)
        gate_out[0] = grad_gate
        up_out[0] = grad_up
        total_ref[0] += dot(dot(grad_gate, gate_ref[0], 1, 1).astype(BF), take, 0, 0)
        total_ref[1] += dot(dot(grad_up, up_ref[0], 1, 1).astype(BF), take, 0, 0)

        @pl.when(j == local - 1)
        def _():
            hand_out(total_ref, sent, me, 2)

    outs = [
        shaped((local, slots, rank), BF),
        shaped((local, slots, hid), BF),
        shaped((local, slots, hid), BF),
        shaped((local, slots, 1), FL),
    ]
    chunks = [shaped((n_ex, 2 * rows, half), BF)] * n_dp
    ins = (pick, weight, mixed, act, lift, gate_factor, up_factor, down_factor)
    got = pl.pallas_call(
        kernel,
        grid=(local,),
        out_shape=outs + chunks,
        in_specs=[SCALAR] + [whole(piece) for piece in pieces] + [each(x) for x in ins],
        out_specs=[each(out) for out in outs] + [whole(chunk) for chunk in chunks],
        scratch_shapes=[pltpu.VMEM((1, rank, total), rows_kind(rows)), pltpu.VMEM((2, rank, total), FL)],
        compiler_params=params(total, True),
        cost_estimate=FREE,
        name="backward",
    )(dp.reshape(1), *pieces, *ins)
    return got[:4], got[4:]


def factor_grads(hg, grad_gate, hu, grad_up, hidden, back, total, first):
    local, slots, rank = hg.shape
    hid = hidden.shape[2]

    def kernel(hg_ref, gate_ref, hu_ref, up_ref, hidden_ref, back_ref, _, out_g, out_u, out_d):
        out_g[0] = dot(hg_ref[0], gate_ref[0], 0, 0)
        out_u[0] = dot(hu_ref[0], up_ref[0], 0, 0)
        out_d[0] = dot(hidden_ref[0], back_ref[0], 0, 0)

    outs = [
        shaped((local, rank, hid), FL),
        shaped((local, rank, hid), FL),
        shaped((local, hid, rank), FL),
    ]
    ins = (hg, grad_gate, hu, grad_up, hidden, back)
    return pl.pallas_call(
        kernel,
        grid=(local,),
        out_shape=outs,
        in_specs=[each(x) for x in ins] + [ANYWHERE],
        out_specs=[each(out) for out in outs],
        compiler_params=params(total),
        cost_estimate=FREE,
        name="factor_grads",
    )(*ins, first)


def body(
    tokens,
    grad_out,
    route_ids,
    route_weight,
    cluster_of,
    gate_basis,
    up_basis,
    down_basis,
    gate_factor,
    up_factor,
    down_factor,
):
    n_dp = lax.axis_size("dp")
    n_z = lax.axis_size("ez")
    n_ex = n_z * 2
    dp = lax.axis_index("dp")
    z = lax.axis_index("ez")
    core = lax.axis_index("core")
    me_e = z * 2 + core
    tok_rows, model_width = tokens.shape
    top = route_ids.shape[1]
    local = gate_factor.shape[0]
    experts = local * n_ex
    capacity = max(2, 5 * tok_rows * top // (4 * experts))
    blocks = n_dp * n_ex
    total = blocks * tok_rows
    half = total // 2
    slots = blocks * capacity
    clusters, rank_own, width = gate_basis.shape
    parts_core = n_dp // 2
    rank_part = rank_own // parts_core

    lanes = 128

    def own_columns(rows, more):
        rows = rows.reshape(tok_rows, n_dp, width).transpose(1, 0, 2)
        if more is not None:
            more = jnp.broadcast_to(more[None], (n_dp, tok_rows, lanes))
            rows = jnp.concatenate([rows, more], axis=2)
        rows = jnp.broadcast_to(rows[:, None], (n_dp, n_z) + rows.shape[1:])
        rows = rows.reshape(n_dp * n_z, tok_rows, -1)
        got = lax.all_to_all(rows, ("dp", "ez"), split_axis=0, concat_axis=0, tiled=True)
        return got.reshape(half, -1)

    routing = jnp.concatenate([route_ids.astype(BF), route_weight], axis=1)
    routing = jnp.pad(routing, ((0, 0), (0, lanes - 2 * top)))
    x_half = own_columns(tokens, routing)
    dy_half = own_columns(after(grad_out, x_half), None)
    spot = jnp.stack([dp, core]).astype(jnp.int32)

    def chip_rows(own, other):
        if rank_part % 16 == 0:
            return None
        count = len(own)
        shape = (clusters, count, parts_core, rank_part, width)
        own = jnp.stack(own, axis=1).reshape(shape)
        other = jnp.stack(other, axis=1).reshape(shape)
        result = []
        for k in range(n_dp):
            part = dp ^ k
            at = part % parts_core
            mine = lax.dynamic_index_in_dim(own, at, 2, False)
            theirs = lax.dynamic_index_in_dim(other, at, 2, False)
            rows = jnp.where(part // parts_core == core, mine, theirs)
            result.append(rows.reshape(clusters * count * rank_part, width))
        return result

    own_in, own_out = [gate_basis, up_basis], [down_basis]
    other_in = [core_swap(basis) for basis in own_in]
    other_out = [core_swap(basis) for basis in own_out]

    routing = x_half[:, width:]
    swapped = core_swap(routing)
    routing = jnp.stack(
        [jnp.where(core == 0, routing, swapped), jnp.where(core == 0, swapped, routing)]
    )
    routing = routing.reshape(blocks, tok_rows, lanes)
    ids = routing[:, :, :top].astype(jnp.int32)
    weights = routing[:, :, top : 2 * top].astype(FL)
    own_ids = me_e * local + jnp.arange(local, dtype=jnp.int32)
    hit = ids[None] == own_ids[:, None, None, None]
    named = jnp.any(hit, axis=3)
    weight_of = jnp.sum(jnp.where(hit, weights[None], 0.0), axis=3)
    order = jnp.cumsum(named.astype(jnp.int32), axis=2) - 1
    cell = jnp.arange(blocks, dtype=jnp.int32)[None, :, None] * capacity + order
    cell = jnp.where(named, cell, -1).reshape(local, 1, total)
    weight_of = weight_of.reshape(local, 1, total)
    pick, slot_weight = make_picks(cell, weight_of, slots)

    group_cluster = cluster_of.reshape(n_ex, local)[:, 0]

    def sum_parts(got):
        return sum(piece.astype(FL) for piece in got).astype(BF)

    def to_group(mine):
        mine = mine.reshape(clusters, -1, half)
        send = mine.at[group_cluster].get(mode="promise_in_bounds")
        return lax.all_to_all(send, ("ez", "core"), split_axis=0, concat_axis=0, tiled=True)

    rows_in, terms = project(
        x_half, chip_rows(own_in, other_in), own_in, other_in, spot, n_dp
    )
    mine_in = sum_parts(trade(lambda k: terms[k], "dp"))
    got_in = to_group(mine_in)
    _, terms_out = project(
        dy_half, chip_rows(own_out, other_out), own_out, other_out, spot, n_dp
    )
    mine_out = sum_parts(trade(lambda k: terms_out[k], "dp"))
    got_out = to_group(mine_out)
    h_pieces = trade(lambda k: got_in, "dp")
    (hg, hu, hidden, mixed, act, lift), mixed_chunks = forward(
        h_pieces, pick, weight_of, gate_factor, up_factor, down_factor, dp
    )
    d_pieces = trade(lambda k: got_out, "dp")
    (back, grad_gate, grad_up, dots), in_chunks = backward(
        d_pieces, pick, slot_weight, mixed, act, lift, gate_factor, up_factor, down_factor, dp
    )

    owner = group_cluster[None, :] == jnp.arange(clusters, dtype=jnp.int32)[:, None]

    def from_groups(mine):
        got = lax.all_to_all(mine, ("ez", "core"), split_axis=0, concat_axis=0, tiled=True)
        return jnp.sum(
            jnp.where(owner[:, :, None, None], got.astype(FL)[None], 0.0), axis=1
        ).astype(BF).reshape(-1, half)

    mixed_mine = sum_parts(trade(lambda k: mixed_chunks[k], "dp"))
    in_mine = sum_parts(trade(lambda k: in_chunks[k], "dp"))
    grad_gate_factor, grad_up_factor, grad_down_factor = factor_grads(
        hg, grad_gate, hu, grad_up, hidden, back, total, in_mine
    )
    mixed_sum = from_groups(mixed_mine)
    in_sum = after(from_groups(in_mine), grad_gate_factor)
    in_parts = trade(lambda k: in_sum, "dp")
    mixed_parts = trade(lambda k: mixed_sum, "dp")

    placed = cell == jnp.arange(slots, dtype=jnp.int32)[None, :, None]
    scores = jnp.sum(jnp.where(placed, dots, 0.0), axis=1).reshape(local, 2, half)
    mine = jnp.where(core == 0, scores[:, 0], scores[:, 1])
    theirs = core_swap(jnp.where(core == 0, scores[:, 1], scores[:, 0]))
    first = jnp.where(core == 0, mine, theirs)
    second = jnp.where(core == 0, theirs, mine)
    scores = jnp.concatenate([first, second], axis=0).T.astype(BF)
    scores = jnp.pad(scores, ((0, 0), (0, lanes - 2 * local)))

    grad_x = sum(mm("rt,rf->tf", part, rows) for part, rows in zip(in_parts, rows_in))
    rows = jnp.concatenate([grad_x.astype(BF), scores], axis=1)
    rows = rows.reshape(n_dp * n_z, tok_rows, width + lanes)
    rows = lax.all_to_all(rows, ("dp", "ez"), split_axis=0, concat_axis=0, tiled=True)
    rows = rows.reshape(n_dp, n_z, tok_rows, width + lanes)

    x_both = lax.all_gather(x_half, "core", axis=0)
    dy_both = lax.all_gather(dy_half, "core", axis=0)
    same = core == dp // parts_core

    def own_ranks(parts):
        near, far = parts[:parts_core], parts[parts_core:]
        keep = [jnp.where(same, a, b) for a, b in zip(near, far)]
        other = [core_swap(jnp.where(same, b, a)) for a, b in zip(near, far)]
        return keep, other

    shape = (clusters, rank_own, width)
    grad_gate_basis, grad_up_basis = basis_grads(
        *own_ranks(in_parts), x_both, spot, shape, n_dp
    )
    (grad_down_basis,) = basis_grads(
        *own_ranks(mixed_parts), dy_both, spot, shape, n_dp
    )

    grad_rows = jnp.sum(rows[..., :width].astype(FL), axis=1)
    for part in (grad_gate_basis, grad_down_basis):
        grad_rows = after(grad_rows, part)
    grad_tokens = grad_rows.astype(BF).transpose(1, 0, 2).reshape(tok_rows, model_width)
    by_expert = jnp.sum(rows[..., width : width + 2 * local].astype(FL), axis=0)
    by_expert = by_expert.transpose(1, 0, 2).reshape(tok_rows, 1, experts)
    chosen = route_ids[:, :, None] == jnp.arange(experts, dtype=jnp.int32)[None, None, :]
    grad_route = jnp.sum(jnp.where(chosen, by_expert, 0.0), axis=2)
    return (
        grad_tokens,
        grad_route,
        grad_gate_basis,
        grad_up_basis,
        grad_down_basis,
        grad_gate_factor,
        grad_up_factor,
        grad_down_factor,
    )


def solution(mesh):
    n_dp, n_ex = mesh.shape["dp"], mesh.shape["expert"]
    split = Mesh(mesh.devices.reshape(n_dp, n_ex // 2, 2), ("dp", "ez", "core"))
    ex = ("ez", "core")
    rows = P(("dp", "ez", "core"), None)
    basis = P(None, ex, "dp")
    in_specs = (
        rows,
        rows,
        rows,
        rows,
        P(),
        basis,
        basis,
        basis,
        P(ex, None, "dp"),
        P(ex, None, "dp"),
        P(ex, "dp", None),
    )
    out_specs = (
        rows,
        rows,
        basis,
        basis,
        basis,
        P(ex, None, "dp"),
        P(ex, None, "dp"),
        P(ex, "dp", None),
    )
    return jax.shard_map(body, mesh=split, in_specs=in_specs, out_specs=out_specs, check_vma=False)
```

```python
import functools

import jax
import jax.numpy as jnp
from jax import lax
from jax.experimental import pallas as pl
from jax.experimental.pallas import tpu as pltpu
from jax.sharding import Mesh
from jax.sharding import PartitionSpec as P

FL = jnp.float32
BF = jnp.bfloat16
VMEM = pltpu.VMEM


def mm(spec, a, b):
    return jnp.einsum(spec, a, b, preferred_element_type=FL)


def dot(a, b, a_dim, b_dim):
    return lax.dot_general(a, b, (((a_dim,), (b_dim,)), ((), ())), preferred_element_type=FL)


def after(value, first):
    mark = lax.slice(first, (0,) * first.ndim, (1,) * first.ndim).reshape(()).astype(FL) * 0.0
    return value + mark.astype(value.dtype)


def core_swap(value):
    return lax.ppermute(value, "core", [(0, 1), (1, 0)])


def in_order(pieces, me):
    bit = 1
    while bit < len(pieces):
        odd = (me & bit) != 0
        pieces = [
            jnp.where(odd, pieces[j ^ bit], pieces[j]) for j in range(len(pieces))
        ]
        bit *= 2
    return pieces


def trade(chunk_for, axis):
    n = lax.axis_size(axis)
    sent = [lax.ppermute(chunk_for(k), axis, [(i, i ^ k) for i in range(n)]) for k in range(1, n)]
    return [chunk_for(0)] + sent


def whole(array):
    return pl.BlockSpec(array.shape, lambda *_: (0,) * array.ndim, memory_space=VMEM)


def each(array):
    shape = (1,) + array.shape[1:]
    return pl.BlockSpec(shape, lambda j: (j,) + (0,) * (array.ndim - 1), memory_space=VMEM)


SCALAR = pl.BlockSpec(memory_space=pltpu.SMEM)
ANYWHERE = pl.BlockSpec(memory_space=pl.ANY)


FREE = pl.CostEstimate(flops=0, bytes_accessed=0, transcendentals=0)


def params(total, big=False):
    return pltpu.CompilerParams(vmem_limit_bytes=(56 if big else 8 + total * 15 // 1024) << 20)


def shaped(shape, kind):
    return jax.ShapeDtypeStruct(shape, kind)


def place_rows(own, other, target, part, from_own, low):
    count = len(own)

    def fill(source):
        for c in range(own[0].shape[0]):
            for b in range(count):
                to = (c * count + b) * part
                target[to : to + part, :] = source[b][c, pl.ds(low, part), :]

    pl.when(from_own)(functools.partial(fill, own))
    pl.when(jnp.logical_not(from_own))(functools.partial(fill, other))


def project(cols, rows, own, other, spot, n_dp):
    half = cols.shape[0]
    count = len(own)
    clusters, rank_own, width = own[0].shape
    parts_core = n_dp // 2
    part = rank_own // parts_core
    row_count = clusters * count * part
    built = rows is None
    ins = [cols] + (list(own) + list(other) if built else list(rows))

    def kernel(spot_ref, cols_ref, *refs):
        sources, outs = refs[: len(ins) - 1], refs[len(ins) - 1 :]
        dp, core = spot_ref[0], spot_ref[1]
        parts, products = sources, outs[-n_dp:]
        if built:
            parts = outs[:n_dp]
            for k in range(n_dp):
                low = pl.multiple_of(lax.rem(dp ^ k, parts_core) * part, part)
                from_own = core == (dp ^ k) // parts_core
                place_rows(sources[:count], sources[count:], parts[k], part, from_own, low)
        for base, product in zip(parts, products):
            product[...] = dot(base[...], cols_ref[:, :width], 1, 1).astype(BF)

    outs = [shaped((row_count, width), BF)] * n_dp if built else []
    outs += [shaped((row_count, half), BF)] * n_dp
    got = pl.pallas_call(
        kernel,
        out_shape=outs,
        in_specs=[SCALAR] + [whole(x) for x in ins],
        out_specs=[whole(out) for out in outs],
        compiler_params=params(2 * half, True),
        cost_estimate=FREE,
        name="project",
    )(spot, *ins)
    return (got[:n_dp] if built else rows), got[-n_dp:]


def basis_grads(keep, other, cols, other_cols, spot, shape, n_dp):
    clusters, rank_own, width = shape
    parts_core = n_dp // 2
    part = rank_own // parts_core
    half = cols.shape[0]
    count = keep[0].shape[0] // (clusters * part)
    block = width // 2 if width % 256 == 0 else width

    def kernel(spot_ref, *refs):
        ours, theirs = refs[:parts_core], refs[parts_core : 2 * parts_core]
        cols_ref, other_ref = refs[2 * parts_core : 2 * parts_core + 2]
        outs, rows_ref = refs[-1 - count : -1], refs[-1]
        dp = spot_ref[0]

        @pl.when(pl.program_id(0) == 0)
        def _():
            for k in range(parts_core):
                low = (lax.rem(dp, parts_core) ^ k) * part
                for c in range(clusters):
                    at = pl.multiple_of(c * rank_own + low, part)
                    for b in range(count):
                        take = slice((c * count + b) * part, (c * count + b + 1) * part)
                        kind = rows_ref.dtype
                        rows_ref[0, b, pl.ds(at, part), :] = ours[k][take, :].astype(kind)
                        rows_ref[1, b, pl.ds(at, part), :] = theirs[k][take, :].astype(kind)

        for b in range(count):
            total = dot(rows_ref[0, b].astype(BF), cols_ref[...], 1, 0)
            total += dot(rows_ref[1, b].astype(BF), other_ref[...], 1, 0)
            outs[b][...] = total

    ins = list(keep) + list(other)
    out = shaped((clusters * rank_own, width), FL)
    got = pl.pallas_call(
        kernel,
        grid=(width // block,),
        out_shape=[out] * count,
        in_specs=[SCALAR]
        + [whole(x) for x in ins]
        + [pl.BlockSpec((half, block), lambda j: (0, j), memory_space=VMEM)] * 2,
        out_specs=[
            pl.BlockSpec((clusters * rank_own, block), lambda j: (0, j), memory_space=VMEM)
        ]
        * count,
        scratch_shapes=[pltpu.VMEM((2, count, clusters * rank_own, half), rows_kind(part))],
        compiler_params=params(2 * half),
        cost_estimate=FREE,
        name="basis_grads",
    )(spot, *ins, cols, other_cols)
    return [grad.reshape(shape) for grad in got]


def make_picks(cell, weight, slots):
    local, _, total = cell.shape

    def kernel(cell_ref, weight_ref, pick_ref, slot_ref):
        hit = cell_ref[0] == lax.broadcasted_iota(jnp.int32, (slots, total), 0)
        pick_ref[0] = jnp.where(hit, 1.0, 0.0).astype(BF)
        slot_ref[0] = jnp.sum(jnp.where(hit, weight_ref[0], 0.0), axis=1, keepdims=True)

    outs = [shaped((local, slots, total), BF), shaped((local, slots, 1), FL)]
    return pl.pallas_call(
        kernel,
        grid=(local,),
        out_shape=outs,
        in_specs=[each(cell), each(weight)],
        out_specs=[each(out) for out in outs],
        compiler_params=params(total),
        cost_estimate=FREE,
        name="make_picks",
    )(cell, weight)


def lay_out(pieces, target, me, count):
    n_dp = len(pieces)
    n_ex, rows, half = pieces[0].shape
    part = rows // count
    for k in range(n_dp):
        for e in range(n_ex):
            at = pl.multiple_of(((e // 2) * n_dp + (me ^ k)) * part, part)
            for b in range(count):
                piece = pieces[k][e, b * part : (b + 1) * part, :]
                target[b, pl.ds(at, part), (e % 2) * half : (e % 2 + 1) * half] = piece.astype(
                    target.dtype
                )


def rows_kind(part):
    return BF if part % 16 == 0 else FL


def hand_out(source, pieces, me, count):
    n_dp = len(pieces)
    n_ex, rows, half = pieces[0].shape
    part = rows // count
    for k in range(n_dp):
        for e in range(n_ex):
            at = pl.multiple_of(((e // 2) * n_dp + (me ^ k)) * part, part)
            for b in range(count):
                pieces[k][e, b * part : (b + 1) * part, :] = source[
                    b, pl.ds(at, part), (e % 2) * half : (e % 2 + 1) * half
                ].astype(BF)


def forward(pieces, pick, gate_factor, up_factor, down_factor, dp):
    n_dp = len(pieces)
    n_ex, rows, half = pieces[0].shape
    local, slots, total = pick.shape
    rank, hid = gate_factor.shape[1:]

    def kernel(dp_ref, *refs):
        got, refs = refs[:n_dp], refs[n_dp:]
        pick_ref, gate_ref, up_ref, down_ref = refs[:4]
        hg_ref, hu_ref, hidden_ref, mixed_ref, act_ref, lift_ref, rows_ref = refs[4:]
        j = pl.program_id(0)
        me = dp_ref[0]

        @pl.when(j == 0)
        def _():
            lay_out(got, rows_ref, me, 2)

        take = pick_ref[0]
        hg = dot(take, rows_ref[0].astype(BF), 1, 1).astype(BF)
        hu = dot(take, rows_ref[1].astype(BF), 1, 1).astype(BF)
        hg_ref[0] = hg
        hu_ref[0] = hu
        gate_pre = dot(hg, gate_ref[0], 1, 0)
        up_pre = dot(hu, up_ref[0], 1, 0)
        sig = 1.0 / (1.0 + jnp.exp(-gate_pre))
        act = gate_pre * sig
        act_ref[0] = act
        lift_ref[0] = up_pre * (sig * (1.0 + gate_pre * (1.0 - sig)))
        hidden = (act * up_pre).astype(BF)
        hidden_ref[0] = hidden
        mixed_ref[0] = dot(hidden, down_ref[0], 1, 0).astype(BF)

    slot_shape = (local, slots, rank)
    hid_shape = (local, slots, hid)
    outs = [
        shaped(slot_shape, BF),
        shaped(slot_shape, BF),
        shaped(hid_shape, BF),
        shaped(slot_shape, BF),
        shaped(hid_shape, FL),
        shaped(hid_shape, FL),
    ]
    return pl.pallas_call(
        kernel,
        grid=(local,),
        out_shape=outs,
        in_specs=[SCALAR]
        + [whole(piece) for piece in pieces]
        + [each(x) for x in (pick, gate_factor, up_factor, down_factor)],
        out_specs=[each(out) for out in outs],
        scratch_shapes=[pltpu.VMEM((2, rank, total), rows_kind(rows // 2))],
        compiler_params=params(total, True),
        cost_estimate=FREE,
        name="forward",
    )(dp.reshape(1), *pieces, pick, gate_factor, up_factor, down_factor)


def backward(pieces, pick, weight, mixed, act, lift, gate_factor, up_factor, down_factor, dp):
    n_dp = len(pieces)
    n_ex, rows, half = pieces[0].shape
    local, slots, total = pick.shape
    rank, hid = gate_factor.shape[1:]

    def kernel(dp_ref, *refs):
        got, refs = refs[:n_dp], refs[n_dp:]
        pick_ref, weight_ref, mixed_ref, act_ref, lift_ref = refs[:5]
        gate_ref, up_ref, down_ref = refs[5:8]
        back_ref, gate_out, up_out, dots_ref = refs[8:12]
        sent = refs[12 : 12 + n_dp]
        rows_ref, total_ref = refs[12 + n_dp :]
        j = pl.program_id(0)
        me = dp_ref[0]

        @pl.when(j == 0)
        def _():
            lay_out(got, rows_ref, me, 1)
            total_ref[...] = jnp.zeros_like(total_ref)

        take = pick_ref[0]
        hd = dot(take, rows_ref[0].astype(BF), 1, 1)
        dots_ref[0] = jnp.sum(mixed_ref[0].astype(FL) * hd, axis=1, keepdims=True)
        back = (weight_ref[0] * hd).astype(BF)
        back_ref[0] = back
        grad_hidden = dot(back, down_ref[0], 1, 1)
        grad_gate = (grad_hidden * lift_ref[0]).astype(BF)
        grad_up = (grad_hidden * act_ref[0]).astype(BF)
        gate_out[0] = grad_gate
        up_out[0] = grad_up
        total_ref[0] += dot(dot(grad_gate, gate_ref[0], 1, 1).astype(BF), take, 0, 0)
        total_ref[1] += dot(dot(grad_up, up_ref[0], 1, 1).astype(BF), take, 0, 0)

        @pl.when(j == local - 1)
        def _():
            hand_out(total_ref, sent, me, 2)

    outs = [
        shaped((local, slots, rank), BF),
        shaped((local, slots, hid), BF),
        shaped((local, slots, hid), BF),
        shaped((local, slots, 1), FL),
    ]
    chunks = [shaped((n_ex, 2 * rows, half), BF)] * n_dp
    ins = (pick, weight, mixed, act, lift, gate_factor, up_factor, down_factor)
    got = pl.pallas_call(
        kernel,
        grid=(local,),
        out_shape=outs + chunks,
        in_specs=[SCALAR] + [whole(piece) for piece in pieces] + [each(x) for x in ins],
        out_specs=[each(out) for out in outs] + [whole(chunk) for chunk in chunks],
        scratch_shapes=[pltpu.VMEM((1, rank, total), rows_kind(rows)), pltpu.VMEM((2, rank, total), FL)],
        compiler_params=params(total, True),
        cost_estimate=FREE,
        name="backward",
    )(dp.reshape(1), *pieces, *ins)
    return got[:4], got[4:]


def mixed_sums(mixed, pick, weight, dp, chunk, n_dp, first):
    local, slots, rank = mixed.shape
    total = pick.shape[2]

    def kernel(dp_ref, mixed_ref, pick_ref, weight_ref, *refs):
        sent, total_ref = refs[1:-1], refs[-1]
        j = pl.program_id(0)
        heavy = (pick_ref[0] * weight_ref[0]).astype(BF)
        term = dot(mixed_ref[0], heavy, 0, 0)

        @pl.when(j == 0)
        def _():
            total_ref[0] = term

        @pl.when(j > 0)
        def _():
            total_ref[0] += term

        @pl.when(j == local - 1)
        def _():
            hand_out(total_ref, sent, dp_ref[0], 1)

    chunks = [shaped(chunk, BF)] * n_dp
    return pl.pallas_call(
        kernel,
        grid=(local,),
        out_shape=chunks,
        in_specs=[SCALAR, each(mixed), each(pick), each(weight), ANYWHERE],
        out_specs=[whole(out) for out in chunks],
        scratch_shapes=[pltpu.VMEM((1, rank, total), FL)],
        compiler_params=params(total),
        cost_estimate=FREE,
        name="mixed_sums",
    )(dp.reshape(1), mixed, pick, weight, first)


def factor_grads(hg, grad_gate, hu, grad_up, hidden, back, total, first):
    local, slots, rank = hg.shape
    hid = hidden.shape[2]

    def kernel(hg_ref, gate_ref, hu_ref, up_ref, hidden_ref, back_ref, _, out_g, out_u, out_d):
        out_g[0] = dot(hg_ref[0], gate_ref[0], 0, 0)
        out_u[0] = dot(hu_ref[0], up_ref[0], 0, 0)
        out_d[0] = dot(hidden_ref[0], back_ref[0], 0, 0)

    outs = [
        shaped((local, rank, hid), FL),
        shaped((local, rank, hid), FL),
        shaped((local, hid, rank), FL),
    ]
    ins = (hg, grad_gate, hu, grad_up, hidden, back)
    return pl.pallas_call(
        kernel,
        grid=(local,),
        out_shape=outs,
        in_specs=[each(x) for x in ins] + [ANYWHERE],
        out_specs=[each(out) for out in outs],
        compiler_params=params(total),
        cost_estimate=FREE,
        name="factor_grads",
    )(*ins, first)


def body(
    tokens,
    grad_out,
    route_ids,
    route_weight,
    cluster_of,
    gate_basis,
    up_basis,
    down_basis,
    gate_factor,
    up_factor,
    down_factor,
):
    n_dp = lax.axis_size("dp")
    n_z = lax.axis_size("ez")
    n_ex = n_z * 2
    dp = lax.axis_index("dp")
    z = lax.axis_index("ez")
    core = lax.axis_index("core")
    me_e = z * 2 + core
    tok_rows, model_width = tokens.shape
    top = route_ids.shape[1]
    local = gate_factor.shape[0]
    experts = local * n_ex
    capacity = max(2, 5 * tok_rows * top // (4 * experts))
    blocks = n_dp * n_ex
    total = blocks * tok_rows
    half = total // 2
    slots = blocks * capacity
    clusters, rank_own, width = gate_basis.shape
    parts_core = n_dp // 2
    rank_part = rank_own // parts_core

    lanes = 128

    def own_columns(rows, more):
        rows = rows.reshape(tok_rows, n_dp, width).transpose(1, 0, 2)
        if more is not None:
            more = jnp.broadcast_to(more[None], (n_dp, tok_rows, lanes))
            rows = jnp.concatenate([rows, more], axis=2)
        rows = jnp.broadcast_to(rows[:, None], (n_dp, n_z) + rows.shape[1:])
        rows = rows.reshape(n_dp * n_z, tok_rows, -1)
        got = lax.all_to_all(rows, ("dp", "ez"), split_axis=0, concat_axis=0, tiled=True)
        return got.reshape(half, -1)

    routing = jnp.concatenate([route_ids.astype(BF), route_weight], axis=1)
    routing = jnp.pad(routing, ((0, 0), (0, lanes - 2 * top)))
    x_half = own_columns(tokens, routing)
    dy_half = own_columns(after(grad_out, x_half), None)
    spot = jnp.stack([dp, core]).astype(jnp.int32)

    def chip_rows(own, other):
        if rank_part % 16 == 0:
            return None
        count = len(own)
        shape = (clusters, count, parts_core, rank_part, width)
        own = jnp.stack(own, axis=1).reshape(shape)
        other = jnp.stack(other, axis=1).reshape(shape)
        result = []
        for k in range(n_dp):
            part = dp ^ k
            at = part % parts_core
            mine = lax.dynamic_index_in_dim(own, at, 2, False)
            theirs = lax.dynamic_index_in_dim(other, at, 2, False)
            rows = jnp.where(part // parts_core == core, mine, theirs)
            result.append(rows.reshape(clusters * count * rank_part, width))
        return result

    own_in, own_out = [gate_basis, up_basis], [down_basis]
    other_in = [core_swap(basis) for basis in own_in]
    other_out = [core_swap(basis) for basis in own_out]

    routing = x_half[:, width:]
    swapped = core_swap(routing)
    routing = jnp.stack(
        [jnp.where(core == 0, routing, swapped), jnp.where(core == 0, swapped, routing)]
    )
    routing = routing.reshape(blocks, tok_rows, lanes)
    ids = routing[:, :, :top].astype(jnp.int32)
    weights = routing[:, :, top : 2 * top].astype(FL)
    own_ids = me_e * local + jnp.arange(local, dtype=jnp.int32)
    hit = ids[None] == own_ids[:, None, None, None]
    named = jnp.any(hit, axis=3)
    weight_of = jnp.sum(jnp.where(hit, weights[None], 0.0), axis=3)
    order = jnp.cumsum(named.astype(jnp.int32), axis=2) - 1
    cell = jnp.arange(blocks, dtype=jnp.int32)[None, :, None] * capacity + order
    cell = jnp.where(named, cell, -1).reshape(local, 1, total)
    weight_of = weight_of.reshape(local, 1, total)
    pick, slot_weight = make_picks(cell, weight_of, slots)

    group_cluster = cluster_of.reshape(n_ex, local)[:, 0]

    def sum_parts(got):
        return sum(piece.astype(FL) for piece in got).astype(BF)

    def to_group(mine):
        mine = mine.reshape(clusters, -1, half)
        send = mine.at[group_cluster].get(mode="promise_in_bounds")
        return lax.all_to_all(send, ("ez", "core"), split_axis=0, concat_axis=0, tiled=True)

    rows_in, terms = project(
        x_half, chip_rows(own_in, other_in), own_in, other_in, spot, n_dp
    )
    mine_in = sum_parts(trade(lambda k: terms[k], "dp"))
    got_in = to_group(mine_in)
    _, terms_out = project(
        dy_half, chip_rows(own_out, other_out), own_out, other_out, spot, n_dp
    )
    mine_out = sum_parts(trade(lambda k: terms_out[k], "dp"))
    got_out = to_group(mine_out)
    h_pieces = trade(lambda k: got_in, "dp")
    hg, hu, hidden, mixed, act, lift = forward(
        h_pieces, pick, gate_factor, up_factor, down_factor, dp
    )
    d_pieces = trade(lambda k: got_out, "dp")
    (back, grad_gate, grad_up, dots), in_chunks = backward(
        d_pieces, pick, slot_weight, mixed, act, lift, gate_factor, up_factor, down_factor, dp
    )

    numbers = jnp.arange(clusters, dtype=jnp.int32)[:, None]

    def by_cluster(got, groups):
        owner = (groups[None, :] == numbers)[:, :, None, None]
        summed = jnp.sum(jnp.where(owner, got.astype(FL)[None], 0.0), axis=1)
        return summed.astype(BF).reshape(-1, half)

    in_mine = sum_parts(trade(lambda k: in_chunks[k], "dp"))
    mixed_chunks = mixed_sums(mixed, pick, weight_of, dp, got_out.shape, n_dp, in_mine)
    mixed_mine = sum_parts(trade(lambda k: mixed_chunks[k], "dp"))
    got = lax.all_to_all(in_mine, ("ez", "core"), split_axis=0, concat_axis=0, tiled=True)
    in_sum = after(by_cluster(got, group_cluster), mixed_mine)
    in_parts = trade(lambda k: in_sum, "dp")

    mixed_mine = after(mixed_mine, in_parts[-1])
    got = [lax.dynamic_index_in_dim(mixed_mine, me_e, 0, False)]
    for k in range(1, n_ex):
        piece = lax.dynamic_index_in_dim(mixed_mine, me_e ^ k, 0, False)
        got.append(lax.ppermute(piece, ("ez", "core"), [(i, i ^ k) for i in range(n_ex)]))
    partners = group_cluster[me_e ^ jnp.arange(n_ex, dtype=jnp.int32)]
    mixed_sum = by_cluster(jnp.stack(got), partners)
    mixed_parts = trade(lambda k: mixed_sum, "dp")
    grad_gate_factor, grad_up_factor, grad_down_factor = factor_grads(
        hg, grad_gate, hu, grad_up, hidden, back, total, in_parts[-1]
    )

    placed = cell == jnp.arange(slots, dtype=jnp.int32)[None, :, None]
    scores = jnp.sum(jnp.where(placed, dots, 0.0), axis=1).reshape(local, 2, half)
    mine = jnp.where(core == 0, scores[:, 0], scores[:, 1])
    theirs = core_swap(jnp.where(core == 0, scores[:, 1], scores[:, 0]))
    first = jnp.where(core == 0, mine, theirs)
    second = jnp.where(core == 0, theirs, mine)
    scores = jnp.concatenate([first, second], axis=0).T.astype(BF)
    scores = jnp.pad(scores, ((0, 0), (0, lanes - 2 * local)))

    grad_x = sum(mm("rt,rf->tf", part, rows) for part, rows in zip(in_parts, rows_in))
    rows = jnp.concatenate([grad_x.astype(BF), scores], axis=1)
    rows = rows.reshape(n_dp * n_z, tok_rows, width + lanes)
    rows = lax.all_to_all(rows, ("dp", "ez"), split_axis=0, concat_axis=0, tiled=True)
    rows = rows.reshape(n_dp, n_z, tok_rows, width + lanes)

    x_other = core_swap(x_half)
    dy_other = core_swap(dy_half)
    same = core == dp // parts_core

    def own_ranks(parts):
        near, far = parts[:parts_core], parts[parts_core:]
        keep = [jnp.where(same, a, b) for a, b in zip(near, far)]
        other = [core_swap(jnp.where(same, b, a)) for a, b in zip(near, far)]
        return keep, other

    shape = (clusters, rank_own, width)
    grad_gate_basis, grad_up_basis = basis_grads(
        *own_ranks(in_parts), x_half, x_other, spot, shape, n_dp
    )
    (grad_down_basis,) = basis_grads(
        *own_ranks(mixed_parts), dy_half, dy_other, spot, shape, n_dp
    )

    grad_rows = jnp.sum(rows[..., :width].astype(FL), axis=1)
    for part in (grad_gate_factor, grad_gate_basis, grad_down_basis):
        grad_rows = after(grad_rows, part)
    grad_tokens = grad_rows.astype(BF).transpose(1, 0, 2).reshape(tok_rows, model_width)
    by_expert = jnp.sum(rows[..., width : width + 2 * local].astype(FL), axis=0)
    by_expert = by_expert.transpose(1, 0, 2).reshape(tok_rows, 1, experts)
    chosen = route_ids[:, :, None] == jnp.arange(experts, dtype=jnp.int32)[None, None, :]
    grad_route = jnp.sum(jnp.where(chosen, by_expert, 0.0), axis=2)
    return (
        grad_tokens,
        grad_route,
        grad_gate_basis,
        grad_up_basis,
        grad_down_basis,
        grad_gate_factor,
        grad_up_factor,
        grad_down_factor,
    )


def solution(mesh):
    n_dp, n_ex = mesh.shape["dp"], mesh.shape["expert"]
    split = Mesh(mesh.devices.reshape(n_dp, n_ex // 2, 2), ("dp", "ez", "core"))
    ex = ("ez", "core")
    rows = P(("dp", "ez", "core"), None)
    basis = P(None, ex, "dp")
    in_specs = (
        rows,
        rows,
        rows,
        rows,
        P(),
        basis,
        basis,
        basis,
        P(ex, None, "dp"),
        P(ex, None, "dp"),
        P(ex, "dp", None),
    )
    out_specs = (
        rows,
        rows,
        basis,
        basis,
        basis,
        P(ex, None, "dp"),
        P(ex, None, "dp"),
        P(ex, "dp", None),
    )
    return jax.shard_map(body, mesh=split, in_specs=in_specs, out_specs=out_specs, check_vma=False)
```

```python
import functools

import jax
import jax.numpy as jnp
from jax import lax
from jax.experimental import pallas as pl
from jax.experimental.pallas import tpu as pltpu
from jax.sharding import Mesh
from jax.sharding import PartitionSpec as P

FL = jnp.float32
BF = jnp.bfloat16
VMEM = pltpu.VMEM


def mm(spec, a, b):
    return jnp.einsum(spec, a, b, preferred_element_type=FL)


def dot(a, b, a_dim, b_dim):
    return lax.dot_general(a, b, (((a_dim,), (b_dim,)), ((), ())), preferred_element_type=FL)


def after(value, first):
    mark = lax.slice(first, (0,) * first.ndim, (1,) * first.ndim).reshape(()).astype(FL) * 0.0
    return value + mark.astype(value.dtype)


def core_swap(value):
    return lax.ppermute(value, "core", [(0, 1), (1, 0)])


def in_order(pieces, me):
    bit = 1
    while bit < len(pieces):
        odd = (me & bit) != 0
        pieces = [
            jnp.where(odd, pieces[j ^ bit], pieces[j]) for j in range(len(pieces))
        ]
        bit *= 2
    return pieces


def trade(chunk_for, axis):
    n = lax.axis_size(axis)
    sent = [lax.ppermute(chunk_for(k), axis, [(i, i ^ k) for i in range(n)]) for k in range(1, n)]
    return [chunk_for(0)] + sent


def whole(array):
    return pl.BlockSpec(array.shape, lambda *_: (0,) * array.ndim, memory_space=VMEM)


def each(array):
    shape = (1,) + array.shape[1:]
    return pl.BlockSpec(shape, lambda j: (j,) + (0,) * (array.ndim - 1), memory_space=VMEM)


SCALAR = pl.BlockSpec(memory_space=pltpu.SMEM)
ANYWHERE = pl.BlockSpec(memory_space=pl.ANY)


FREE = pl.CostEstimate(flops=0, bytes_accessed=0, transcendentals=0)


def params(total, big=False):
    return pltpu.CompilerParams(vmem_limit_bytes=(56 if big else 8 + total * 15 // 1024) << 20)


def shaped(shape, kind):
    return jax.ShapeDtypeStruct(shape, kind)


def place_rows(own, other, target, part, from_own, low):
    count = len(own)

    def fill(source):
        for c in range(own[0].shape[0]):
            for b in range(count):
                to = (c * count + b) * part
                target[to : to + part, :] = source[b][c, pl.ds(low, part), :]

    pl.when(from_own)(functools.partial(fill, own))
    pl.when(jnp.logical_not(from_own))(functools.partial(fill, other))


def project(cols, rows, own, other, spot, n_dp):
    half = cols.shape[0]
    count = len(own)
    clusters, rank_own, width = own[0].shape
    parts_core = n_dp // 2
    part = rank_own // parts_core
    row_count = clusters * count * part
    built = rows is None
    ins = [cols] + (list(own) + list(other) if built else list(rows))

    def kernel(spot_ref, cols_ref, *refs):
        sources, outs = refs[: len(ins) - 1], refs[len(ins) - 1 :]
        dp, core = spot_ref[0], spot_ref[1]
        parts, products = sources, outs[-n_dp:]
        if built:
            parts = outs[:n_dp]
            for k in range(n_dp):
                low = pl.multiple_of(lax.rem(dp ^ k, parts_core) * part, part)
                from_own = core == (dp ^ k) // parts_core
                place_rows(sources[:count], sources[count:], parts[k], part, from_own, low)
        for base, product in zip(parts, products):
            product[...] = dot(base[...], cols_ref[:, :width], 1, 1).astype(BF)

    outs = [shaped((row_count, width), BF)] * n_dp if built else []
    outs += [shaped((row_count, half), BF)] * n_dp
    got = pl.pallas_call(
        kernel,
        out_shape=outs,
        in_specs=[SCALAR] + [whole(x) for x in ins],
        out_specs=[whole(out) for out in outs],
        compiler_params=params(2 * half, True),
        cost_estimate=FREE,
        name="project",
    )(spot, *ins)
    return (got[:n_dp] if built else rows), got[-n_dp:]


def basis_grads(keep, other, cols, other_cols, spot, shape, n_dp, first):
    clusters, rank_own, width = shape
    parts_core = n_dp // 2
    part = rank_own // parts_core
    half = cols.shape[0]
    count = keep[0].shape[0] // (clusters * part)
    block = width // 2 if width % 256 == 0 else width

    def kernel(spot_ref, *refs):
        ours, theirs = refs[:parts_core], refs[parts_core : 2 * parts_core]
        cols_ref, other_ref = refs[2 * parts_core : 2 * parts_core + 2]
        outs, rows_ref = refs[-1 - count : -1], refs[-1]
        dp = spot_ref[0]

        @pl.when(pl.program_id(0) == 0)
        def _():
            for k in range(parts_core):
                low = (lax.rem(dp, parts_core) ^ k) * part
                for c in range(clusters):
                    at = pl.multiple_of(c * rank_own + low, part)
                    for b in range(count):
                        take = slice((c * count + b) * part, (c * count + b + 1) * part)
                        kind = rows_ref.dtype
                        rows_ref[0, b, pl.ds(at, part), :] = ours[k][take, :].astype(kind)
                        rows_ref[1, b, pl.ds(at, part), :] = theirs[k][take, :].astype(kind)

        for b in range(count):
            total = dot(rows_ref[0, b].astype(BF), cols_ref[...], 1, 0)
            total += dot(rows_ref[1, b].astype(BF), other_ref[...], 1, 0)
            outs[b][...] = total

    ins = list(keep) + list(other)
    out = shaped((clusters * rank_own, width), FL)
    got = pl.pallas_call(
        kernel,
        grid=(width // block,),
        out_shape=[out] * count,
        in_specs=[SCALAR]
        + [whole(x) for x in ins]
        + [pl.BlockSpec((half, block), lambda j: (0, j), memory_space=VMEM)] * 2
        + [ANYWHERE],
        out_specs=[
            pl.BlockSpec((clusters * rank_own, block), lambda j: (0, j), memory_space=VMEM)
        ]
        * count,
        scratch_shapes=[pltpu.VMEM((2, count, clusters * rank_own, half), rows_kind(part))],
        compiler_params=params(2 * half),
        cost_estimate=FREE,
        name="basis_grads",
    )(spot, *ins, cols, other_cols, first)
    return [grad.reshape(shape) for grad in got]


def make_picks(cell, weight, slots):
    local, _, total = cell.shape

    def kernel(cell_ref, weight_ref, pick_ref, slot_ref):
        hit = cell_ref[0] == lax.broadcasted_iota(jnp.int32, (slots, total), 0)
        pick_ref[0] = jnp.where(hit, 1.0, 0.0).astype(BF)
        slot_ref[0] = jnp.sum(jnp.where(hit, weight_ref[0], 0.0), axis=1, keepdims=True)

    outs = [shaped((local, slots, total), BF), shaped((local, slots, 1), FL)]
    return pl.pallas_call(
        kernel,
        grid=(local,),
        out_shape=outs,
        in_specs=[each(cell), each(weight)],
        out_specs=[each(out) for out in outs],
        compiler_params=params(total),
        cost_estimate=FREE,
        name="make_picks",
    )(cell, weight)


def lay_out(pieces, target, me, count):
    n_dp = len(pieces)
    n_ex, rows, half = pieces[0].shape
    part = rows // count
    for k in range(n_dp):
        for e in range(n_ex):
            at = pl.multiple_of(((e // 2) * n_dp + (me ^ k)) * part, part)
            for b in range(count):
                piece = pieces[k][e, b * part : (b + 1) * part, :]
                target[b, pl.ds(at, part), (e % 2) * half : (e % 2 + 1) * half] = piece.astype(
                    target.dtype
                )


def rows_kind(part):
    return BF if part % 16 == 0 else FL


def hand_out(source, pieces, me, count):
    n_dp = len(pieces)
    n_ex, rows, half = pieces[0].shape
    part = rows // count
    for k in range(n_dp):
        for e in range(n_ex):
            at = pl.multiple_of(((e // 2) * n_dp + (me ^ k)) * part, part)
            for b in range(count):
                pieces[k][e, b * part : (b + 1) * part, :] = source[
                    b, pl.ds(at, part), (e % 2) * half : (e % 2 + 1) * half
                ].astype(BF)


def forward(pieces, pick, weight, gate_factor, up_factor, down_factor, dp):
    n_dp = len(pieces)
    n_ex, rows, half = pieces[0].shape
    local, slots, total = pick.shape
    rank, hid = gate_factor.shape[1:]

    def kernel(dp_ref, *refs):
        got, refs = refs[:n_dp], refs[n_dp:]
        pick_ref, weight_ref, gate_ref, up_ref, down_ref = refs[:5]
        hg_ref, hu_ref, hidden_ref, mixed_ref, act_ref, lift_ref = refs[5:11]
        sent = refs[11 : 11 + n_dp]
        rows_ref, total_ref = refs[11 + n_dp :]
        j = pl.program_id(0)
        me = dp_ref[0]

        @pl.when(j == 0)
        def _():
            lay_out(got, rows_ref, me, 2)
            total_ref[...] = jnp.zeros_like(total_ref)

        take = pick_ref[0]
        hg = dot(take, rows_ref[0].astype(BF), 1, 1).astype(BF)
        hu = dot(take, rows_ref[1].astype(BF), 1, 1).astype(BF)
        hg_ref[0] = hg
        hu_ref[0] = hu
        gate_pre = dot(hg, gate_ref[0], 1, 0)
        up_pre = dot(hu, up_ref[0], 1, 0)
        sig = 1.0 / (1.0 + jnp.exp(-gate_pre))
        act = gate_pre * sig
        act_ref[0] = act
        lift_ref[0] = up_pre * (sig * (1.0 + gate_pre * (1.0 - sig)))
        hidden = (act * up_pre).astype(BF)
        hidden_ref[0] = hidden
        mixed = dot(hidden, down_ref[0], 1, 0).astype(BF)
        mixed_ref[0] = mixed
        total_ref[0] += dot(mixed, (take * weight_ref[0]).astype(BF), 0, 0)

        @pl.when(j == local - 1)
        def _():
            hand_out(total_ref, sent, me, 1)

    slot_shape = (local, slots, rank)
    hid_shape = (local, slots, hid)
    outs = [
        shaped(slot_shape, BF),
        shaped(slot_shape, BF),
        shaped(hid_shape, BF),
        shaped(slot_shape, BF),
        shaped(hid_shape, FL),
        shaped(hid_shape, FL),
    ]
    chunks = [shaped((n_ex, rows // 2, half), BF)] * n_dp
    got = pl.pallas_call(
        kernel,
        grid=(local,),
        out_shape=outs + chunks,
        in_specs=[SCALAR]
        + [whole(piece) for piece in pieces]
        + [each(x) for x in (pick, weight, gate_factor, up_factor, down_factor)],
        out_specs=[each(out) for out in outs] + [whole(chunk) for chunk in chunks],
        scratch_shapes=[pltpu.VMEM((2, rank, total), rows_kind(rows // 2)), pltpu.VMEM((1, rank, total), FL)],
        compiler_params=params(total, True),
        cost_estimate=FREE,
        name="forward",
    )(dp.reshape(1), *pieces, pick, weight, gate_factor, up_factor, down_factor)
    return got[:6], got[6:]


def backward(pieces, pick, weight, mixed, act, lift, gate_factor, up_factor, down_factor, dp):
    n_dp = len(pieces)
    n_ex, rows, half = pieces[0].shape
    local, slots, total = pick.shape
    rank, hid = gate_factor.shape[1:]

    def kernel(dp_ref, *refs):
        got, refs = refs[:n_dp], refs[n_dp:]
        pick_ref, weight_ref, mixed_ref, act_ref, lift_ref = refs[:5]
        gate_ref, up_ref, down_ref = refs[5:8]
        back_ref, gate_out, up_out, dots_ref = refs[8:12]
        sent = refs[12 : 12 + n_dp]
        rows_ref, total_ref = refs[12 + n_dp :]
        j = pl.program_id(0)
        me = dp_ref[0]

        @pl.when(j == 0)
        def _():
            lay_out(got, rows_ref, me, 1)
            total_ref[...] = jnp.zeros_like(total_ref)

        take = pick_ref[0]
        hd = dot(take, rows_ref[0].astype(BF), 1, 1)
        dots_ref[0] = jnp.sum(mixed_ref[0].astype(FL) * hd, axis=1, keepdims=True)
        back = (weight_ref[0] * hd).astype(BF)
        back_ref[0] = back
        grad_hidden = dot(back, down_ref[0], 1, 1)
        grad_gate = (grad_hidden * lift_ref[0]).astype(BF)
        grad_up = (grad_hidden * act_ref[0]).astype(BF)
        gate_out[0] = grad_gate
        up_out[0] = grad_up
        total_ref[0] += dot(dot(grad_gate, gate_ref[0], 1, 1).astype(BF), take, 0, 0)
        total_ref[1] += dot(dot(grad_up, up_ref[0], 1, 1).astype(BF), take, 0, 0)

        @pl.when(j == local - 1)
        def _():
            hand_out(total_ref, sent, me, 2)

    outs = [
        shaped((local, slots, rank), BF),
        shaped((local, slots, hid), BF),
        shaped((local, slots, hid), BF),
        shaped((local, slots, 1), FL),
    ]
    chunks = [shaped((n_ex, 2 * rows, half), BF)] * n_dp
    ins = (pick, weight, mixed, act, lift, gate_factor, up_factor, down_factor)
    got = pl.pallas_call(
        kernel,
        grid=(local,),
        out_shape=outs + chunks,
        in_specs=[SCALAR] + [whole(piece) for piece in pieces] + [each(x) for x in ins],
        out_specs=[each(out) for out in outs] + [whole(chunk) for chunk in chunks],
        scratch_shapes=[pltpu.VMEM((1, rank, total), rows_kind(rows)), pltpu.VMEM((2, rank, total), FL)],
        compiler_params=params(total, True),
        cost_estimate=pl.CostEstimate(
            flops=local * slots * rank * (6 * total + 6 * hid),
            bytes_accessed=32 << 20,
            transcendentals=0,
        ),
        name="backward",
    )(dp.reshape(1), *pieces, *ins)
    return got[:4], got[4:]


def factor_grads(hg, grad_gate, hu, grad_up, hidden, back, total, first):
    local, slots, rank = hg.shape
    hid = hidden.shape[2]

    def kernel(hg_ref, gate_ref, hu_ref, up_ref, hidden_ref, back_ref, _, out_g, out_u, out_d):
        out_g[0] = dot(hg_ref[0], gate_ref[0], 0, 0)
        out_u[0] = dot(hu_ref[0], up_ref[0], 0, 0)
        out_d[0] = dot(hidden_ref[0], back_ref[0], 0, 0)

    outs = [
        shaped((local, rank, hid), FL),
        shaped((local, rank, hid), FL),
        shaped((local, hid, rank), FL),
    ]
    ins = (hg, grad_gate, hu, grad_up, hidden, back)
    return pl.pallas_call(
        kernel,
        grid=(local,),
        out_shape=outs,
        in_specs=[each(x) for x in ins] + [ANYWHERE],
        out_specs=[each(out) for out in outs],
        compiler_params=params(total),
        cost_estimate=FREE,
        name="factor_grads",
    )(*ins, first)


def body(
    tokens,
    grad_out,
    route_ids,
    route_weight,
    cluster_of,
    gate_basis,
    up_basis,
    down_basis,
    gate_factor,
    up_factor,
    down_factor,
):
    n_dp = lax.axis_size("dp")
    n_z = lax.axis_size("ez")
    n_ex = n_z * 2
    dp = lax.axis_index("dp")
    z = lax.axis_index("ez")
    core = lax.axis_index("core")
    me_e = z * 2 + core
    tok_rows, model_width = tokens.shape
    top = route_ids.shape[1]
    local = gate_factor.shape[0]
    experts = local * n_ex
    capacity = max(2, 5 * tok_rows * top // (4 * experts))
    blocks = n_dp * n_ex
    total = blocks * tok_rows
    half = total // 2
    slots = blocks * capacity
    clusters, rank_own, width = gate_basis.shape
    parts_core = n_dp // 2
    rank_part = rank_own // parts_core

    lanes = 128

    def own_columns(rows, more):
        rows = rows.reshape(tok_rows, n_dp, width).transpose(1, 0, 2)
        if more is not None:
            more = jnp.broadcast_to(more[None], (n_dp, tok_rows, lanes))
            rows = jnp.concatenate([rows, more], axis=2)
        rows = jnp.broadcast_to(rows[:, None], (n_dp, n_z) + rows.shape[1:])
        rows = rows.reshape(n_dp * n_z, tok_rows, -1)
        got = lax.all_to_all(rows, ("dp", "ez"), split_axis=0, concat_axis=0, tiled=True)
        return got.reshape(half, -1)

    routing = jnp.concatenate([route_ids.astype(BF), route_weight], axis=1)
    routing = jnp.pad(routing, ((0, 0), (0, lanes - 2 * top)))
    x_half = own_columns(tokens, routing)
    dy_half = own_columns(after(grad_out, x_half), None)
    spot = jnp.stack([dp, core]).astype(jnp.int32)

    def chip_rows(own, other):
        if rank_part % 16 == 0:
            return None
        count = len(own)
        shape = (clusters, count, parts_core, rank_part, width)
        own = jnp.stack(own, axis=1).reshape(shape)
        other = jnp.stack(other, axis=1).reshape(shape)
        result = []
        for k in range(n_dp):
            part = dp ^ k
            at = part % parts_core
            mine = lax.dynamic_index_in_dim(own, at, 2, False)
            theirs = lax.dynamic_index_in_dim(other, at, 2, False)
            rows = jnp.where(part // parts_core == core, mine, theirs)
            result.append(rows.reshape(clusters * count * rank_part, width))
        return result

    own_in, own_out = [gate_basis, up_basis], [down_basis]
    other_in = [core_swap(basis) for basis in own_in]
    other_out = [core_swap(basis) for basis in own_out]

    routing = x_half[:, width:]
    swapped = core_swap(routing)
    routing = jnp.stack(
        [jnp.where(core == 0, routing, swapped), jnp.where(core == 0, swapped, routing)]
    )
    routing = routing.reshape(blocks, tok_rows, lanes)
    ids = routing[:, :, :top].astype(jnp.int32)
    weights = routing[:, :, top : 2 * top].astype(FL)
    own_ids = me_e * local + jnp.arange(local, dtype=jnp.int32)
    hit = ids[None] == own_ids[:, None, None, None]
    named = jnp.any(hit, axis=3)
    weight_of = jnp.sum(jnp.where(hit, weights[None], 0.0), axis=3)
    order = jnp.cumsum(named.astype(jnp.int32), axis=2) - 1
    cell = jnp.arange(blocks, dtype=jnp.int32)[None, :, None] * capacity + order
    cell = jnp.where(named, cell, -1).reshape(local, 1, total)
    weight_of = weight_of.reshape(local, 1, total)
    pick, slot_weight = make_picks(cell, weight_of, slots)

    group_cluster = cluster_of.reshape(n_ex, local)[:, 0]

    def sum_parts(got):
        return sum(piece.astype(FL) for piece in got).astype(BF)

    def to_group(mine):
        mine = mine.reshape(clusters, -1, half)
        send = mine.at[group_cluster].get(mode="promise_in_bounds")
        return lax.all_to_all(send, ("ez", "core"), split_axis=0, concat_axis=0, tiled=True)

    rows_in, terms = project(
        x_half, chip_rows(own_in, other_in), own_in, other_in, spot, n_dp
    )
    mine_in = sum_parts(trade(lambda k: terms[k], "dp"))
    got_in = to_group(mine_in)
    _, terms_out = project(
        dy_half, chip_rows(own_out, other_out), own_out, other_out, spot, n_dp
    )
    mine_out = sum_parts(trade(lambda k: terms_out[k], "dp"))
    h_pieces = trade(lambda k: got_in, "dp")
    for piece in h_pieces[1:]:
        mine_out = after(mine_out, piece)
    got_out = to_group(mine_out)
    (hg, hu, hidden, mixed, act, lift), mixed_chunks = forward(
        h_pieces, pick, weight_of, gate_factor, up_factor, down_factor, dp
    )
    d_pieces = trade(lambda k: got_out, "dp")
    (back, grad_gate, grad_up, dots), in_chunks = backward(
        d_pieces, pick, slot_weight, mixed, act, lift, gate_factor, up_factor, down_factor, dp
    )

    numbers = jnp.arange(clusters, dtype=jnp.int32)[:, None]

    def by_cluster(got, groups):
        owner = (groups[None, :] == numbers)[:, :, None, None]
        summed = jnp.sum(jnp.where(owner, got.astype(FL)[None], 0.0), axis=1)
        return summed.astype(BF).reshape(-1, half)

    mixed_mine = sum_parts(trade(lambda k: mixed_chunks[k], "dp"))
    in_mine = sum_parts(trade(lambda k: in_chunks[k], "dp"))
    grad_gate_factor, grad_up_factor, grad_down_factor = factor_grads(
        hg, grad_gate, hu, grad_up, hidden, back, total, in_mine
    )
    mine = jnp.concatenate([in_mine, mixed_mine], axis=1)
    got = lax.all_to_all(mine, ("ez", "core"), split_axis=0, concat_axis=0, tiled=True)
    in_sum = after(by_cluster(got[:, : 2 * rank_part], group_cluster), grad_gate_factor)
    mixed_sum = by_cluster(got[:, 2 * rank_part :], group_cluster)
    in_parts = trade(lambda k: in_sum, "dp")

    placed = cell == jnp.arange(slots, dtype=jnp.int32)[None, :, None]
    scores = jnp.sum(jnp.where(placed, dots, 0.0), axis=1).reshape(local, 2, half)
    mine = jnp.where(core == 0, scores[:, 0], scores[:, 1])
    theirs = core_swap(jnp.where(core == 0, scores[:, 1], scores[:, 0]))
    first = jnp.where(core == 0, mine, theirs)
    second = jnp.where(core == 0, theirs, mine)
    scores = jnp.concatenate([first, second], axis=0).T.astype(BF)
    scores = jnp.pad(scores, ((0, 0), (0, lanes - 2 * local)))

    grad_x = sum(mm("rt,rf->tf", part, rows) for part, rows in zip(in_parts, rows_in))
    leaving = jnp.concatenate([grad_x.astype(BF), scores], axis=1)
    rows = leaving.reshape(n_dp * n_z, tok_rows, width + lanes)
    rows = lax.all_to_all(rows, ("dp", "ez"), split_axis=0, concat_axis=0, tiled=True)
    rows = rows.reshape(n_dp, n_z, tok_rows, width + lanes)
    x_other = core_swap(x_half)
    dy_other = core_swap(dy_half)
    same = core == dp // parts_core

    def own_ranks(parts):
        near, far = parts[:parts_core], parts[parts_core:]
        keep = [jnp.where(same, a, b) for a, b in zip(near, far)]
        other = [core_swap(jnp.where(same, b, a)) for a, b in zip(near, far)]
        return keep, other

    shape = (clusters, rank_own, width)
    grad_gate_basis, grad_up_basis = basis_grads(
        *own_ranks(in_parts), x_half, x_other, spot, shape, n_dp, leaving
    )
    mixed_sum = after(mixed_sum, grad_gate_basis)
    mixed_parts = trade(lambda k: mixed_sum, "dp")
    (grad_down_basis,) = basis_grads(
        *own_ranks(mixed_parts), dy_half, dy_other, spot, shape, n_dp, leaving
    )

    grad_rows = jnp.sum(rows[..., :width].astype(FL), axis=1)
    grad_rows = after(grad_rows, grad_down_basis)
    grad_tokens = grad_rows.astype(BF).transpose(1, 0, 2).reshape(tok_rows, model_width)
    by_expert = jnp.sum(rows[..., width : width + 2 * local].astype(FL), axis=0)
    by_expert = by_expert.transpose(1, 0, 2).reshape(tok_rows, 1, experts)
    chosen = route_ids[:, :, None] == jnp.arange(experts, dtype=jnp.int32)[None, None, :]
    grad_route = jnp.sum(jnp.where(chosen, by_expert, 0.0), axis=2)
    return (
        grad_tokens,
        grad_route,
        grad_gate_basis,
        grad_up_basis,
        grad_down_basis,
        grad_gate_factor,
        grad_up_factor,
        grad_down_factor,
    )


def solution(mesh):
    n_dp, n_ex = mesh.shape["dp"], mesh.shape["expert"]
    split = Mesh(mesh.devices.reshape(n_dp, n_ex // 2, 2), ("dp", "ez", "core"))
    ex = ("ez", "core")
    rows = P(("dp", "ez", "core"), None)
    basis = P(None, ex, "dp")
    in_specs = (
        rows,
        rows,
        rows,
        rows,
        P(),
        basis,
        basis,
        basis,
        P(ex, None, "dp"),
        P(ex, None, "dp"),
        P(ex, "dp", None),
    )
    out_specs = (
        rows,
        rows,
        basis,
        basis,
        basis,
        P(ex, None, "dp"),
        P(ex, None, "dp"),
        P(ex, "dp", None),
    )
    return jax.shard_map(body, mesh=split, in_specs=in_specs, out_specs=out_specs, check_vma=False)
```

```python
import functools

import jax
import jax.numpy as jnp
from jax import lax
from jax.experimental import pallas as pl
from jax.experimental.pallas import tpu as pltpu
from jax.sharding import Mesh
from jax.sharding import PartitionSpec as P

FL = jnp.float32
BF = jnp.bfloat16
VMEM = pltpu.VMEM


def mm(spec, a, b):
    return jnp.einsum(spec, a, b, preferred_element_type=FL)


def dot(a, b, a_dim, b_dim):
    return lax.dot_general(a, b, (((a_dim,), (b_dim,)), ((), ())), preferred_element_type=FL)


def after(value, first):
    mark = lax.slice(first, (0,) * first.ndim, (1,) * first.ndim).reshape(()).astype(FL) * 0.0
    return value + mark.astype(value.dtype)


def core_swap(value):
    return lax.ppermute(value, "core", [(0, 1), (1, 0)])


def in_order(pieces, me):
    bit = 1
    while bit < len(pieces):
        odd = (me & bit) != 0
        pieces = [
            jnp.where(odd, pieces[j ^ bit], pieces[j]) for j in range(len(pieces))
        ]
        bit *= 2
    return pieces


def trade(chunk_for, axis):
    n = lax.axis_size(axis)
    sent = [lax.ppermute(chunk_for(k), axis, [(i, i ^ k) for i in range(n)]) for k in range(1, n)]
    return [chunk_for(0)] + sent


def gather_z(share):
    n = lax.axis_size("ez")
    if n != 4:
        return trade(lambda k: share, "ez")
    far = lax.ppermute(share, "ez", [(0, 2), (2, 0), (1, 3), (3, 1)])
    near = lax.ppermute(share, "ez", [(0, 1), (1, 0), (2, 3), (3, 2)])
    inner = lax.ppermute(share, "ez", [(1, 2), (2, 1)])
    ends = lax.ppermute(after(far, near), "ez", [(2, 3), (1, 0)])
    return [share, near, far, inner, ends]


def scatter_z(share_of):
    n = lax.axis_size("ez")
    if n != 4:
        got = trade(lambda k: share_of(k).astype(BF), "ez")
        return share_of(0) + sum(piece.astype(FL) for piece in got[1:]), got[1]
    third = share_of(3).astype(BF)
    ends = lax.ppermute(third, "ez", [(0, 1), (3, 2)])
    near = lax.ppermute(share_of(1).astype(BF), "ez", [(0, 1), (1, 0), (2, 3), (3, 2)])
    inner = lax.ppermute(third, "ez", [(1, 2), (2, 1)])
    second = (share_of(2) + ends.astype(FL)).astype(BF)
    far = lax.ppermute(second, "ez", [(0, 2), (2, 0), (1, 3), (3, 1)])
    return share_of(0) + near.astype(FL) + inner.astype(FL) + far.astype(FL), second


def whole(array):
    return pl.BlockSpec(array.shape, lambda *_: (0,) * array.ndim, memory_space=VMEM)


def each(array):
    shape = (1,) + array.shape[1:]
    return pl.BlockSpec(shape, lambda j: (j,) + (0,) * (array.ndim - 1), memory_space=VMEM)


SCALAR = pl.BlockSpec(memory_space=pltpu.SMEM)
ANYWHERE = pl.BlockSpec(memory_space=pl.ANY)


FREE = pl.CostEstimate(flops=0, bytes_accessed=0, transcendentals=0)


def params(total, big=False):
    return pltpu.CompilerParams(vmem_limit_bytes=(56 if big else 8 + total * 15 // 1024) << 20)


def shaped(shape, kind):
    return jax.ShapeDtypeStruct(shape, kind)


def place_rows(own, other, target, part, from_own, low):
    count = len(own)

    def fill(source):
        for c in range(own[0].shape[0]):
            for b in range(count):
                to = (b * own[0].shape[0] + c) * part
                target[to : to + part, :] = source[b][c, pl.ds(low, part), :]

    pl.when(from_own)(functools.partial(fill, own))
    pl.when(jnp.logical_not(from_own))(functools.partial(fill, other))


def project(pieces, rows, own, other, spot, n_dp, n_z, first):
    gathered = len(pieces) == 1
    share, lanes = pieces[0].shape
    half = share * (1 if gathered else n_z)
    count = len(own)
    clusters, rank_own, width = own[0].shape
    parts_core = n_dp // 2
    part = rank_own // parts_core
    row_count = clusters * count * part
    built = rows is None
    given = list(own) + list(other) if built else list(rows)
    ins = list(pieces) + given

    def kernel(spot_ref, *refs):
        got, sources = refs[: len(pieces)], refs[len(pieces) : len(ins)]
        outs = list(refs[len(ins) + 1 :])
        dp, core, z = spot_ref[0], spot_ref[1], spot_ref[2]
        cols = got[0] if gathered else outs.pop(0)
        parts, products = sources, outs[-n_dp:]
        if built:
            parts = outs[:n_dp]
            for k in range(n_dp):
                low = pl.multiple_of(lax.rem(dp ^ k, parts_core) * part, part)
                from_own = core == (dp ^ k) // parts_core
                place_rows(sources[:count], sources[count:], parts[k], part, from_own, low)
        if not gathered:
            for k in range(n_z):
                at = pl.multiple_of((z ^ k) * share, 16)
                piece = got[k][...]
                if k == 3 and len(pieces) > n_z:
                    middle = jnp.logical_or(z == 1, z == 2)
                    piece = jnp.where(middle, piece, got[4][...])
                cols[pl.ds(at, share), :] = piece
        for base, product in zip(parts, products):
            product[...] = dot(base[...], cols[:, :width], 1, 1).astype(BF)

    outs = [] if gathered else [shaped((half, lanes), BF)]
    outs += [shaped((row_count, width), BF)] * n_dp if built else []
    outs += [shaped((row_count, half), BF)] * n_dp
    got = pl.pallas_call(
        kernel,
        out_shape=outs,
        in_specs=[SCALAR] + [whole(x) for x in ins] + [ANYWHERE],
        out_specs=[whole(out) for out in outs],
        compiler_params=params(2 * half, True),
        cost_estimate=FREE,
        name="project",
    )(spot, *ins, first)
    cols = pieces[0] if gathered else got[0]
    return cols, (got[-2 * n_dp : -n_dp] if built else rows), got[-n_dp:]


def sum_for_groups(pieces, groups, clusters, count, firsts):
    rows, half = pieces[0].shape
    part = rows // (clusters * count)
    n_ex = groups.shape[0]

    def kernel(groups_ref, *refs):
        got, out_ref, sum_ref = refs[: len(pieces)], refs[-2], refs[-1]
        for b in range(count):
            for c in range(clusters):
                take = slice((b * clusters + c) * part, (b * clusters + c + 1) * part)
                total = got[0][take, :].astype(FL)
                for piece in got[1:]:
                    total += piece[take, :].astype(FL)
                sum_ref[c, b] = total.astype(BF)
        for e in range(n_ex):
            for b in range(count):
                out_ref[e, b * part : (b + 1) * part, :] = sum_ref[groups_ref[e], b]

    out = shaped((n_ex, count * part, half), BF)
    return pl.pallas_call(
        kernel,
        out_shape=out,
        in_specs=[SCALAR] + [whole(x) for x in pieces] + [ANYWHERE] * len(firsts),
        out_specs=whole(out),
        scratch_shapes=[pltpu.VMEM((clusters, count, part, half), BF)],
        compiler_params=params(2 * half),
        cost_estimate=FREE,
        name="sum_for_groups",
    )(groups, *pieces, *firsts)


def basis_grads(keep, other, x_cols, dy_cols, spot, shape, n_dp, first):
    clusters, rank_own, width = shape
    parts_core = n_dp // 2
    part = rank_own // parts_core
    half = x_cols[0].shape[0]
    count = 3
    block = width // 2 if width % 256 == 0 else width

    def kernel(spot_ref, *refs):
        ours, theirs = refs[:parts_core], refs[parts_core : 2 * parts_core]
        x_refs = refs[2 * parts_core : 2 * parts_core + 2]
        dy_refs = refs[2 * parts_core + 2 : 2 * parts_core + 4]
        outs, rows_ref = refs[-1 - count : -1], refs[-1]
        dp = spot_ref[0]

        @pl.when(pl.program_id(0) == 0)
        def _():
            kind = rows_ref.dtype
            for k in range(parts_core):
                low = (lax.rem(dp, parts_core) ^ k) * part
                for c in range(clusters):
                    at = pl.multiple_of(c * rank_own + low, part)
                    for b in range(count):
                        take = slice((b * clusters + c) * part, (b * clusters + c + 1) * part)
                        rows_ref[0, b, pl.ds(at, part), :] = ours[k][take, :].astype(kind)
                        rows_ref[1, b, pl.ds(at, part), :] = theirs[k][take, :].astype(kind)

        for b in range(count):
            cols = dy_refs if b == 2 else x_refs
            total = dot(rows_ref[0, b].astype(BF), cols[0][...], 1, 0)
            total += dot(rows_ref[1, b].astype(BF), cols[1][...], 1, 0)
            outs[b][...] = total

    ins = list(keep) + list(other)
    out = shaped((clusters * rank_own, width), FL)
    got = pl.pallas_call(
        kernel,
        grid=(width // block,),
        out_shape=[out] * count,
        in_specs=[SCALAR]
        + [whole(x) for x in ins]
        + [pl.BlockSpec((half, block), lambda j: (0, j), memory_space=VMEM)] * 4
        + [ANYWHERE],
        out_specs=[
            pl.BlockSpec((clusters * rank_own, block), lambda j: (0, j), memory_space=VMEM)
        ]
        * count,
        scratch_shapes=[pltpu.VMEM((2, count, clusters * rank_own, half), rows_kind(part))],
        compiler_params=params(2 * half, True),
        cost_estimate=FREE,
        name="basis_grads",
    )(spot, *ins, *x_cols, *dy_cols, first)
    return [grad.reshape(shape) for grad in got]


def make_picks(cell, weight, slots):
    local, _, total = cell.shape

    def kernel(cell_ref, weight_ref, pick_ref, slot_ref):
        hit = cell_ref[0] == lax.broadcasted_iota(jnp.int32, (slots, total), 0)
        pick_ref[0] = jnp.where(hit, 1.0, 0.0).astype(BF)
        slot_ref[0] = jnp.sum(jnp.where(hit, weight_ref[0], 0.0), axis=1, keepdims=True)

    outs = [shaped((local, slots, total), BF), shaped((local, slots, 1), FL)]
    return pl.pallas_call(
        kernel,
        grid=(local,),
        out_shape=outs,
        in_specs=[each(cell), each(weight)],
        out_specs=[each(out) for out in outs],
        compiler_params=params(total),
        cost_estimate=FREE,
        name="make_picks",
    )(cell, weight)


def lay_out(pieces, target, me, count):
    n_dp = len(pieces)
    n_ex, rows, half = pieces[0].shape
    part = rows // count
    for k in range(n_dp):
        for e in range(n_ex):
            at = pl.multiple_of(((e // 2) * n_dp + (me ^ k)) * part, part)
            for b in range(count):
                piece = pieces[k][e, b * part : (b + 1) * part, :]
                target[b, pl.ds(at, part), (e % 2) * half : (e % 2 + 1) * half] = piece.astype(
                    target.dtype
                )


def rows_kind(part):
    return BF if part % 16 == 0 else FL


def hand_out(source, pieces, me, count):
    n_dp = len(pieces)
    n_ex, rows, half = pieces[0].shape
    part = rows // count
    for k in range(n_dp):
        for e in range(n_ex):
            at = pl.multiple_of(((e // 2) * n_dp + (me ^ k)) * part, part)
            for b in range(count):
                pieces[k][e, b * part : (b + 1) * part, :] = source[
                    b, pl.ds(at, part), (e % 2) * half : (e % 2 + 1) * half
                ].astype(BF)


def forward(pieces, pick, weight, gate_factor, up_factor, down_factor, dp):
    n_dp = len(pieces)
    n_ex, rows, half = pieces[0].shape
    local, slots, total = pick.shape
    rank, hid = gate_factor.shape[1:]

    def kernel(dp_ref, *refs):
        got, refs = refs[:n_dp], refs[n_dp:]
        pick_ref, weight_ref, gate_ref, up_ref, down_ref = refs[:5]
        hg_ref, hu_ref, hidden_ref, mixed_ref, act_ref, lift_ref = refs[5:11]
        sent = refs[11 : 11 + n_dp]
        rows_ref, total_ref = refs[11 + n_dp :]
        j = pl.program_id(0)
        me = dp_ref[0]

        @pl.when(j == 0)
        def _():
            lay_out(got, rows_ref, me, 2)
            total_ref[...] = jnp.zeros_like(total_ref)

        take = pick_ref[0]
        hg = dot(take, rows_ref[0].astype(BF), 1, 1).astype(BF)
        hu = dot(take, rows_ref[1].astype(BF), 1, 1).astype(BF)
        hg_ref[0] = hg
        hu_ref[0] = hu
        gate_pre = dot(hg, gate_ref[0], 1, 0)
        up_pre = dot(hu, up_ref[0], 1, 0)
        sig = 1.0 / (1.0 + jnp.exp(-gate_pre))
        act = gate_pre * sig
        act_ref[0] = act
        lift_ref[0] = up_pre * (sig * (1.0 + gate_pre * (1.0 - sig)))
        hidden = (act * up_pre).astype(BF)
        hidden_ref[0] = hidden
        mixed = dot(hidden, down_ref[0], 1, 0).astype(BF)
        mixed_ref[0] = mixed
        total_ref[0] += dot(mixed, (take * weight_ref[0]).astype(BF), 0, 0)

        @pl.when(j == local - 1)
        def _():
            hand_out(total_ref, sent, me, 1)

    slot_shape = (local, slots, rank)
    hid_shape = (local, slots, hid)
    outs = [
        shaped(slot_shape, BF),
        shaped(slot_shape, BF),
        shaped(hid_shape, BF),
        shaped(slot_shape, BF),
        shaped(hid_shape, FL),
        shaped(hid_shape, FL),
    ]
    chunks = [shaped((n_ex, rows // 2, half), BF)] * n_dp
    got = pl.pallas_call(
        kernel,
        grid=(local,),
        out_shape=outs + chunks,
        in_specs=[SCALAR]
        + [whole(piece) for piece in pieces]
        + [each(x) for x in (pick, weight, gate_factor, up_factor, down_factor)],
        out_specs=[each(out) for out in outs] + [whole(chunk) for chunk in chunks],
        scratch_shapes=[pltpu.VMEM((2, rank, total), rows_kind(rows // 2)), pltpu.VMEM((1, rank, total), FL)],
        compiler_params=params(total, True),
        cost_estimate=FREE,
        name="forward",
    )(dp.reshape(1), *pieces, pick, weight, gate_factor, up_factor, down_factor)
    return got[:6], got[6:]


def backward(pieces, pick, weight, mixed, act, lift, gate_factor, up_factor, down_factor, dp):
    n_dp = len(pieces)
    n_ex, rows, half = pieces[0].shape
    local, slots, total = pick.shape
    rank, hid = gate_factor.shape[1:]

    def kernel(dp_ref, *refs):
        got, refs = refs[:n_dp], refs[n_dp:]
        pick_ref, weight_ref, mixed_ref, act_ref, lift_ref = refs[:5]
        gate_ref, up_ref, down_ref = refs[5:8]
        back_ref, gate_out, up_out, dots_ref = refs[8:12]
        sent = refs[12 : 12 + n_dp]
        rows_ref, total_ref = refs[12 + n_dp :]
        j = pl.program_id(0)
        me = dp_ref[0]

        @pl.when(j == 0)
        def _():
            lay_out(got, rows_ref, me, 1)
            total_ref[...] = jnp.zeros_like(total_ref)

        take = pick_ref[0]
        hd = dot(take, rows_ref[0].astype(BF), 1, 1)
        dots_ref[0] = jnp.sum(mixed_ref[0].astype(FL) * hd, axis=1, keepdims=True)
        back = (weight_ref[0] * hd).astype(BF)
        back_ref[0] = back
        grad_hidden = dot(back, down_ref[0], 1, 1)
        grad_gate = (grad_hidden * lift_ref[0]).astype(BF)
        grad_up = (grad_hidden * act_ref[0]).astype(BF)
        gate_out[0] = grad_gate
        up_out[0] = grad_up
        total_ref[0] += dot(dot(grad_gate, gate_ref[0], 1, 1).astype(BF), take, 0, 0)
        total_ref[1] += dot(dot(grad_up, up_ref[0], 1, 1).astype(BF), take, 0, 0)

        @pl.when(j == local - 1)
        def _():
            hand_out(total_ref, sent, me, 2)

    outs = [
        shaped((local, slots, rank), BF),
        shaped((local, slots, hid), BF),
        shaped((local, slots, hid), BF),
        shaped((local, slots, 1), FL),
    ]
    chunks = [shaped((n_ex, 2 * rows, half), BF)] * n_dp
    ins = (pick, weight, mixed, act, lift, gate_factor, up_factor, down_factor)
    got = pl.pallas_call(
        kernel,
        grid=(local,),
        out_shape=outs + chunks,
        in_specs=[SCALAR] + [whole(piece) for piece in pieces] + [each(x) for x in ins],
        out_specs=[each(out) for out in outs] + [whole(chunk) for chunk in chunks],
        scratch_shapes=[pltpu.VMEM((1, rank, total), rows_kind(rows)), pltpu.VMEM((2, rank, total), FL)],
        compiler_params=params(total, True),
        cost_estimate=pl.CostEstimate(
            flops=local * slots * rank * (6 * total + 6 * hid),
            bytes_accessed=32 << 20,
            transcendentals=0,
        ),
        name="backward",
    )(dp.reshape(1), *pieces, *ins)
    return got[:4], got[4:]


def factor_grads(hg, grad_gate, hu, grad_up, hidden, back, total, first):
    local, slots, rank = hg.shape
    hid = hidden.shape[2]

    def kernel(hg_ref, gate_ref, hu_ref, up_ref, hidden_ref, back_ref, _, out_g, out_u, out_d):
        out_g[0] = dot(hg_ref[0], gate_ref[0], 0, 0)
        out_u[0] = dot(hu_ref[0], up_ref[0], 0, 0)
        out_d[0] = dot(hidden_ref[0], back_ref[0], 0, 0)

    outs = [
        shaped((local, rank, hid), FL),
        shaped((local, rank, hid), FL),
        shaped((local, hid, rank), FL),
    ]
    ins = (hg, grad_gate, hu, grad_up, hidden, back)
    return pl.pallas_call(
        kernel,
        grid=(local,),
        out_shape=outs,
        in_specs=[each(x) for x in ins] + [ANYWHERE],
        out_specs=[each(out) for out in outs],
        compiler_params=params(total),
        cost_estimate=FREE,
        name="factor_grads",
    )(*ins, first)


def body(
    tokens,
    grad_out,
    route_ids,
    route_weight,
    cluster_of,
    gate_basis,
    up_basis,
    down_basis,
    gate_factor,
    up_factor,
    down_factor,
):
    n_dp = lax.axis_size("dp")
    n_z = lax.axis_size("ez")
    n_ex = n_z * 2
    dp = lax.axis_index("dp")
    z = lax.axis_index("ez")
    core = lax.axis_index("core")
    me_e = z * 2 + core
    tok_rows, model_width = tokens.shape
    top = route_ids.shape[1]
    local = gate_factor.shape[0]
    experts = local * n_ex
    capacity = max(2, 5 * tok_rows * top // (4 * experts))
    blocks = n_dp * n_ex
    total = blocks * tok_rows
    half = total // 2
    slots = blocks * capacity
    clusters, rank_own, width = gate_basis.shape
    parts_core = n_dp // 2
    rank_part = rank_own // parts_core

    lanes = 128

    routing = jnp.concatenate([route_ids.astype(BF), route_weight], axis=1)
    routing = jnp.pad(routing, ((0, 0), (0, lanes - 2 * top)))

    def slice_for(k):
        cols = lax.dynamic_slice_in_dim(tokens, (dp ^ k) * width, width, 1)
        return jnp.concatenate([cols, routing], axis=1)

    x_pieces = gather_z(jnp.concatenate(in_order(trade(slice_for, "dp"), dp), axis=0))
    dy_cols = after(grad_out, x_pieces[-1]).reshape(tok_rows, n_dp, width).transpose(1, 0, 2)
    dy_cols = jnp.broadcast_to(dy_cols[None], (n_z, n_dp, tok_rows, width))
    dy_half = lax.all_to_all(
        dy_cols.reshape(n_z * n_dp, tok_rows, width),
        ("ez", "dp"),
        split_axis=0,
        concat_axis=0,
        tiled=True,
    ).reshape(half, width)
    spot = jnp.stack([dp, core, z]).astype(jnp.int32)

    def chip_rows(own, other):
        if rank_part % 16 == 0:
            return None
        count = len(own)
        shape = (count, clusters, parts_core, rank_part, width)
        own = jnp.stack(own).reshape(shape)
        other = jnp.stack(other).reshape(shape)
        result = []
        for k in range(n_dp):
            part = dp ^ k
            at = part % parts_core
            mine = lax.dynamic_index_in_dim(own, at, 2, False)
            theirs = lax.dynamic_index_in_dim(other, at, 2, False)
            rows = jnp.where(part // parts_core == core, mine, theirs)
            result.append(rows.reshape(clusters * count * rank_part, width))
        return result

    own_in, own_out = [gate_basis, up_basis], [down_basis]
    other_in = [core_swap(basis) for basis in own_in]
    other_out = [core_swap(basis) for basis in own_out]

    x_half, rows_in, terms = project(
        x_pieces, chip_rows(own_in, other_in), own_in, other_in, spot, n_dp, n_z, route_ids
    )

    routing = x_half[:, width:]
    swapped = core_swap(routing)
    routing = jnp.stack(
        [jnp.where(core == 0, routing, swapped), jnp.where(core == 0, swapped, routing)]
    )
    routing = routing.reshape(blocks, tok_rows, lanes)
    ids = routing[:, :, :top].astype(jnp.int32)
    weights = routing[:, :, top : 2 * top].astype(FL)
    own_ids = me_e * local + jnp.arange(local, dtype=jnp.int32)
    hit = ids[None] == own_ids[:, None, None, None]
    named = jnp.any(hit, axis=3)
    weight_of = jnp.sum(jnp.where(hit, weights[None], 0.0), axis=3)
    order = jnp.cumsum(named.astype(jnp.int32), axis=2) - 1
    cell = jnp.arange(blocks, dtype=jnp.int32)[None, :, None] * capacity + order
    cell = jnp.where(named, cell, -1).reshape(local, 1, total)
    weight_of = weight_of.reshape(local, 1, total)
    pick, slot_weight = make_picks(cell, weight_of, slots)

    group_cluster = cluster_of.reshape(n_ex, local)[:, 0]

    def sum_parts(got):
        return sum(piece.astype(FL) for piece in got).astype(BF)

    def spread(mine):
        return lax.all_to_all(mine, ("ez", "core"), split_axis=0, concat_axis=0, tiled=True)

    mine_in = sum_for_groups(
        trade(lambda k: terms[k], "dp"), group_cluster, clusters, 2, [dy_half]
    )
    got_in = spread(mine_in)
    h_pieces = trade(lambda k: got_in, "dp")
    _, _, terms_out = project(
        [dy_half], chip_rows(own_out, other_out), own_out, other_out, spot, n_dp, n_z, mine_in
    )
    mine_out = sum_for_groups(
        trade(lambda k: terms_out[k], "dp"), group_cluster, clusters, 1, h_pieces[1:]
    )
    got_out = spread(mine_out)
    (hg, hu, hidden, mixed, act, lift), mixed_chunks = forward(
        h_pieces, pick, weight_of, gate_factor, up_factor, down_factor, dp
    )
    d_pieces = trade(lambda k: got_out, "dp")
    (back, grad_gate, grad_up, dots), in_chunks = backward(
        d_pieces, pick, slot_weight, mixed, act, lift, gate_factor, up_factor, down_factor, dp
    )

    mixed_mine = sum_parts(trade(lambda k: mixed_chunks[k], "dp"))
    in_mine = sum_parts(trade(lambda k: in_chunks[k], "dp"))
    grad_gate_factor, grad_up_factor, grad_down_factor = factor_grads(
        hg, grad_gate, hu, grad_up, hidden, back, total, in_mine
    )
    got = spread(jnp.concatenate([in_mine, mixed_mine], axis=1))
    owner = group_cluster[:, None] == jnp.arange(clusters, dtype=jnp.int32)[None, :]
    got = got.reshape(n_ex, 3, 1, rank_part, half).astype(FL)
    sums = jnp.sum(jnp.where(owner[:, None, :, None, None], got, 0.0), axis=0)
    sums = after(sums.astype(BF).reshape(-1, half), grad_gate_factor)
    parts = trade(lambda k: sums, "dp")

    placed = cell == jnp.arange(slots, dtype=jnp.int32)[None, :, None]
    scores = jnp.sum(jnp.where(placed, dots, 0.0), axis=1).reshape(local, 2, half)
    mine = jnp.where(core == 0, scores[:, 0], scores[:, 1])
    theirs = core_swap(jnp.where(core == 0, scores[:, 1], scores[:, 0]))
    first = jnp.where(core == 0, mine, theirs)
    second = jnp.where(core == 0, theirs, mine)
    scores = jnp.concatenate([first, second], axis=0).T
    lane = jnp.arange(lanes, dtype=jnp.int32) // (2 * local)
    scores = jnp.where(lane == z, jnp.tile(scores, (1, lanes // (2 * local))), 0.0)

    terms_in = 2 * clusters * rank_part
    grad_x = sum(mm("rt,rf->tf", part[:terms_in], rows) for part, rows in zip(parts, rows_in))
    leaving = jnp.concatenate([grad_x, scores], axis=1).reshape(n_z, -1, width + lanes)
    mine, early = scatter_z(lambda k: lax.dynamic_index_in_dim(leaving, z ^ k, 0, False))

    x_other = core_swap(x_half)
    dy_other = core_swap(dy_half)
    same = core == dp // parts_core
    near, far = parts[:parts_core], parts[parts_core:]
    keep = [jnp.where(same, a, b) for a, b in zip(near, far)]
    other = [core_swap(jnp.where(same, b, a)) for a, b in zip(near, far)]
    grad_gate_basis, grad_up_basis, grad_down_basis = basis_grads(
        keep,
        other,
        [x_half, x_other],
        [dy_half, dy_other],
        spot,
        (clusters, rank_own, width),
        n_dp,
        early,
    )

    mine = after(mine, grad_gate_basis).astype(BF)
    pieces = trade(
        lambda k: lax.dynamic_slice_in_dim(mine, (dp ^ k) * tok_rows, tok_rows, 0), "dp"
    )
    grad_tokens = jnp.concatenate([x[:, :width] for x in in_order(pieces, dp)], axis=1)
    by_expert = sum(x[:, width : width + experts].astype(FL) for x in pieces)[:, None, :]
    chosen = route_ids[:, :, None] == jnp.arange(experts, dtype=jnp.int32)[None, None, :]
    grad_route = jnp.sum(jnp.where(chosen, by_expert, 0.0), axis=2)
    return (
        grad_tokens,
        grad_route,
        grad_gate_basis,
        grad_up_basis,
        grad_down_basis,
        grad_gate_factor,
        grad_up_factor,
        grad_down_factor,
    )


def solution(mesh):
    n_dp, n_ex = mesh.shape["dp"], mesh.shape["expert"]
    split = Mesh(mesh.devices.reshape(n_dp, n_ex // 2, 2), ("dp", "ez", "core"))
    ex = ("ez", "core")
    rows = P(("dp", "ez", "core"), None)
    basis = P(None, ex, "dp")
    in_specs = (
        rows,
        rows,
        rows,
        rows,
        P(),
        basis,
        basis,
        basis,
        P(ex, None, "dp"),
        P(ex, None, "dp"),
        P(ex, "dp", None),
    )
    out_specs = (
        rows,
        rows,
        basis,
        basis,
        basis,
        P(ex, None, "dp"),
        P(ex, None, "dp"),
        P(ex, "dp", None),
    )
    return jax.shard_map(body, mesh=split, in_specs=in_specs, out_specs=out_specs, check_vma=False)
```

```python
import functools

import jax
import jax.numpy as jnp
from jax import lax
from jax.experimental import pallas as pl
from jax.experimental.pallas import tpu as pltpu
from jax.sharding import Mesh
from jax.sharding import PartitionSpec as P

FL = jnp.float32
BF = jnp.bfloat16
VMEM = pltpu.VMEM


def mm(spec, a, b):
    return jnp.einsum(spec, a, b, preferred_element_type=FL)


def dot(a, b, a_dim, b_dim):
    return lax.dot_general(a, b, (((a_dim,), (b_dim,)), ((), ())), preferred_element_type=FL)


def after(value, first):
    mark = lax.slice(first, (0,) * first.ndim, (1,) * first.ndim).reshape(()).astype(FL) * 0.0
    return value + mark.astype(value.dtype)


def core_swap(value):
    return lax.ppermute(value, "core", [(0, 1), (1, 0)])


def in_order(pieces, me):
    bit = 1
    while bit < len(pieces):
        odd = (me & bit) != 0
        pieces = [
            jnp.where(odd, pieces[j ^ bit], pieces[j]) for j in range(len(pieces))
        ]
        bit *= 2
    return pieces


def trade(chunk_for, axis):
    n = lax.axis_size(axis)
    sent = [lax.ppermute(chunk_for(k), axis, [(i, i ^ k) for i in range(n)]) for k in range(1, n)]
    return [chunk_for(0)] + sent


def whole(array):
    return pl.BlockSpec(array.shape, lambda *_: (0,) * array.ndim, memory_space=VMEM)


def each(array):
    shape = (1,) + array.shape[1:]
    return pl.BlockSpec(shape, lambda j: (j,) + (0,) * (array.ndim - 1), memory_space=VMEM)


SCALAR = pl.BlockSpec(memory_space=pltpu.SMEM)
ANYWHERE = pl.BlockSpec(memory_space=pl.ANY)


FREE = pl.CostEstimate(flops=0, bytes_accessed=0, transcendentals=0)


def params(total, big=False):
    return pltpu.CompilerParams(vmem_limit_bytes=(56 if big else 8 + total * 15 // 1024) << 20)


def shaped(shape, kind):
    return jax.ShapeDtypeStruct(shape, kind)


def place_rows(own, other, target, part, from_own, low):
    count = len(own)

    def fill(source):
        for c in range(own[0].shape[0]):
            for b in range(count):
                to = (c * count + b) * part
                target[to : to + part, :] = source[b][c, pl.ds(low, part), :]

    pl.when(from_own)(functools.partial(fill, own))
    pl.when(jnp.logical_not(from_own))(functools.partial(fill, other))


def project(cols, at, rows, own, other, spot, n_dp):
    half = cols.shape[0]
    count = len(own)
    clusters, rank_own, width = own[0].shape
    parts_core = n_dp // 2
    part = rank_own // parts_core
    row_count = clusters * count * part
    built = rows is None
    given = list(own) + list(other) if built else list(rows)

    def kernel(spot_ref, cols_ref, *refs):
        sources, outs = refs[: len(given)], refs[len(given) :]
        dp, core = spot_ref[0], spot_ref[1]
        parts, products = sources, outs[-n_dp:]
        if built:
            parts = outs[:n_dp]
            for k in range(n_dp):
                low = pl.multiple_of(lax.rem(dp ^ k, parts_core) * part, part)
                from_own = core == (dp ^ k) // parts_core
                place_rows(sources[:count], sources[count:], parts[k], part, from_own, low)
        for base, product in zip(parts, products):
            product[...] = dot(base[...], cols_ref[...], 1, 1).astype(BF)

    outs = [shaped((row_count, width), BF)] * n_dp if built else []
    outs += [shaped((row_count, half), BF)] * n_dp
    got = pl.pallas_call(
        kernel,
        grid=(1,),
        out_shape=outs,
        in_specs=[SCALAR, pl.BlockSpec((half, width), lambda _: (0, at), memory_space=VMEM)]
        + [whole(x) for x in given],
        out_specs=[whole(out) for out in outs],
        compiler_params=params(2 * half, True),
        cost_estimate=FREE,
        name="project",
    )(spot, cols, *given)
    return (got[:n_dp] if built else rows), got[-n_dp:]


def sum_for_groups(pieces, groups, clusters, count, firsts):
    rows, half = pieces[0].shape
    part = rows // (clusters * count)
    n_ex = groups.shape[0]

    def kernel(groups_ref, *refs):
        got, out_ref, sum_ref = refs[: len(pieces)], refs[-2], refs[-1]
        for b in range(count):
            for c in range(clusters):
                take = slice((c * count + b) * part, (c * count + b + 1) * part)
                total = got[0][take, :].astype(FL)
                for piece in got[1:]:
                    total += piece[take, :].astype(FL)
                sum_ref[c, b] = total.astype(BF)
        for e in range(n_ex):
            for b in range(count):
                out_ref[e, b * part : (b + 1) * part, :] = sum_ref[groups_ref[e], b]

    out = shaped((n_ex, count * part, half), BF)
    return pl.pallas_call(
        kernel,
        out_shape=out,
        in_specs=[SCALAR] + [whole(x) for x in pieces] + [ANYWHERE] * len(firsts),
        out_specs=whole(out),
        scratch_shapes=[pltpu.VMEM((clusters, count, part, half), BF)],
        compiler_params=params(2 * half),
        cost_estimate=FREE,
        name="sum_for_groups",
    )(groups, *pieces, *firsts)


def basis_grads(keep, other, cols, other_cols, at, spot, shape, n_dp, first):
    clusters, rank_own, width = shape
    parts_core = n_dp // 2
    part = rank_own // parts_core
    half = cols.shape[0]
    count = keep[0].shape[0] // (clusters * part)
    block = width // 2 if width % 256 == 0 else width

    skip = at * (width // block)

    def kernel(spot_ref, *refs):
        ours, theirs = refs[:parts_core], refs[parts_core : 2 * parts_core]
        cols_ref, other_ref = refs[2 * parts_core : 2 * parts_core + 2]
        outs, rows_ref = refs[-1 - count : -1], refs[-1]
        dp = spot_ref[0]

        @pl.when(pl.program_id(0) == 0)
        def _():
            for k in range(parts_core):
                low = (lax.rem(dp, parts_core) ^ k) * part
                for c in range(clusters):
                    at = pl.multiple_of(c * rank_own + low, part)
                    for b in range(count):
                        take = slice((c * count + b) * part, (c * count + b + 1) * part)
                        kind = rows_ref.dtype
                        rows_ref[0, b, pl.ds(at, part), :] = ours[k][take, :].astype(kind)
                        rows_ref[1, b, pl.ds(at, part), :] = theirs[k][take, :].astype(kind)

        for b in range(count):
            total = dot(rows_ref[0, b].astype(BF), cols_ref[...], 1, 0)
            total += dot(rows_ref[1, b].astype(BF), other_ref[...], 1, 0)
            outs[b][...] = total

    ins = list(keep) + list(other)
    out = shaped((clusters * rank_own, width), FL)
    got = pl.pallas_call(
        kernel,
        grid=(width // block,),
        out_shape=[out] * count,
        in_specs=[SCALAR]
        + [whole(x) for x in ins]
        + [pl.BlockSpec((half, block), lambda j: (0, skip + j), memory_space=VMEM)] * 2
        + [ANYWHERE],
        out_specs=[
            pl.BlockSpec((clusters * rank_own, block), lambda j: (0, j), memory_space=VMEM)
        ]
        * count,
        scratch_shapes=[pltpu.VMEM((2, count, clusters * rank_own, half), rows_kind(part))],
        compiler_params=params(2 * half),
        cost_estimate=FREE,
        name="basis_grads",
    )(spot, *ins, cols, other_cols, first)
    return [grad.reshape(shape) for grad in got]


def make_picks(cell, weight, slots):
    local, _, total = cell.shape

    def kernel(cell_ref, weight_ref, pick_ref, slot_ref):
        hit = cell_ref[0] == lax.broadcasted_iota(jnp.int32, (slots, total), 0)
        pick_ref[0] = jnp.where(hit, 1.0, 0.0).astype(BF)
        slot_ref[0] = jnp.sum(jnp.where(hit, weight_ref[0], 0.0), axis=1, keepdims=True)

    outs = [shaped((local, slots, total), BF), shaped((local, slots, 1), FL)]
    return pl.pallas_call(
        kernel,
        grid=(local,),
        out_shape=outs,
        in_specs=[each(cell), each(weight)],
        out_specs=[each(out) for out in outs],
        compiler_params=params(total),
        cost_estimate=FREE,
        name="make_picks",
    )(cell, weight)


def lay_out(pieces, target, me, count):
    n_dp = len(pieces)
    n_ex, rows, half = pieces[0].shape
    part = rows // count
    for k in range(n_dp):
        for e in range(n_ex):
            at = pl.multiple_of(((e // 2) * n_dp + (me ^ k)) * part, part)
            for b in range(count):
                piece = pieces[k][e, b * part : (b + 1) * part, :]
                target[b, pl.ds(at, part), (e % 2) * half : (e % 2 + 1) * half] = piece.astype(
                    target.dtype
                )


def rows_kind(part):
    return BF if part % 16 == 0 else FL


def hand_out(source, pieces, me, count):
    n_dp = len(pieces)
    n_ex, rows, half = pieces[0].shape
    part = rows // count
    for k in range(n_dp):
        for e in range(n_ex):
            at = pl.multiple_of(((e // 2) * n_dp + (me ^ k)) * part, part)
            for b in range(count):
                pieces[k][e, b * part : (b + 1) * part, :] = source[
                    b, pl.ds(at, part), (e % 2) * half : (e % 2 + 1) * half
                ].astype(BF)


def forward(pieces, pick, weight, gate_factor, up_factor, down_factor, dp):
    n_dp = len(pieces)
    n_ex, rows, half = pieces[0].shape
    local, slots, total = pick.shape
    rank, hid = gate_factor.shape[1:]

    def kernel(dp_ref, *refs):
        got, refs = refs[:n_dp], refs[n_dp:]
        pick_ref, weight_ref, gate_ref, up_ref, down_ref = refs[:5]
        hg_ref, hu_ref, hidden_ref, mixed_ref, act_ref, lift_ref = refs[5:11]
        sent = refs[11 : 11 + n_dp]
        rows_ref, total_ref = refs[11 + n_dp :]
        j = pl.program_id(0)
        me = dp_ref[0]

        @pl.when(j == 0)
        def _():
            lay_out(got, rows_ref, me, 2)
            total_ref[...] = jnp.zeros_like(total_ref)

        take = pick_ref[0]
        hg = dot(take, rows_ref[0].astype(BF), 1, 1).astype(BF)
        hu = dot(take, rows_ref[1].astype(BF), 1, 1).astype(BF)
        hg_ref[0] = hg
        hu_ref[0] = hu
        gate_pre = dot(hg, gate_ref[0], 1, 0)
        up_pre = dot(hu, up_ref[0], 1, 0)
        sig = 1.0 / (1.0 + jnp.exp(-gate_pre))
        act = gate_pre * sig
        act_ref[0] = act
        lift_ref[0] = up_pre * (sig * (1.0 + gate_pre * (1.0 - sig)))
        hidden = (act * up_pre).astype(BF)
        hidden_ref[0] = hidden
        mixed = dot(hidden, down_ref[0], 1, 0).astype(BF)
        mixed_ref[0] = mixed
        total_ref[0] += dot(mixed, (take * weight_ref[0]).astype(BF), 0, 0)

        @pl.when(j == local - 1)
        def _():
            hand_out(total_ref, sent, me, 1)

    slot_shape = (local, slots, rank)
    hid_shape = (local, slots, hid)
    outs = [
        shaped(slot_shape, BF),
        shaped(slot_shape, BF),
        shaped(hid_shape, BF),
        shaped(slot_shape, BF),
        shaped(hid_shape, FL),
        shaped(hid_shape, FL),
    ]
    chunks = [shaped((n_ex, rows // 2, half), BF)] * n_dp
    got = pl.pallas_call(
        kernel,
        grid=(local,),
        out_shape=outs + chunks,
        in_specs=[SCALAR]
        + [whole(piece) for piece in pieces]
        + [each(x) for x in (pick, weight, gate_factor, up_factor, down_factor)],
        out_specs=[each(out) for out in outs] + [whole(chunk) for chunk in chunks],
        scratch_shapes=[pltpu.VMEM((2, rank, total), rows_kind(rows // 2)), pltpu.VMEM((1, rank, total), FL)],
        compiler_params=params(total, True),
        cost_estimate=FREE,
        name="forward",
    )(dp.reshape(1), *pieces, pick, weight, gate_factor, up_factor, down_factor)
    return got[:6], got[6:]


def backward(pieces, pick, weight, mixed, act, lift, gate_factor, up_factor, down_factor, dp):
    n_dp = len(pieces)
    n_ex, rows, half = pieces[0].shape
    local, slots, total = pick.shape
    rank, hid = gate_factor.shape[1:]

    def kernel(dp_ref, *refs):
        got, refs = refs[:n_dp], refs[n_dp:]
        pick_ref, weight_ref, mixed_ref, act_ref, lift_ref = refs[:5]
        gate_ref, up_ref, down_ref = refs[5:8]
        back_ref, gate_out, up_out, dots_ref = refs[8:12]
        sent = refs[12 : 12 + n_dp]
        rows_ref, total_ref = refs[12 + n_dp :]
        j = pl.program_id(0)
        me = dp_ref[0]

        @pl.when(j == 0)
        def _():
            lay_out(got, rows_ref, me, 1)
            total_ref[...] = jnp.zeros_like(total_ref)

        take = pick_ref[0]
        hd = dot(take, rows_ref[0].astype(BF), 1, 1)
        dots_ref[0] = jnp.sum(mixed_ref[0].astype(FL) * hd, axis=1, keepdims=True)
        back = (weight_ref[0] * hd).astype(BF)
        back_ref[0] = back
        grad_hidden = dot(back, down_ref[0], 1, 1)
        grad_gate = (grad_hidden * lift_ref[0]).astype(BF)
        grad_up = (grad_hidden * act_ref[0]).astype(BF)
        gate_out[0] = grad_gate
        up_out[0] = grad_up
        total_ref[0] += dot(dot(grad_gate, gate_ref[0], 1, 1).astype(BF), take, 0, 0)
        total_ref[1] += dot(dot(grad_up, up_ref[0], 1, 1).astype(BF), take, 0, 0)

        @pl.when(j == local - 1)
        def _():
            hand_out(total_ref, sent, me, 2)

    outs = [
        shaped((local, slots, rank), BF),
        shaped((local, slots, hid), BF),
        shaped((local, slots, hid), BF),
        shaped((local, slots, 1), FL),
    ]
    chunks = [shaped((n_ex, 2 * rows, half), BF)] * n_dp
    ins = (pick, weight, mixed, act, lift, gate_factor, up_factor, down_factor)
    got = pl.pallas_call(
        kernel,
        grid=(local,),
        out_shape=outs + chunks,
        in_specs=[SCALAR] + [whole(piece) for piece in pieces] + [each(x) for x in ins],
        out_specs=[each(out) for out in outs] + [whole(chunk) for chunk in chunks],
        scratch_shapes=[pltpu.VMEM((1, rank, total), rows_kind(rows)), pltpu.VMEM((2, rank, total), FL)],
        compiler_params=params(total, True),
        cost_estimate=pl.CostEstimate(
            flops=local * slots * rank * (6 * total + 6 * hid),
            bytes_accessed=32 << 20,
            transcendentals=0,
        ),
        name="backward",
    )(dp.reshape(1), *pieces, *ins)
    return got[:4], got[4:]


def factor_grads(hg, grad_gate, hu, grad_up, hidden, back, total, first):
    local, slots, rank = hg.shape
    hid = hidden.shape[2]

    def kernel(hg_ref, gate_ref, hu_ref, up_ref, hidden_ref, back_ref, _, out_g, out_u, out_d):
        out_g[0] = dot(hg_ref[0], gate_ref[0], 0, 0)
        out_u[0] = dot(hu_ref[0], up_ref[0], 0, 0)
        out_d[0] = dot(hidden_ref[0], back_ref[0], 0, 0)

    outs = [
        shaped((local, rank, hid), FL),
        shaped((local, rank, hid), FL),
        shaped((local, hid, rank), FL),
    ]
    ins = (hg, grad_gate, hu, grad_up, hidden, back)
    return pl.pallas_call(
        kernel,
        grid=(local,),
        out_shape=outs,
        in_specs=[each(x) for x in ins] + [ANYWHERE],
        out_specs=[each(out) for out in outs],
        compiler_params=params(total),
        cost_estimate=FREE,
        name="factor_grads",
    )(*ins, first)


def body(
    tokens,
    grad_out,
    route_ids,
    route_weight,
    cluster_of,
    gate_basis,
    up_basis,
    down_basis,
    gate_factor,
    up_factor,
    down_factor,
):
    n_dp = lax.axis_size("dp")
    n_z = lax.axis_size("ez")
    n_ex = n_z * 2
    dp = lax.axis_index("dp")
    z = lax.axis_index("ez")
    core = lax.axis_index("core")
    me_e = z * 2 + core
    tok_rows, model_width = tokens.shape
    top = route_ids.shape[1]
    local = gate_factor.shape[0]
    experts = local * n_ex
    capacity = max(2, 5 * tok_rows * top // (4 * experts))
    blocks = n_dp * n_ex
    total = blocks * tok_rows
    half = total // 2
    slots = blocks * capacity
    clusters, rank_own, width = gate_basis.shape
    parts_core = n_dp // 2
    rank_part = rank_own // parts_core

    lanes = 128

    routing = jnp.concatenate([route_ids.astype(BF), route_weight], axis=1)
    routing = jnp.pad(routing, ((0, 0), (0, lanes - 2 * top)))
    leaving = [
        grad_out.reshape(tok_rows, n_dp, width),
        tokens.reshape(tok_rows, n_dp, width),
        jnp.broadcast_to(routing[:, None], (tok_rows, n_dp, lanes)),
    ]
    leaving = jnp.concatenate(leaving, axis=2).transpose(1, 0, 2)
    leaving = jnp.broadcast_to(leaving[:, None], (n_dp, n_z) + leaving.shape[1:])
    cols = lax.all_to_all(
        leaving.reshape(n_dp * n_z, tok_rows, -1),
        ("dp", "ez"),
        split_axis=0,
        concat_axis=0,
        tiled=True,
    ).reshape(half, 2 * width + lanes)
    spot = jnp.stack([dp, core]).astype(jnp.int32)

    def chip_rows(own, other):
        if rank_part % 16 == 0:
            return None
        count = len(own)
        shape = (clusters, count, parts_core, rank_part, width)
        own = jnp.stack(own, axis=1).reshape(shape)
        other = jnp.stack(other, axis=1).reshape(shape)
        result = []
        for k in range(n_dp):
            part = dp ^ k
            at = part % parts_core
            mine = lax.dynamic_index_in_dim(own, at, 2, False)
            theirs = lax.dynamic_index_in_dim(other, at, 2, False)
            rows = jnp.where(part // parts_core == core, mine, theirs)
            result.append(rows.reshape(clusters * count * rank_part, width))
        return result

    own_in, own_out = [gate_basis, up_basis], [down_basis]
    other_in = [core_swap(basis) for basis in own_in]
    other_out = [core_swap(basis) for basis in own_out]

    routing = cols[:, 2 * width :]
    swapped = core_swap(routing)
    routing = jnp.stack(
        [jnp.where(core == 0, routing, swapped), jnp.where(core == 0, swapped, routing)]
    )
    routing = routing.reshape(blocks, tok_rows, lanes)
    ids = routing[:, :, :top].astype(jnp.int32)
    weights = routing[:, :, top : 2 * top].astype(FL)
    own_ids = me_e * local + jnp.arange(local, dtype=jnp.int32)
    hit = ids[None] == own_ids[:, None, None, None]
    named = jnp.any(hit, axis=3)
    weight_of = jnp.sum(jnp.where(hit, weights[None], 0.0), axis=3)
    order = jnp.cumsum(named.astype(jnp.int32), axis=2) - 1
    cell = jnp.arange(blocks, dtype=jnp.int32)[None, :, None] * capacity + order
    cell = jnp.where(named, cell, -1).reshape(local, 1, total)
    weight_of = weight_of.reshape(local, 1, total)
    pick, slot_weight = make_picks(cell, weight_of, slots)

    group_cluster = cluster_of.reshape(n_ex, local)[:, 0]

    def sum_parts(got):
        return sum(piece.astype(FL) for piece in got).astype(BF)

    def spread(mine):
        return lax.all_to_all(mine, ("ez", "core"), split_axis=0, concat_axis=0, tiled=True)

    rows_in, terms = project(
        cols, 1, chip_rows(own_in, other_in), own_in, other_in, spot, n_dp
    )
    _, terms_out = project(
        cols, 0, chip_rows(own_out, other_out), own_out, other_out, spot, n_dp
    )
    mine_in = sum_for_groups(trade(lambda k: terms[k], "dp"), group_cluster, clusters, 2, terms_out[:1])
    got_in = spread(mine_in)
    h_pieces = trade(lambda k: got_in, "dp")
    mine_out = sum_for_groups(
        trade(lambda k: terms_out[k], "dp"), group_cluster, clusters, 1, h_pieces[1:]
    )
    got_out = spread(mine_out)
    (hg, hu, hidden, mixed, act, lift), mixed_chunks = forward(
        h_pieces, pick, weight_of, gate_factor, up_factor, down_factor, dp
    )
    d_pieces = trade(lambda k: got_out, "dp")
    (back, grad_gate, grad_up, dots), in_chunks = backward(
        d_pieces, pick, slot_weight, mixed, act, lift, gate_factor, up_factor, down_factor, dp
    )

    numbers = jnp.arange(clusters, dtype=jnp.int32)[:, None]

    def by_cluster(got, groups):
        owner = (groups[None, :] == numbers)[:, :, None, None]
        summed = jnp.sum(jnp.where(owner, got.astype(FL)[None], 0.0), axis=1)
        return summed.astype(BF).reshape(-1, half)

    mixed_mine = sum_parts(trade(lambda k: mixed_chunks[k], "dp"))
    in_mine = sum_parts(trade(lambda k: in_chunks[k], "dp"))
    grad_gate_factor, grad_up_factor, grad_down_factor = factor_grads(
        hg, grad_gate, hu, grad_up, hidden, back, total, in_mine
    )
    mine = jnp.concatenate([in_mine, mixed_mine], axis=1)
    got = spread(mine)
    in_sum = after(by_cluster(got[:, : 2 * rank_part], group_cluster), grad_gate_factor)
    mixed_sum = by_cluster(got[:, 2 * rank_part :], group_cluster)
    in_parts = trade(lambda k: in_sum, "dp")

    placed = cell == jnp.arange(slots, dtype=jnp.int32)[None, :, None]
    scores = jnp.sum(jnp.where(placed, dots, 0.0), axis=1).reshape(local, 2, half)
    mine = jnp.where(core == 0, scores[:, 0], scores[:, 1])
    theirs = core_swap(jnp.where(core == 0, scores[:, 1], scores[:, 0]))
    first = jnp.where(core == 0, mine, theirs)
    second = jnp.where(core == 0, theirs, mine)
    scores = jnp.concatenate([first, second], axis=0).T.astype(BF)
    scores = jnp.pad(scores, ((0, 0), (0, lanes - 2 * local)))

    grad_x = sum(mm("rt,rf->tf", part, rows) for part, rows in zip(in_parts, rows_in))
    leaving = jnp.concatenate([grad_x.astype(BF), scores], axis=1)
    rows = leaving.reshape(n_dp * n_z, tok_rows, width + lanes)
    rows = lax.all_to_all(rows, ("dp", "ez"), split_axis=0, concat_axis=0, tiled=True)
    rows = rows.reshape(n_dp, n_z, tok_rows, width + lanes)
    other_cols = core_swap(cols)
    same = core == dp // parts_core

    def own_ranks(parts):
        near, far = parts[:parts_core], parts[parts_core:]
        keep = [jnp.where(same, a, b) for a, b in zip(near, far)]
        other = [core_swap(jnp.where(same, b, a)) for a, b in zip(near, far)]
        return keep, other

    shape = (clusters, rank_own, width)
    grad_gate_basis, grad_up_basis = basis_grads(
        *own_ranks(in_parts), cols, other_cols, 1, spot, shape, n_dp, leaving
    )
    mixed_sum = after(mixed_sum, grad_gate_basis)
    mixed_parts = trade(lambda k: mixed_sum, "dp")
    (grad_down_basis,) = basis_grads(
        *own_ranks(mixed_parts), cols, other_cols, 0, spot, shape, n_dp, leaving
    )

    grad_rows = jnp.sum(rows[..., :width].astype(FL), axis=1)
    grad_rows = after(grad_rows, grad_down_basis)
    grad_tokens = grad_rows.astype(BF).transpose(1, 0, 2).reshape(tok_rows, model_width)
    by_expert = jnp.sum(rows[..., width : width + 2 * local].astype(FL), axis=0)
    by_expert = by_expert.transpose(1, 0, 2).reshape(tok_rows, 1, experts)
    chosen = route_ids[:, :, None] == jnp.arange(experts, dtype=jnp.int32)[None, None, :]
    grad_route = jnp.sum(jnp.where(chosen, by_expert, 0.0), axis=2)
    return (
        grad_tokens,
        grad_route,
        grad_gate_basis,
        grad_up_basis,
        grad_down_basis,
        grad_gate_factor,
        grad_up_factor,
        grad_down_factor,
    )


def solution(mesh):
    n_dp, n_ex = mesh.shape["dp"], mesh.shape["expert"]
    split = Mesh(mesh.devices.reshape(n_dp, n_ex // 2, 2), ("dp", "ez", "core"))
    ex = ("ez", "core")
    rows = P(("dp", "ez", "core"), None)
    basis = P(None, ex, "dp")
    in_specs = (
        rows,
        rows,
        rows,
        rows,
        P(),
        basis,
        basis,
        basis,
        P(ex, None, "dp"),
        P(ex, None, "dp"),
        P(ex, "dp", None),
    )
    out_specs = (
        rows,
        rows,
        basis,
        basis,
        basis,
        P(ex, None, "dp"),
        P(ex, None, "dp"),
        P(ex, "dp", None),
    )
    return jax.shard_map(body, mesh=split, in_specs=in_specs, out_specs=out_specs, check_vma=False)
```

```python
import functools

import jax
import jax.numpy as jnp
from jax import lax
from jax.experimental import pallas as pl
from jax.experimental.pallas import tpu as pltpu
from jax.sharding import Mesh
from jax.sharding import PartitionSpec as P

FL = jnp.float32
BF = jnp.bfloat16
VMEM = pltpu.VMEM


def mm(spec, a, b):
    return jnp.einsum(spec, a, b, preferred_element_type=FL)


def dot(a, b, a_dim, b_dim):
    return lax.dot_general(a, b, (((a_dim,), (b_dim,)), ((), ())), preferred_element_type=FL)


def after(value, first):
    mark = lax.slice(first, (0,) * first.ndim, (1,) * first.ndim).reshape(()).astype(FL) * 0.0
    return value + mark.astype(value.dtype)


def core_swap(value):
    return lax.ppermute(value, "core", [(0, 1), (1, 0)])


def in_order(pieces, me):
    bit = 1
    while bit < len(pieces):
        odd = (me & bit) != 0
        pieces = [
            jnp.where(odd, pieces[j ^ bit], pieces[j]) for j in range(len(pieces))
        ]
        bit *= 2
    return pieces


def trade(chunk_for, axis):
    n = lax.axis_size(axis)
    sent = [lax.ppermute(chunk_for(k), axis, [(i, i ^ k) for i in range(n)]) for k in range(1, n)]
    return [chunk_for(0)] + sent


def whole(array):
    return pl.BlockSpec(array.shape, lambda *_: (0,) * array.ndim, memory_space=VMEM)


def each(array):
    shape = (1,) + array.shape[1:]
    return pl.BlockSpec(shape, lambda j: (j,) + (0,) * (array.ndim - 1), memory_space=VMEM)


SCALAR = pl.BlockSpec(memory_space=pltpu.SMEM)
ANYWHERE = pl.BlockSpec(memory_space=pl.ANY)


FREE = pl.CostEstimate(flops=0, bytes_accessed=0, transcendentals=0)


def params(total, big=False):
    return pltpu.CompilerParams(vmem_limit_bytes=(56 if big else 8 + total * 15 // 1024) << 20)


def shaped(shape, kind):
    return jax.ShapeDtypeStruct(shape, kind)


def place_rows(own, other, target, part, from_own, low):
    count = len(own)

    def fill(source):
        for c in range(own[0].shape[0]):
            for b in range(count):
                to = (c * count + b) * part
                target[to : to + part, :] = source[b][c, pl.ds(low, part), :]

    pl.when(from_own)(functools.partial(fill, own))
    pl.when(jnp.logical_not(from_own))(functools.partial(fill, other))


def project(cols, rows, own, other, spot, n_dp):
    half = cols.shape[0]
    count = len(own)
    clusters, rank_own, width = own[0].shape
    parts_core = n_dp // 2
    part = rank_own // parts_core
    row_count = clusters * count * part
    built = rows is None
    ins = [cols] + (list(own) + list(other) if built else list(rows))

    def kernel(spot_ref, cols_ref, *refs):
        sources, outs = refs[: len(ins) - 1], refs[len(ins) - 1 :]
        dp, core = spot_ref[0], spot_ref[1]
        parts, products = sources, outs[-n_dp:]
        if built:
            parts = outs[:n_dp]
            for k in range(n_dp):
                low = pl.multiple_of(lax.rem(dp ^ k, parts_core) * part, part)
                from_own = core == (dp ^ k) // parts_core
                place_rows(sources[:count], sources[count:], parts[k], part, from_own, low)
        for base, product in zip(parts, products):
            product[...] = dot(base[...], cols_ref[:, :width], 1, 1).astype(BF)

    outs = [shaped((row_count, width), BF)] * n_dp if built else []
    outs += [shaped((row_count, half), BF)] * n_dp
    got = pl.pallas_call(
        kernel,
        out_shape=outs,
        in_specs=[SCALAR] + [whole(x) for x in ins],
        out_specs=[whole(out) for out in outs],
        compiler_params=params(2 * half, True),
        cost_estimate=FREE,
        name="project",
    )(spot, *ins)
    return (got[:n_dp] if built else rows), got[-n_dp:]


def sum_for_groups(pieces, groups, clusters, count, firsts):
    rows, half = pieces[0].shape
    part = rows // (clusters * count)
    n_ex = groups.shape[0]

    def kernel(groups_ref, *refs):
        got, out_ref, sum_ref = refs[: len(pieces)], refs[-2], refs[-1]
        for b in range(count):
            for c in range(clusters):
                take = slice((c * count + b) * part, (c * count + b + 1) * part)
                total = got[0][take, :].astype(FL)
                for piece in got[1:]:
                    total += piece[take, :].astype(FL)
                sum_ref[c, b] = total.astype(BF)
        for e in range(n_ex):
            for b in range(count):
                out_ref[e, b * part : (b + 1) * part, :] = sum_ref[groups_ref[e], b]

    out = shaped((n_ex, count * part, half), BF)
    return pl.pallas_call(
        kernel,
        out_shape=out,
        in_specs=[SCALAR] + [whole(x) for x in pieces] + [ANYWHERE] * len(firsts),
        out_specs=whole(out),
        scratch_shapes=[pltpu.VMEM((clusters, count, part, half), BF)],
        compiler_params=params(2 * half),
        cost_estimate=FREE,
        name="sum_for_groups",
    )(groups, *pieces, *firsts)


def basis_grads(keep, other, cols, other_cols, spot, shape, n_dp, first):
    clusters, rank_own, width = shape
    parts_core = n_dp // 2
    part = rank_own // parts_core
    half = cols.shape[0]
    count = keep[0].shape[0] // (clusters * part)
    block = width // 2 if width % 256 == 0 else width

    def kernel(spot_ref, *refs):
        ours, theirs = refs[:parts_core], refs[parts_core : 2 * parts_core]
        cols_ref, other_ref = refs[2 * parts_core : 2 * parts_core + 2]
        outs, rows_ref = refs[-1 - count : -1], refs[-1]
        dp = spot_ref[0]

        @pl.when(pl.program_id(0) == 0)
        def _():
            for k in range(parts_core):
                low = (lax.rem(dp, parts_core) ^ k) * part
                for c in range(clusters):
                    at = pl.multiple_of(c * rank_own + low, part)
                    for b in range(count):
                        take = slice((c * count + b) * part, (c * count + b + 1) * part)
                        kind = rows_ref.dtype
                        rows_ref[0, b, pl.ds(at, part), :] = ours[k][take, :].astype(kind)
                        rows_ref[1, b, pl.ds(at, part), :] = theirs[k][take, :].astype(kind)

        for b in range(count):
            total = dot(rows_ref[0, b].astype(BF), cols_ref[...], 1, 0)
            total += dot(rows_ref[1, b].astype(BF), other_ref[...], 1, 0)
            outs[b][...] = total

    ins = list(keep) + list(other)
    out = shaped((clusters * rank_own, width), FL)
    got = pl.pallas_call(
        kernel,
        grid=(width // block,),
        out_shape=[out] * count,
        in_specs=[SCALAR]
        + [whole(x) for x in ins]
        + [pl.BlockSpec((half, block), lambda j: (0, j), memory_space=VMEM)] * 2
        + [ANYWHERE],
        out_specs=[
            pl.BlockSpec((clusters * rank_own, block), lambda j: (0, j), memory_space=VMEM)
        ]
        * count,
        scratch_shapes=[pltpu.VMEM((2, count, clusters * rank_own, half), rows_kind(part))],
        compiler_params=params(2 * half),
        cost_estimate=FREE,
        name="basis_grads",
    )(spot, *ins, cols, other_cols, first)
    return [grad.reshape(shape) for grad in got]


def make_picks(cell, weight, slots):
    local, _, total = cell.shape

    def kernel(cell_ref, weight_ref, pick_ref, slot_ref):
        hit = cell_ref[0] == lax.broadcasted_iota(jnp.int32, (slots, total), 0)
        pick_ref[0] = jnp.where(hit, 1.0, 0.0).astype(BF)
        slot_ref[0] = jnp.sum(jnp.where(hit, weight_ref[0], 0.0), axis=1, keepdims=True)

    outs = [shaped((local, slots, total), BF), shaped((local, slots, 1), FL)]
    return pl.pallas_call(
        kernel,
        grid=(local,),
        out_shape=outs,
        in_specs=[each(cell), each(weight)],
        out_specs=[each(out) for out in outs],
        compiler_params=params(total),
        cost_estimate=FREE,
        name="make_picks",
    )(cell, weight)


def lay_out(pieces, target, me, count):
    n_dp = len(pieces)
    n_ex, rows, half = pieces[0].shape
    part = rows // count
    for k in range(n_dp):
        for e in range(n_ex):
            at = pl.multiple_of(((e // 2) * n_dp + (me ^ k)) * part, part)
            for b in range(count):
                piece = pieces[k][e, b * part : (b + 1) * part, :]
                target[b, pl.ds(at, part), (e % 2) * half : (e % 2 + 1) * half] = piece.astype(
                    target.dtype
                )


def rows_kind(part):
    return BF if part % 16 == 0 else FL


def hand_out(source, pieces, me, count):
    n_dp = len(pieces)
    n_ex, rows, half = pieces[0].shape
    part = rows // count
    for k in range(n_dp):
        for e in range(n_ex):
            at = pl.multiple_of(((e // 2) * n_dp + (me ^ k)) * part, part)
            for b in range(count):
                pieces[k][e, b * part : (b + 1) * part, :] = source[
                    b, pl.ds(at, part), (e % 2) * half : (e % 2 + 1) * half
                ].astype(BF)


def forward(pieces, pick, gate_factor, up_factor, down_factor, dp):
    n_dp = len(pieces)
    n_ex, rows, half = pieces[0].shape
    local, slots, total = pick.shape
    rank, hid = gate_factor.shape[1:]

    def kernel(dp_ref, *refs):
        got, refs = refs[:n_dp], refs[n_dp:]
        pick_ref, gate_ref, up_ref, down_ref = refs[:4]
        hg_ref, hu_ref, hidden_ref, mixed_ref, act_ref, lift_ref, rows_ref = refs[4:]
        j = pl.program_id(0)
        me = dp_ref[0]

        @pl.when(j == 0)
        def _():
            lay_out(got, rows_ref, me, 2)

        take = pick_ref[0]
        hg = dot(take, rows_ref[0].astype(BF), 1, 1).astype(BF)
        hu = dot(take, rows_ref[1].astype(BF), 1, 1).astype(BF)
        hg_ref[0] = hg
        hu_ref[0] = hu
        gate_pre = dot(hg, gate_ref[0], 1, 0)
        up_pre = dot(hu, up_ref[0], 1, 0)
        sig = 1.0 / (1.0 + jnp.exp(-gate_pre))
        act = gate_pre * sig
        act_ref[0] = act
        lift_ref[0] = up_pre * (sig * (1.0 + gate_pre * (1.0 - sig)))
        hidden = (act * up_pre).astype(BF)
        hidden_ref[0] = hidden
        mixed_ref[0] = dot(hidden, down_ref[0], 1, 0).astype(BF)

    slot_shape = (local, slots, rank)
    hid_shape = (local, slots, hid)
    outs = [
        shaped(slot_shape, BF),
        shaped(slot_shape, BF),
        shaped(hid_shape, BF),
        shaped(slot_shape, BF),
        shaped(hid_shape, FL),
        shaped(hid_shape, FL),
    ]
    return pl.pallas_call(
        kernel,
        grid=(local,),
        out_shape=outs,
        in_specs=[SCALAR]
        + [whole(piece) for piece in pieces]
        + [each(x) for x in (pick, gate_factor, up_factor, down_factor)],
        out_specs=[each(out) for out in outs],
        scratch_shapes=[pltpu.VMEM((2, rank, total), rows_kind(rows // 2))],
        compiler_params=params(total, True),
        cost_estimate=FREE,
        name="forward",
    )(dp.reshape(1), *pieces, pick, gate_factor, up_factor, down_factor)


def backward(pieces, pick, weight, mixed, act, lift, gate_factor, up_factor, down_factor, dp):
    n_dp = len(pieces)
    n_ex, rows, half = pieces[0].shape
    local, slots, total = pick.shape
    rank, hid = gate_factor.shape[1:]

    def kernel(dp_ref, *refs):
        got, refs = refs[:n_dp], refs[n_dp:]
        pick_ref, weight_ref, mixed_ref, act_ref, lift_ref = refs[:5]
        gate_ref, up_ref, down_ref = refs[5:8]
        back_ref, gate_out, up_out, dots_ref = refs[8:12]
        sent = refs[12 : 12 + n_dp]
        rows_ref, total_ref = refs[12 + n_dp :]
        j = pl.program_id(0)
        me = dp_ref[0]

        @pl.when(j == 0)
        def _():
            lay_out(got, rows_ref, me, 1)
            total_ref[...] = jnp.zeros_like(total_ref)

        take = pick_ref[0]
        hd = dot(take, rows_ref[0].astype(BF), 1, 1)
        dots_ref[0] = jnp.sum(mixed_ref[0].astype(FL) * hd, axis=1, keepdims=True)
        back = (weight_ref[0] * hd).astype(BF)
        back_ref[0] = back
        grad_hidden = dot(back, down_ref[0], 1, 1)
        grad_gate = (grad_hidden * lift_ref[0]).astype(BF)
        grad_up = (grad_hidden * act_ref[0]).astype(BF)
        gate_out[0] = grad_gate
        up_out[0] = grad_up
        total_ref[0] += dot(dot(grad_gate, gate_ref[0], 1, 1).astype(BF), take, 0, 0)
        total_ref[1] += dot(dot(grad_up, up_ref[0], 1, 1).astype(BF), take, 0, 0)

        @pl.when(j == local - 1)
        def _():
            hand_out(total_ref, sent, me, 2)

    outs = [
        shaped((local, slots, rank), BF),
        shaped((local, slots, hid), BF),
        shaped((local, slots, hid), BF),
        shaped((local, slots, 1), FL),
    ]
    chunks = [shaped((n_ex, 2 * rows, half), BF)] * n_dp
    ins = (pick, weight, mixed, act, lift, gate_factor, up_factor, down_factor)
    got = pl.pallas_call(
        kernel,
        grid=(local,),
        out_shape=outs + chunks,
        in_specs=[SCALAR] + [whole(piece) for piece in pieces] + [each(x) for x in ins],
        out_specs=[each(out) for out in outs] + [whole(chunk) for chunk in chunks],
        scratch_shapes=[pltpu.VMEM((1, rank, total), rows_kind(rows)), pltpu.VMEM((2, rank, total), FL)],
        compiler_params=params(total, True),
        cost_estimate=pl.CostEstimate(
            flops=local * slots * rank * (6 * total + 6 * hid),
            bytes_accessed=32 << 20,
            transcendentals=0,
        ),
        name="backward",
    )(dp.reshape(1), *pieces, *ins)
    return got[:4], got[4:]


def mixed_sums(mixed, pick, weight, dp, chunk, n_dp, first):
    local, slots, rank = mixed.shape
    total = pick.shape[2]

    def kernel(dp_ref, mixed_ref, pick_ref, weight_ref, *refs):
        sent, total_ref = refs[1:-1], refs[-1]
        j = pl.program_id(0)
        heavy = (pick_ref[0] * weight_ref[0]).astype(BF)
        term = dot(mixed_ref[0], heavy, 0, 0)

        @pl.when(j == 0)
        def _():
            total_ref[0] = term

        @pl.when(j > 0)
        def _():
            total_ref[0] += term

        @pl.when(j == local - 1)
        def _():
            hand_out(total_ref, sent, dp_ref[0], 1)

    chunks = [shaped(chunk, BF)] * n_dp
    return pl.pallas_call(
        kernel,
        grid=(local,),
        out_shape=chunks,
        in_specs=[SCALAR, each(mixed), each(pick), each(weight), ANYWHERE],
        out_specs=[whole(out) for out in chunks],
        scratch_shapes=[pltpu.VMEM((1, rank, total), FL)],
        compiler_params=params(total),
        cost_estimate=FREE,
        name="mixed_sums",
    )(dp.reshape(1), mixed, pick, weight, first)


def factor_grads(hg, grad_gate, hu, grad_up, hidden, back, total, first):
    local, slots, rank = hg.shape
    hid = hidden.shape[2]

    def kernel(hg_ref, gate_ref, hu_ref, up_ref, hidden_ref, back_ref, _, out_g, out_u, out_d):
        out_g[0] = dot(hg_ref[0], gate_ref[0], 0, 0)
        out_u[0] = dot(hu_ref[0], up_ref[0], 0, 0)
        out_d[0] = dot(hidden_ref[0], back_ref[0], 0, 0)

    outs = [
        shaped((local, rank, hid), FL),
        shaped((local, rank, hid), FL),
        shaped((local, hid, rank), FL),
    ]
    ins = (hg, grad_gate, hu, grad_up, hidden, back)
    return pl.pallas_call(
        kernel,
        grid=(local,),
        out_shape=outs,
        in_specs=[each(x) for x in ins] + [ANYWHERE],
        out_specs=[each(out) for out in outs],
        compiler_params=params(total),
        cost_estimate=FREE,
        name="factor_grads",
    )(*ins, first)


def body(
    tokens,
    grad_out,
    route_ids,
    route_weight,
    cluster_of,
    gate_basis,
    up_basis,
    down_basis,
    gate_factor,
    up_factor,
    down_factor,
):
    n_dp = lax.axis_size("dp")
    n_z = lax.axis_size("ez")
    n_ex = n_z * 2
    dp = lax.axis_index("dp")
    z = lax.axis_index("ez")
    core = lax.axis_index("core")
    me_e = z * 2 + core
    tok_rows, model_width = tokens.shape
    top = route_ids.shape[1]
    local = gate_factor.shape[0]
    experts = local * n_ex
    capacity = max(2, 5 * tok_rows * top // (4 * experts))
    blocks = n_dp * n_ex
    total = blocks * tok_rows
    half = total // 2
    slots = blocks * capacity
    clusters, rank_own, width = gate_basis.shape
    parts_core = n_dp // 2
    rank_part = rank_own // parts_core

    lanes = 128

    def own_columns(rows, more):
        rows = rows.reshape(tok_rows, n_dp, width).transpose(1, 0, 2)
        if more is not None:
            more = jnp.broadcast_to(more[None], (n_dp, tok_rows, lanes))
            rows = jnp.concatenate([rows, more], axis=2)
        rows = jnp.broadcast_to(rows[:, None], (n_dp, n_z) + rows.shape[1:])
        rows = rows.reshape(n_dp * n_z, tok_rows, -1)
        got = lax.all_to_all(rows, ("dp", "ez"), split_axis=0, concat_axis=0, tiled=True)
        return got.reshape(half, -1)

    routing = jnp.concatenate([route_ids.astype(BF), route_weight], axis=1)
    routing = jnp.pad(routing, ((0, 0), (0, lanes - 2 * top)))
    x_half = own_columns(tokens, routing)
    dy_half = own_columns(after(grad_out, x_half), None)
    spot = jnp.stack([dp, core]).astype(jnp.int32)

    def chip_rows(own, other):
        if rank_part % 16 == 0:
            return None
        count = len(own)
        shape = (clusters, count, parts_core, rank_part, width)
        own = jnp.stack(own, axis=1).reshape(shape)
        other = jnp.stack(other, axis=1).reshape(shape)
        result = []
        for k in range(n_dp):
            part = dp ^ k
            at = part % parts_core
            mine = lax.dynamic_index_in_dim(own, at, 2, False)
            theirs = lax.dynamic_index_in_dim(other, at, 2, False)
            rows = jnp.where(part // parts_core == core, mine, theirs)
            result.append(rows.reshape(clusters * count * rank_part, width))
        return result

    own_in, own_out = [gate_basis, up_basis], [down_basis]
    other_in = [core_swap(basis) for basis in own_in]
    other_out = [core_swap(basis) for basis in own_out]

    routing = x_half[:, width:]
    swapped = core_swap(routing)
    routing = jnp.stack(
        [jnp.where(core == 0, routing, swapped), jnp.where(core == 0, swapped, routing)]
    )
    routing = routing.reshape(blocks, tok_rows, lanes)
    ids = routing[:, :, :top].astype(jnp.int32)
    weights = routing[:, :, top : 2 * top].astype(FL)
    own_ids = me_e * local + jnp.arange(local, dtype=jnp.int32)
    hit = ids[None] == own_ids[:, None, None, None]
    named = jnp.any(hit, axis=3)
    weight_of = jnp.sum(jnp.where(hit, weights[None], 0.0), axis=3)
    order = jnp.cumsum(named.astype(jnp.int32), axis=2) - 1
    cell = jnp.arange(blocks, dtype=jnp.int32)[None, :, None] * capacity + order
    cell = jnp.where(named, cell, -1).reshape(local, 1, total)
    weight_of = weight_of.reshape(local, 1, total)
    pick, slot_weight = make_picks(cell, weight_of, slots)

    group_cluster = cluster_of.reshape(n_ex, local)[:, 0]

    def sum_parts(got):
        return sum(piece.astype(FL) for piece in got).astype(BF)

    def spread(mine):
        return lax.all_to_all(mine, ("ez", "core"), split_axis=0, concat_axis=0, tiled=True)

    rows_in, terms = project(
        x_half, chip_rows(own_in, other_in), own_in, other_in, spot, n_dp
    )
    got_in = spread(
        sum_for_groups(
            trade(lambda k: terms[k], "dp"), group_cluster, clusters, 2, [dy_half, pick]
        )
    )
    _, terms_out = project(
        dy_half, chip_rows(own_out, other_out), own_out, other_out, spot, n_dp
    )
    got_out = spread(
        sum_for_groups(trade(lambda k: terms_out[k], "dp"), group_cluster, clusters, 1, [])
    )
    h_pieces = trade(lambda k: got_in, "dp")
    hg, hu, hidden, mixed, act, lift = forward(
        h_pieces, pick, gate_factor, up_factor, down_factor, dp
    )
    d_pieces = trade(lambda k: got_out, "dp")
    (back, grad_gate, grad_up, dots), in_chunks = backward(
        d_pieces, pick, slot_weight, mixed, act, lift, gate_factor, up_factor, down_factor, dp
    )

    numbers = jnp.arange(clusters, dtype=jnp.int32)[:, None]

    def by_cluster(got, groups):
        owner = (groups[None, :] == numbers)[:, :, None, None]
        summed = jnp.sum(jnp.where(owner, got.astype(FL)[None], 0.0), axis=1)
        return summed.astype(BF).reshape(-1, half)

    in_got = trade(lambda k: in_chunks[k], "dp")
    mixed_chunks = mixed_sums(mixed, pick, weight_of, dp, got_out.shape, n_dp, in_got[1])
    mixed_mine = sum_parts(trade(lambda k: mixed_chunks[k], "dp"))
    in_mine = sum_parts(in_got)
    grad_gate_factor, grad_up_factor, grad_down_factor = factor_grads(
        hg, grad_gate, hu, grad_up, hidden, back, total, in_mine
    )
    mine = jnp.concatenate([in_mine, mixed_mine], axis=1)
    got = spread(mine)
    in_sum = after(by_cluster(got[:, : 2 * rank_part], group_cluster), grad_gate_factor)
    mixed_sum = by_cluster(got[:, 2 * rank_part :], group_cluster)
    in_parts = trade(lambda k: in_sum, "dp")

    placed = cell == jnp.arange(slots, dtype=jnp.int32)[None, :, None]
    scores = jnp.sum(jnp.where(placed, dots, 0.0), axis=1).reshape(local, 2, half)
    mine = jnp.where(core == 0, scores[:, 0], scores[:, 1])
    theirs = core_swap(jnp.where(core == 0, scores[:, 1], scores[:, 0]))
    first = jnp.where(core == 0, mine, theirs)
    second = jnp.where(core == 0, theirs, mine)
    scores = jnp.concatenate([first, second], axis=0).T.astype(BF)
    scores = jnp.pad(scores, ((0, 0), (0, lanes - 2 * local)))

    grad_x = sum(mm("rt,rf->tf", part, rows) for part, rows in zip(in_parts, rows_in))
    leaving = jnp.concatenate([grad_x.astype(BF), scores], axis=1)
    rows = leaving.reshape(n_dp * n_z, tok_rows, width + lanes)
    rows = lax.all_to_all(rows, ("dp", "ez"), split_axis=0, concat_axis=0, tiled=True)
    rows = rows.reshape(n_dp, n_z, tok_rows, width + lanes)
    x_other = core_swap(x_half)
    dy_other = core_swap(dy_half)
    same = core == dp // parts_core

    def own_ranks(parts):
        near, far = parts[:parts_core], parts[parts_core:]
        keep = [jnp.where(same, a, b) for a, b in zip(near, far)]
        other = [core_swap(jnp.where(same, b, a)) for a, b in zip(near, far)]
        return keep, other

    shape = (clusters, rank_own, width)
    grad_gate_basis, grad_up_basis = basis_grads(
        *own_ranks(in_parts), x_half, x_other, spot, shape, n_dp, leaving
    )
    mixed_sum = after(mixed_sum, grad_gate_basis)
    mixed_parts = trade(lambda k: mixed_sum, "dp")
    (grad_down_basis,) = basis_grads(
        *own_ranks(mixed_parts), dy_half, dy_other, spot, shape, n_dp, leaving
    )

    grad_rows = jnp.sum(rows[..., :width].astype(FL), axis=1)
    grad_rows = after(grad_rows, grad_down_basis)
    grad_tokens = grad_rows.astype(BF).transpose(1, 0, 2).reshape(tok_rows, model_width)
    by_expert = jnp.sum(rows[..., width : width + 2 * local].astype(FL), axis=0)
    by_expert = by_expert.transpose(1, 0, 2).reshape(tok_rows, 1, experts)
    chosen = route_ids[:, :, None] == jnp.arange(experts, dtype=jnp.int32)[None, None, :]
    grad_route = jnp.sum(jnp.where(chosen, by_expert, 0.0), axis=2)
    return (
        grad_tokens,
        grad_route,
        grad_gate_basis,
        grad_up_basis,
        grad_down_basis,
        grad_gate_factor,
        grad_up_factor,
        grad_down_factor,
    )


def solution(mesh):
    n_dp, n_ex = mesh.shape["dp"], mesh.shape["expert"]
    split = Mesh(mesh.devices.reshape(n_dp, n_ex // 2, 2), ("dp", "ez", "core"))
    ex = ("ez", "core")
    rows = P(("dp", "ez", "core"), None)
    basis = P(None, ex, "dp")
    in_specs = (
        rows,
        rows,
        rows,
        rows,
        P(),
        basis,
        basis,
        basis,
        P(ex, None, "dp"),
        P(ex, None, "dp"),
        P(ex, "dp", None),
    )
    out_specs = (
        rows,
        rows,
        basis,
        basis,
        basis,
        P(ex, None, "dp"),
        P(ex, None, "dp"),
        P(ex, "dp", None),
    )
    return jax.shard_map(body, mesh=split, in_specs=in_specs, out_specs=out_specs, check_vma=False)
```

```python
import functools

import jax
import jax.numpy as jnp
from jax import lax
from jax.experimental import pallas as pl
from jax.experimental.pallas import tpu as pltpu
from jax.sharding import Mesh
from jax.sharding import PartitionSpec as P

FL = jnp.float32
BF = jnp.bfloat16
VMEM = pltpu.VMEM


def mm(spec, a, b):
    return jnp.einsum(spec, a, b, preferred_element_type=FL)


def dot(a, b, a_dim, b_dim):
    return lax.dot_general(a, b, (((a_dim,), (b_dim,)), ((), ())), preferred_element_type=FL)


def after(value, first):
    mark = lax.slice(first, (0,) * first.ndim, (1,) * first.ndim).reshape(()).astype(FL) * 0.0
    return value + mark.astype(value.dtype)


def core_swap(value):
    return lax.ppermute(value, "core", [(0, 1), (1, 0)])


def in_order(pieces, me):
    bit = 1
    while bit < len(pieces):
        odd = (me & bit) != 0
        pieces = [
            jnp.where(odd, pieces[j ^ bit], pieces[j]) for j in range(len(pieces))
        ]
        bit *= 2
    return pieces


def trade(chunk_for, axis):
    n = lax.axis_size(axis)
    sent = [lax.ppermute(chunk_for(k), axis, [(i, i ^ k) for i in range(n)]) for k in range(1, n)]
    return [chunk_for(0)] + sent


def whole(array):
    return pl.BlockSpec(array.shape, lambda *_: (0,) * array.ndim, memory_space=VMEM)


def each(array):
    shape = (1,) + array.shape[1:]
    return pl.BlockSpec(shape, lambda j: (j,) + (0,) * (array.ndim - 1), memory_space=VMEM)


SCALAR = pl.BlockSpec(memory_space=pltpu.SMEM)
ANYWHERE = pl.BlockSpec(memory_space=pl.ANY)


FREE = pl.CostEstimate(flops=0, bytes_accessed=0, transcendentals=0)


def params(total, big=False):
    return pltpu.CompilerParams(vmem_limit_bytes=(56 if big else 8 + total * 15 // 1024) << 20)


def shaped(shape, kind):
    return jax.ShapeDtypeStruct(shape, kind)


def place_rows(own, other, target, part, from_own, low):
    count = len(own)

    def fill(source):
        for c in range(own[0].shape[0]):
            for b in range(count):
                to = (c * count + b) * part
                target[to : to + part, :] = source[b][c, pl.ds(low, part), :]

    pl.when(from_own)(functools.partial(fill, own))
    pl.when(jnp.logical_not(from_own))(functools.partial(fill, other))


def project(cols, rows, own, other, spot, n_dp):
    half = cols.shape[0]
    count = len(own)
    clusters, rank_own, width = own[0].shape
    parts_core = n_dp // 2
    part = rank_own // parts_core
    row_count = clusters * count * part
    built = rows is None
    ins = [cols] + (list(own) + list(other) if built else list(rows))

    def kernel(spot_ref, cols_ref, *refs):
        sources, outs = refs[: len(ins) - 1], refs[len(ins) - 1 :]
        dp, core = spot_ref[0], spot_ref[1]
        parts, products = sources, outs[-n_dp:]
        if built:
            parts = outs[:n_dp]
            for k in range(n_dp):
                low = pl.multiple_of(lax.rem(dp ^ k, parts_core) * part, part)
                from_own = core == (dp ^ k) // parts_core
                place_rows(sources[:count], sources[count:], parts[k], part, from_own, low)
        for base, product in zip(parts, products):
            product[...] = dot(base[...], cols_ref[:, :width], 1, 1).astype(BF)

    outs = [shaped((row_count, width), BF)] * n_dp if built else []
    outs += [shaped((row_count, half), BF)] * n_dp
    got = pl.pallas_call(
        kernel,
        out_shape=outs,
        in_specs=[SCALAR] + [whole(x) for x in ins],
        out_specs=[whole(out) for out in outs],
        compiler_params=params(2 * half, True),
        cost_estimate=FREE,
        name="project",
    )(spot, *ins)
    return (got[:n_dp] if built else rows), got[-n_dp:]


def sum_for_groups(pieces, groups, clusters, count, firsts):
    rows, half = pieces[0].shape
    part = rows // (clusters * count)
    n_ex = groups.shape[0]

    def kernel(groups_ref, *refs):
        got, out_ref, sum_ref = refs[: len(pieces)], refs[-2], refs[-1]
        for b in range(count):
            for c in range(clusters):
                take = slice((c * count + b) * part, (c * count + b + 1) * part)
                total = got[0][take, :].astype(FL)
                for piece in got[1:]:
                    total += piece[take, :].astype(FL)
                sum_ref[c, b] = total.astype(BF)
        for e in range(n_ex):
            for b in range(count):
                out_ref[e, b * part : (b + 1) * part, :] = sum_ref[groups_ref[e], b]

    out = shaped((n_ex, count * part, half), BF)
    return pl.pallas_call(
        kernel,
        out_shape=out,
        in_specs=[SCALAR] + [whole(x) for x in pieces] + [ANYWHERE] * len(firsts),
        out_specs=whole(out),
        scratch_shapes=[pltpu.VMEM((clusters, count, part, half), BF)],
        compiler_params=params(2 * half),
        cost_estimate=FREE,
        name="sum_for_groups",
    )(groups, *pieces, *firsts)


def basis_grads(keep, other, cols, other_cols, spot, shape, n_dp, first):
    clusters, rank_own, width = shape
    parts_core = n_dp // 2
    part = rank_own // parts_core
    half = cols.shape[0]
    count = keep[0].shape[0] // (clusters * part)
    block = width // 2 if width % 256 == 0 else width

    def kernel(spot_ref, *refs):
        ours, theirs = refs[:parts_core], refs[parts_core : 2 * parts_core]
        cols_ref, other_ref = refs[2 * parts_core : 2 * parts_core + 2]
        outs, rows_ref = refs[-1 - count : -1], refs[-1]
        dp = spot_ref[0]

        @pl.when(pl.program_id(0) == 0)
        def _():
            for k in range(parts_core):
                low = (lax.rem(dp, parts_core) ^ k) * part
                for c in range(clusters):
                    at = pl.multiple_of(c * rank_own + low, part)
                    for b in range(count):
                        take = slice((c * count + b) * part, (c * count + b + 1) * part)
                        kind = rows_ref.dtype
                        rows_ref[0, b, pl.ds(at, part), :] = ours[k][take, :].astype(kind)
                        rows_ref[1, b, pl.ds(at, part), :] = theirs[k][take, :].astype(kind)

        for b in range(count):
            total = dot(rows_ref[0, b].astype(BF), cols_ref[...], 1, 0)
            total += dot(rows_ref[1, b].astype(BF), other_ref[...], 1, 0)
            outs[b][...] = total

    ins = list(keep) + list(other)
    out = shaped((clusters * rank_own, width), FL)
    got = pl.pallas_call(
        kernel,
        grid=(width // block,),
        out_shape=[out] * count,
        in_specs=[SCALAR]
        + [whole(x) for x in ins]
        + [pl.BlockSpec((half, block), lambda j: (0, j), memory_space=VMEM)] * 2
        + [ANYWHERE],
        out_specs=[
            pl.BlockSpec((clusters * rank_own, block), lambda j: (0, j), memory_space=VMEM)
        ]
        * count,
        scratch_shapes=[pltpu.VMEM((2, count, clusters * rank_own, half), rows_kind(part))],
        compiler_params=params(2 * half),
        cost_estimate=FREE,
        name="basis_grads",
    )(spot, *ins, cols, other_cols, first)
    return [grad.reshape(shape) for grad in got]


def make_picks(cell, weight, slots):
    local, _, total = cell.shape

    def kernel(cell_ref, weight_ref, pick_ref, slot_ref):
        hit = cell_ref[0] == lax.broadcasted_iota(jnp.int32, (slots, total), 0)
        pick_ref[0] = jnp.where(hit, 1.0, 0.0).astype(BF)
        slot_ref[0] = jnp.sum(jnp.where(hit, weight_ref[0], 0.0), axis=1, keepdims=True)

    outs = [shaped((local, slots, total), BF), shaped((local, slots, 1), FL)]
    return pl.pallas_call(
        kernel,
        grid=(local,),
        out_shape=outs,
        in_specs=[each(cell), each(weight)],
        out_specs=[each(out) for out in outs],
        compiler_params=params(total),
        cost_estimate=FREE,
        name="make_picks",
    )(cell, weight)


def lay_out(pieces, target, me, count):
    n_dp = len(pieces)
    n_ex, rows, half = pieces[0].shape
    part = rows // count
    for k in range(n_dp):
        for e in range(n_ex):
            at = pl.multiple_of(((e // 2) * n_dp + (me ^ k)) * part, part)
            for b in range(count):
                piece = pieces[k][e, b * part : (b + 1) * part, :]
                target[b, pl.ds(at, part), (e % 2) * half : (e % 2 + 1) * half] = piece.astype(
                    target.dtype
                )


def rows_kind(part):
    return BF if part % 16 == 0 else FL


def hand_out(source, pieces, me, count):
    n_dp = len(pieces)
    n_ex, rows, half = pieces[0].shape
    part = rows // count
    for k in range(n_dp):
        for e in range(n_ex):
            at = pl.multiple_of(((e // 2) * n_dp + (me ^ k)) * part, part)
            for b in range(count):
                pieces[k][e, b * part : (b + 1) * part, :] = source[
                    b, pl.ds(at, part), (e % 2) * half : (e % 2 + 1) * half
                ].astype(BF)


def forward(pieces, pick, weight, gate_factor, up_factor, down_factor, dp):
    n_dp = len(pieces)
    n_ex, rows, half = pieces[0].shape
    local, slots, total = pick.shape
    rank, hid = gate_factor.shape[1:]

    def kernel(dp_ref, *refs):
        got, refs = refs[:n_dp], refs[n_dp:]
        pick_ref, weight_ref, gate_ref, up_ref, down_ref = refs[:5]
        hg_ref, hu_ref, hidden_ref, mixed_ref, act_ref, lift_ref = refs[5:11]
        sent = refs[11 : 11 + n_dp]
        rows_ref, total_ref = refs[11 + n_dp :]
        j = pl.program_id(0)
        me = dp_ref[0]

        @pl.when(j == 0)
        def _():
            lay_out(got, rows_ref, me, 2)
            total_ref[...] = jnp.zeros_like(total_ref)

        take = pick_ref[0]
        hg = dot(take, rows_ref[0].astype(BF), 1, 1).astype(BF)
        hu = dot(take, rows_ref[1].astype(BF), 1, 1).astype(BF)
        hg_ref[0] = hg
        hu_ref[0] = hu
        gate_pre = dot(hg, gate_ref[0], 1, 0)
        up_pre = dot(hu, up_ref[0], 1, 0)
        sig = 1.0 / (1.0 + jnp.exp(-gate_pre))
        act = gate_pre * sig
        act_ref[0] = act
        lift_ref[0] = up_pre * (sig * (1.0 + gate_pre * (1.0 - sig)))
        hidden = (act * up_pre).astype(BF)
        hidden_ref[0] = hidden
        mixed = dot(hidden, down_ref[0], 1, 0).astype(BF)
        mixed_ref[0] = mixed
        total_ref[0] += dot(mixed, (take * weight_ref[0]).astype(BF), 0, 0)

        @pl.when(j == local - 1)
        def _():
            hand_out(total_ref, sent, me, 1)

    slot_shape = (local, slots, rank)
    hid_shape = (local, slots, hid)
    outs = [
        shaped(slot_shape, BF),
        shaped(slot_shape, BF),
        shaped(hid_shape, BF),
        shaped(slot_shape, BF),
        shaped(hid_shape, FL),
        shaped(hid_shape, FL),
    ]
    chunks = [shaped((n_ex, rows // 2, half), BF)] * n_dp
    got = pl.pallas_call(
        kernel,
        grid=(local,),
        out_shape=outs + chunks,
        in_specs=[SCALAR]
        + [whole(piece) for piece in pieces]
        + [each(x) for x in (pick, weight, gate_factor, up_factor, down_factor)],
        out_specs=[each(out) for out in outs] + [whole(chunk) for chunk in chunks],
        scratch_shapes=[pltpu.VMEM((2, rank, total), rows_kind(rows // 2)), pltpu.VMEM((1, rank, total), FL)],
        compiler_params=params(total, True),
        cost_estimate=FREE,
        name="forward",
    )(dp.reshape(1), *pieces, pick, weight, gate_factor, up_factor, down_factor)
    return got[:6], got[6:]


def backward(pieces, pick, weight, mixed, act, lift, gate_factor, up_factor, down_factor, dp):
    n_dp = len(pieces)
    n_ex, rows, half = pieces[0].shape
    local, slots, total = pick.shape
    rank, hid = gate_factor.shape[1:]

    def kernel(dp_ref, *refs):
        got, refs = refs[:n_dp], refs[n_dp:]
        pick_ref, weight_ref, mixed_ref, act_ref, lift_ref = refs[:5]
        gate_ref, up_ref, down_ref = refs[5:8]
        back_ref, gate_out, up_out, dots_ref = refs[8:12]
        sent = refs[12 : 12 + n_dp]
        rows_ref, total_ref = refs[12 + n_dp :]
        j = pl.program_id(0)
        me = dp_ref[0]

        @pl.when(j == 0)
        def _():
            lay_out(got, rows_ref, me, 1)
            total_ref[...] = jnp.zeros_like(total_ref)

        take = pick_ref[0]
        hd = dot(take, rows_ref[0].astype(BF), 1, 1)
        dots_ref[0] = jnp.sum(mixed_ref[0].astype(FL) * hd, axis=1, keepdims=True)
        back = (weight_ref[0] * hd).astype(BF)
        back_ref[0] = back
        grad_hidden = dot(back, down_ref[0], 1, 1)
        grad_gate = (grad_hidden * lift_ref[0]).astype(BF)
        grad_up = (grad_hidden * act_ref[0]).astype(BF)
        gate_out[0] = grad_gate
        up_out[0] = grad_up
        total_ref[0] += dot(dot(grad_gate, gate_ref[0], 1, 1).astype(BF), take, 0, 0)
        total_ref[1] += dot(dot(grad_up, up_ref[0], 1, 1).astype(BF), take, 0, 0)

        @pl.when(j == local - 1)
        def _():
            hand_out(total_ref, sent, me, 2)

    outs = [
        shaped((local, slots, rank), BF),
        shaped((local, slots, hid), BF),
        shaped((local, slots, hid), BF),
        shaped((local, slots, 1), FL),
    ]
    chunks = [shaped((n_ex, 2 * rows, half), BF)] * n_dp
    ins = (pick, weight, mixed, act, lift, gate_factor, up_factor, down_factor)
    got = pl.pallas_call(
        kernel,
        grid=(local,),
        out_shape=outs + chunks,
        in_specs=[SCALAR] + [whole(piece) for piece in pieces] + [each(x) for x in ins],
        out_specs=[each(out) for out in outs] + [whole(chunk) for chunk in chunks],
        scratch_shapes=[pltpu.VMEM((1, rank, total), rows_kind(rows)), pltpu.VMEM((2, rank, total), FL)],
        compiler_params=params(total, True),
        cost_estimate=pl.CostEstimate(
            flops=local * slots * rank * (6 * total + 6 * hid),
            bytes_accessed=32 << 20,
            transcendentals=0,
        ),
        name="backward",
    )(dp.reshape(1), *pieces, *ins)
    return got[:4], got[4:]


def factor_grads(hg, grad_gate, hu, grad_up, hidden, back, total, first):
    local, slots, rank = hg.shape
    hid = hidden.shape[2]

    def kernel(hg_ref, gate_ref, hu_ref, up_ref, hidden_ref, back_ref, _, out_g, out_u, out_d):
        out_g[0] = dot(hg_ref[0], gate_ref[0], 0, 0)
        out_u[0] = dot(hu_ref[0], up_ref[0], 0, 0)
        out_d[0] = dot(hidden_ref[0], back_ref[0], 0, 0)

    outs = [
        shaped((local, rank, hid), FL),
        shaped((local, rank, hid), FL),
        shaped((local, hid, rank), FL),
    ]
    ins = (hg, grad_gate, hu, grad_up, hidden, back)
    return pl.pallas_call(
        kernel,
        grid=(local,),
        out_shape=outs,
        in_specs=[each(x) for x in ins] + [ANYWHERE],
        out_specs=[each(out) for out in outs],
        compiler_params=params(total),
        cost_estimate=FREE,
        name="factor_grads",
    )(*ins, first)


def body(
    tokens,
    grad_out,
    route_ids,
    route_weight,
    cluster_of,
    gate_basis,
    up_basis,
    down_basis,
    gate_factor,
    up_factor,
    down_factor,
):
    n_dp = lax.axis_size("dp")
    n_z = lax.axis_size("ez")
    n_ex = n_z * 2
    dp = lax.axis_index("dp")
    z = lax.axis_index("ez")
    core = lax.axis_index("core")
    me_e = z * 2 + core
    tok_rows, model_width = tokens.shape
    top = route_ids.shape[1]
    local = gate_factor.shape[0]
    experts = local * n_ex
    capacity = max(2, 5 * tok_rows * top // (4 * experts))
    blocks = n_dp * n_ex
    total = blocks * tok_rows
    half = total // 2
    slots = blocks * capacity
    clusters, rank_own, width = gate_basis.shape
    parts_core = n_dp // 2
    rank_part = rank_own // parts_core

    lanes = 128

    def own_columns(rows, more):
        rows = rows.reshape(tok_rows, n_dp, width).transpose(1, 0, 2)
        if more is not None:
            more = jnp.broadcast_to(more[None], (n_dp, tok_rows, lanes))
            rows = jnp.concatenate([rows, more], axis=2)
        rows = jnp.broadcast_to(rows[:, None], (n_dp, n_z) + rows.shape[1:])
        rows = rows.reshape(n_dp * n_z, tok_rows, -1)
        got = lax.all_to_all(rows, ("dp", "ez"), split_axis=0, concat_axis=0, tiled=True)
        return got.reshape(half, -1)

    routing = jnp.concatenate([route_ids.astype(BF), route_weight], axis=1)
    routing = jnp.pad(routing, ((0, 0), (0, lanes - 2 * top)))
    x_half = own_columns(tokens, routing)
    dy_half = own_columns(after(grad_out, x_half), None)
    spot = jnp.stack([dp, core]).astype(jnp.int32)

    def chip_rows(own, other):
        if rank_part % 16 == 0:
            return None
        count = len(own)
        shape = (clusters, count, parts_core, rank_part, width)
        own = jnp.stack(own, axis=1).reshape(shape)
        other = jnp.stack(other, axis=1).reshape(shape)
        result = []
        for k in range(n_dp):
            part = dp ^ k
            at = part % parts_core
            mine = lax.dynamic_index_in_dim(own, at, 2, False)
            theirs = lax.dynamic_index_in_dim(other, at, 2, False)
            rows = jnp.where(part // parts_core == core, mine, theirs)
            result.append(rows.reshape(clusters * count * rank_part, width))
        return result

    own_in, own_out = [gate_basis, up_basis], [down_basis]
    other_in = [core_swap(basis) for basis in own_in]
    other_out = [core_swap(basis) for basis in own_out]

    routing = x_half[:, width:]
    swapped = core_swap(routing)
    routing = jnp.stack(
        [jnp.where(core == 0, routing, swapped), jnp.where(core == 0, swapped, routing)]
    )
    routing = routing.reshape(blocks, tok_rows, lanes)
    ids = routing[:, :, :top].astype(jnp.int32)
    weights = routing[:, :, top : 2 * top].astype(FL)
    own_ids = me_e * local + jnp.arange(local, dtype=jnp.int32)
    hit = ids[None] == own_ids[:, None, None, None]
    named = jnp.any(hit, axis=3)
    weight_of = jnp.sum(jnp.where(hit, weights[None], 0.0), axis=3)
    order = jnp.cumsum(named.astype(jnp.int32), axis=2) - 1
    cell = jnp.arange(blocks, dtype=jnp.int32)[None, :, None] * capacity + order
    cell = jnp.where(named, cell, -1).reshape(local, 1, total)
    weight_of = weight_of.reshape(local, 1, total)
    pick, slot_weight = make_picks(cell, weight_of, slots)

    group_cluster = cluster_of.reshape(n_ex, local)[:, 0]

    def sum_parts(got):
        return sum(piece.astype(FL) for piece in got).astype(BF)

    def spread(mine):
        return lax.all_to_all(mine, ("ez", "core"), split_axis=0, concat_axis=0, tiled=True)

    rows_in, terms = project(
        x_half, chip_rows(own_in, other_in), own_in, other_in, spot, n_dp
    )
    got_in = spread(
        sum_for_groups(
            trade(lambda k: terms[k], "dp"), group_cluster, clusters, 2, [dy_half, pick]
        )
    )
    _, terms_out = project(
        dy_half, chip_rows(own_out, other_out), own_out, other_out, spot, n_dp
    )
    h_pieces = trade(lambda k: got_in, "dp")
    got_out = spread(
        sum_for_groups(
            trade(lambda k: terms_out[k], "dp"), group_cluster, clusters, 1, h_pieces[1:]
        )
    )
    (hg, hu, hidden, mixed, act, lift), mixed_chunks = forward(
        h_pieces, pick, weight_of, gate_factor, up_factor, down_factor, dp
    )
    d_pieces = trade(lambda k: got_out, "dp")
    (back, grad_gate, grad_up, dots), in_chunks = backward(
        d_pieces, pick, slot_weight, mixed, act, lift, gate_factor, up_factor, down_factor, dp
    )

    numbers = jnp.arange(clusters, dtype=jnp.int32)[:, None]

    def by_cluster(got, groups):
        owner = (groups[None, :] == numbers)[:, :, None, None]
        summed = jnp.sum(jnp.where(owner, got.astype(FL)[None], 0.0), axis=1)
        return summed.astype(BF).reshape(-1, half)

    mixed_mine = sum_parts(trade(lambda k: mixed_chunks[k], "dp"))
    in_mine = sum_parts(trade(lambda k: in_chunks[k], "dp"))
    grad_gate_factor, grad_up_factor, grad_down_factor = factor_grads(
        hg, grad_gate, hu, grad_up, hidden, back, total, in_mine
    )
    mine = jnp.concatenate([in_mine, mixed_mine], axis=1)
    got = spread(mine)
    in_sum = after(by_cluster(got[:, : 2 * rank_part], group_cluster), grad_gate_factor)
    mixed_sum = by_cluster(got[:, 2 * rank_part :], group_cluster)
    in_parts = trade(lambda k: in_sum, "dp")

    placed = cell == jnp.arange(slots, dtype=jnp.int32)[None, :, None]
    scores = jnp.sum(jnp.where(placed, dots, 0.0), axis=1).reshape(local, 2, half)
    mine = jnp.where(core == 0, scores[:, 0], scores[:, 1])
    theirs = core_swap(jnp.where(core == 0, scores[:, 1], scores[:, 0]))
    first = jnp.where(core == 0, mine, theirs)
    second = jnp.where(core == 0, theirs, mine)
    scores = jnp.concatenate([first, second], axis=0).T.astype(BF)
    scores = jnp.pad(scores, ((0, 0), (0, lanes - 2 * local)))

    grad_x = sum(mm("rt,rf->tf", part, rows) for part, rows in zip(in_parts, rows_in))
    leaving = jnp.concatenate([grad_x.astype(BF), scores], axis=1)
    rows = leaving.reshape(n_dp * n_z, tok_rows, width + lanes)
    rows = lax.all_to_all(rows, ("dp", "ez"), split_axis=0, concat_axis=0, tiled=True)
    rows = rows.reshape(n_dp, n_z, tok_rows, width + lanes)
    x_other = core_swap(x_half)
    dy_other = core_swap(dy_half)
    same = core == dp // parts_core

    def own_ranks(parts):
        near, far = parts[:parts_core], parts[parts_core:]
        keep = [jnp.where(same, a, b) for a, b in zip(near, far)]
        other = [core_swap(jnp.where(same, b, a)) for a, b in zip(near, far)]
        return keep, other

    shape = (clusters, rank_own, width)
    grad_gate_basis, grad_up_basis = basis_grads(
        *own_ranks(in_parts), x_half, x_other, spot, shape, n_dp, leaving
    )
    mixed_sum = after(mixed_sum, grad_gate_basis)
    mixed_parts = trade(lambda k: mixed_sum, "dp")
    (grad_down_basis,) = basis_grads(
        *own_ranks(mixed_parts), dy_half, dy_other, spot, shape, n_dp, leaving
    )

    grad_rows = jnp.sum(rows[..., :width].astype(FL), axis=1)
    grad_rows = after(grad_rows, grad_down_basis)
    grad_tokens = grad_rows.astype(BF).transpose(1, 0, 2).reshape(tok_rows, model_width)
    by_expert = jnp.sum(rows[..., width : width + 2 * local].astype(FL), axis=0)
    by_expert = by_expert.transpose(1, 0, 2).reshape(tok_rows, 1, experts)
    chosen = route_ids[:, :, None] == jnp.arange(experts, dtype=jnp.int32)[None, None, :]
    grad_route = jnp.sum(jnp.where(chosen, by_expert, 0.0), axis=2)
    return (
        grad_tokens,
        grad_route,
        grad_gate_basis,
        grad_up_basis,
        grad_down_basis,
        grad_gate_factor,
        grad_up_factor,
        grad_down_factor,
    )


def solution(mesh):
    n_dp, n_ex = mesh.shape["dp"], mesh.shape["expert"]
    split = Mesh(mesh.devices.reshape(n_dp, n_ex // 2, 2), ("dp", "ez", "core"))
    ex = ("ez", "core")
    rows = P(("dp", "ez", "core"), None)
    basis = P(None, ex, "dp")
    in_specs = (
        rows,
        rows,
        rows,
        rows,
        P(),
        basis,
        basis,
        basis,
        P(ex, None, "dp"),
        P(ex, None, "dp"),
        P(ex, "dp", None),
    )
    out_specs = (
        rows,
        rows,
        basis,
        basis,
        basis,
        P(ex, None, "dp"),
        P(ex, None, "dp"),
        P(ex, "dp", None),
    )
    return jax.shard_map(body, mesh=split, in_specs=in_specs, out_specs=out_specs, check_vma=False)
```

```python
import functools

import jax
import jax.numpy as jnp
from jax import lax
from jax.experimental import pallas as pl
from jax.experimental.pallas import tpu as pltpu
from jax.sharding import Mesh
from jax.sharding import PartitionSpec as P

FL = jnp.float32
BF = jnp.bfloat16
VMEM = pltpu.VMEM


def mm(spec, a, b):
    return jnp.einsum(spec, a, b, preferred_element_type=FL)


def dot(a, b, a_dim, b_dim):
    return lax.dot_general(a, b, (((a_dim,), (b_dim,)), ((), ())), preferred_element_type=FL)


def after(value, first):
    mark = lax.slice(first, (0,) * first.ndim, (1,) * first.ndim).reshape(()).astype(FL) * 0.0
    return value + mark.astype(value.dtype)


def core_swap(value):
    return lax.ppermute(value, "core", [(0, 1), (1, 0)])


def in_order(pieces, me):
    bit = 1
    while bit < len(pieces):
        odd = (me & bit) != 0
        pieces = [
            jnp.where(odd, pieces[j ^ bit], pieces[j]) for j in range(len(pieces))
        ]
        bit *= 2
    return pieces


def trade(chunk_for, axis):
    n = lax.axis_size(axis)
    sent = [lax.ppermute(chunk_for(k), axis, [(i, i ^ k) for i in range(n)]) for k in range(1, n)]
    return [chunk_for(0)] + sent


def whole(array):
    return pl.BlockSpec(array.shape, lambda *_: (0,) * array.ndim, memory_space=VMEM)


def each(array):
    shape = (1,) + array.shape[1:]
    return pl.BlockSpec(shape, lambda j: (j,) + (0,) * (array.ndim - 1), memory_space=VMEM)


SCALAR = pl.BlockSpec(memory_space=pltpu.SMEM)
ANYWHERE = pl.BlockSpec(memory_space=pl.ANY)


FREE = pl.CostEstimate(flops=0, bytes_accessed=0, transcendentals=0)


def params(total, big=False):
    return pltpu.CompilerParams(vmem_limit_bytes=(56 if big else 8 + total * 15 // 1024) << 20)


def shaped(shape, kind):
    return jax.ShapeDtypeStruct(shape, kind)


def place_rows(own, other, target, part, from_own, low):
    count = len(own)

    def fill(source):
        for c in range(own[0].shape[0]):
            for b in range(count):
                to = (c * count + b) * part
                target[to : to + part, :] = source[b][c, pl.ds(low, part), :]

    pl.when(from_own)(functools.partial(fill, own))
    pl.when(jnp.logical_not(from_own))(functools.partial(fill, other))


def project(cols, rows, own, other, spot, n_dp):
    half = cols.shape[0]
    count = len(own)
    clusters, rank_own, width = own[0].shape
    parts_core = n_dp // 2
    part = rank_own // parts_core
    row_count = clusters * count * part
    built = rows is None
    ins = [cols] + (list(own) + list(other) if built else list(rows))

    def kernel(spot_ref, cols_ref, *refs):
        sources, outs = refs[: len(ins) - 1], refs[len(ins) - 1 :]
        dp, core = spot_ref[0], spot_ref[1]
        parts, products = sources, outs[-n_dp:]
        if built:
            parts = outs[:n_dp]
            for k in range(n_dp):
                low = pl.multiple_of(lax.rem(dp ^ k, parts_core) * part, part)
                from_own = core == (dp ^ k) // parts_core
                place_rows(sources[:count], sources[count:], parts[k], part, from_own, low)
        for base, product in zip(parts, products):
            product[...] = dot(base[...], cols_ref[:, :width], 1, 1).astype(BF)

    outs = [shaped((row_count, width), BF)] * n_dp if built else []
    outs += [shaped((row_count, half), BF)] * n_dp
    got = pl.pallas_call(
        kernel,
        out_shape=outs,
        in_specs=[SCALAR] + [whole(x) for x in ins],
        out_specs=[whole(out) for out in outs],
        compiler_params=params(2 * half, True),
        cost_estimate=FREE,
        name="project",
    )(spot, *ins)
    return (got[:n_dp] if built else rows), got[-n_dp:]


def sum_for_groups(pieces, groups, clusters, count, firsts):
    rows, half = pieces[0].shape
    part = rows // (clusters * count)
    n_ex = groups.shape[0]

    def kernel(groups_ref, *refs):
        got, out_ref, sum_ref = refs[: len(pieces)], refs[-2], refs[-1]
        for b in range(count):
            for c in range(clusters):
                take = slice((c * count + b) * part, (c * count + b + 1) * part)
                total = got[0][take, :].astype(FL)
                for piece in got[1:]:
                    total += piece[take, :].astype(FL)
                sum_ref[c, b] = total.astype(BF)
        for e in range(n_ex):
            for b in range(count):
                out_ref[e, b * part : (b + 1) * part, :] = sum_ref[groups_ref[e], b]

    out = shaped((n_ex, count * part, half), BF)
    return pl.pallas_call(
        kernel,
        out_shape=out,
        in_specs=[SCALAR] + [whole(x) for x in pieces] + [ANYWHERE] * len(firsts),
        out_specs=whole(out),
        scratch_shapes=[pltpu.VMEM((clusters, count, part, half), BF)],
        compiler_params=params(2 * half),
        cost_estimate=FREE,
        name="sum_for_groups",
    )(groups, *pieces, *firsts)


def hold(value, firsts):
    def kernel(value_ref, *refs):
        refs[-1][...] = value_ref[...]

    return pl.pallas_call(
        kernel,
        out_shape=shaped(value.shape, value.dtype),
        in_specs=[whole(value)] + [ANYWHERE] * len(firsts),
        out_specs=whole(value),
        compiler_params=params(2 * value.shape[-1]),
        cost_estimate=FREE,
        name="hold",
    )(value, *firsts)


def basis_grads(keep, other, cols, other_cols, spot, shape, n_dp, first):
    clusters, rank_own, width = shape
    parts_core = n_dp // 2
    part = rank_own // parts_core
    half = cols.shape[0]
    count = keep[0].shape[0] // (clusters * part)
    block = width // 2 if width % 256 == 0 else width

    def kernel(spot_ref, *refs):
        ours, theirs = refs[:parts_core], refs[parts_core : 2 * parts_core]
        cols_ref, other_ref = refs[2 * parts_core : 2 * parts_core + 2]
        outs, rows_ref = refs[-1 - count : -1], refs[-1]
        dp = spot_ref[0]

        @pl.when(pl.program_id(0) == 0)
        def _():
            for k in range(parts_core):
                low = (lax.rem(dp, parts_core) ^ k) * part
                for c in range(clusters):
                    at = pl.multiple_of(c * rank_own + low, part)
                    for b in range(count):
                        take = slice((c * count + b) * part, (c * count + b + 1) * part)
                        kind = rows_ref.dtype
                        rows_ref[0, b, pl.ds(at, part), :] = ours[k][take, :].astype(kind)
                        rows_ref[1, b, pl.ds(at, part), :] = theirs[k][take, :].astype(kind)

        for b in range(count):
            total = dot(rows_ref[0, b].astype(BF), cols_ref[...], 1, 0)
            total += dot(rows_ref[1, b].astype(BF), other_ref[...], 1, 0)
            outs[b][...] = total

    ins = list(keep) + list(other)
    out = shaped((clusters * rank_own, width), FL)
    got = pl.pallas_call(
        kernel,
        grid=(width // block,),
        out_shape=[out] * count,
        in_specs=[SCALAR]
        + [whole(x) for x in ins]
        + [pl.BlockSpec((half, block), lambda j: (0, j), memory_space=VMEM)] * 2
        + [ANYWHERE],
        out_specs=[
            pl.BlockSpec((clusters * rank_own, block), lambda j: (0, j), memory_space=VMEM)
        ]
        * count,
        scratch_shapes=[pltpu.VMEM((2, count, clusters * rank_own, half), rows_kind(part))],
        compiler_params=params(2 * half),
        cost_estimate=FREE,
        name="basis_grads",
    )(spot, *ins, cols, other_cols, first)
    return [grad.reshape(shape) for grad in got]


def make_picks(cell, weight, slots):
    local, _, total = cell.shape

    def kernel(cell_ref, weight_ref, pick_ref, slot_ref):
        hit = cell_ref[0] == lax.broadcasted_iota(jnp.int32, (slots, total), 0)
        pick_ref[0] = jnp.where(hit, 1.0, 0.0).astype(BF)
        slot_ref[0] = jnp.sum(jnp.where(hit, weight_ref[0], 0.0), axis=1, keepdims=True)

    outs = [shaped((local, slots, total), BF), shaped((local, slots, 1), FL)]
    return pl.pallas_call(
        kernel,
        grid=(local,),
        out_shape=outs,
        in_specs=[each(cell), each(weight)],
        out_specs=[each(out) for out in outs],
        compiler_params=params(total),
        cost_estimate=FREE,
        name="make_picks",
    )(cell, weight)


def lay_out(pieces, target, me, count):
    n_dp = len(pieces)
    n_ex, rows, half = pieces[0].shape
    part = rows // count
    for k in range(n_dp):
        for e in range(n_ex):
            at = pl.multiple_of(((e // 2) * n_dp + (me ^ k)) * part, part)
            for b in range(count):
                piece = pieces[k][e, b * part : (b + 1) * part, :]
                target[b, pl.ds(at, part), (e % 2) * half : (e % 2 + 1) * half] = piece.astype(
                    target.dtype
                )


def rows_kind(part):
    return BF if part % 16 == 0 else FL


def hand_out(source, pieces, me, count):
    n_dp = len(pieces)
    n_ex, rows, half = pieces[0].shape
    part = rows // count
    for k in range(n_dp):
        for e in range(n_ex):
            at = pl.multiple_of(((e // 2) * n_dp + (me ^ k)) * part, part)
            for b in range(count):
                pieces[k][e, b * part : (b + 1) * part, :] = source[
                    b, pl.ds(at, part), (e % 2) * half : (e % 2 + 1) * half
                ].astype(BF)


def forward(pieces, pick, weight, gate_factor, up_factor, down_factor, dp):
    n_dp = len(pieces)
    n_ex, rows, half = pieces[0].shape
    local, slots, total = pick.shape
    rank, hid = gate_factor.shape[1:]

    def kernel(dp_ref, *refs):
        got, refs = refs[:n_dp], refs[n_dp:]
        pick_ref, weight_ref, gate_ref, up_ref, down_ref = refs[:5]
        hg_ref, hu_ref, hidden_ref, mixed_ref, act_ref, lift_ref = refs[5:11]
        sent = refs[11 : 11 + n_dp]
        rows_ref, total_ref = refs[11 + n_dp :]
        j = pl.program_id(0)
        me = dp_ref[0]

        @pl.when(j == 0)
        def _():
            lay_out(got, rows_ref, me, 2)
            total_ref[...] = jnp.zeros_like(total_ref)

        take = pick_ref[0]
        hg = dot(take, rows_ref[0].astype(BF), 1, 1).astype(BF)
        hu = dot(take, rows_ref[1].astype(BF), 1, 1).astype(BF)
        hg_ref[0] = hg
        hu_ref[0] = hu
        gate_pre = dot(hg, gate_ref[0], 1, 0)
        up_pre = dot(hu, up_ref[0], 1, 0)
        sig = 1.0 / (1.0 + jnp.exp(-gate_pre))
        act = gate_pre * sig
        act_ref[0] = act
        lift_ref[0] = up_pre * (sig * (1.0 + gate_pre * (1.0 - sig)))
        hidden = (act * up_pre).astype(BF)
        hidden_ref[0] = hidden
        mixed = dot(hidden, down_ref[0], 1, 0).astype(BF)
        mixed_ref[0] = mixed
        total_ref[0] += dot(mixed, (take * weight_ref[0]).astype(BF), 0, 0)

        @pl.when(j == local - 1)
        def _():
            hand_out(total_ref, sent, me, 1)

    slot_shape = (local, slots, rank)
    hid_shape = (local, slots, hid)
    outs = [
        shaped(slot_shape, BF),
        shaped(slot_shape, BF),
        shaped(hid_shape, BF),
        shaped(slot_shape, BF),
        shaped(hid_shape, FL),
        shaped(hid_shape, FL),
    ]
    chunks = [shaped((n_ex, rows // 2, half), BF)] * n_dp
    got = pl.pallas_call(
        kernel,
        grid=(local,),
        out_shape=outs + chunks,
        in_specs=[SCALAR]
        + [whole(piece) for piece in pieces]
        + [each(x) for x in (pick, weight, gate_factor, up_factor, down_factor)],
        out_specs=[each(out) for out in outs] + [whole(chunk) for chunk in chunks],
        scratch_shapes=[pltpu.VMEM((2, rank, total), rows_kind(rows // 2)), pltpu.VMEM((1, rank, total), FL)],
        compiler_params=params(total, True),
        cost_estimate=FREE,
        name="forward",
    )(dp.reshape(1), *pieces, pick, weight, gate_factor, up_factor, down_factor)
    return got[:6], got[6:]


def backward(pieces, pick, weight, mixed, act, lift, gate_factor, up_factor, down_factor, dp):
    n_dp = len(pieces)
    n_ex, rows, half = pieces[0].shape
    local, slots, total = pick.shape
    rank, hid = gate_factor.shape[1:]

    def kernel(dp_ref, *refs):
        got, refs = refs[:n_dp], refs[n_dp:]
        pick_ref, weight_ref, mixed_ref, act_ref, lift_ref = refs[:5]
        gate_ref, up_ref, down_ref = refs[5:8]
        back_ref, gate_out, up_out, dots_ref = refs[8:12]
        sent = refs[12 : 12 + n_dp]
        rows_ref, total_ref = refs[12 + n_dp :]
        j = pl.program_id(0)
        me = dp_ref[0]

        @pl.when(j == 0)
        def _():
            lay_out(got, rows_ref, me, 1)
            total_ref[...] = jnp.zeros_like(total_ref)

        take = pick_ref[0]
        hd = dot(take, rows_ref[0].astype(BF), 1, 1)
        dots_ref[0] = jnp.sum(mixed_ref[0].astype(FL) * hd, axis=1, keepdims=True)
        back = (weight_ref[0] * hd).astype(BF)
        back_ref[0] = back
        grad_hidden = dot(back, down_ref[0], 1, 1)
        grad_gate = (grad_hidden * lift_ref[0]).astype(BF)
        grad_up = (grad_hidden * act_ref[0]).astype(BF)
        gate_out[0] = grad_gate
        up_out[0] = grad_up
        total_ref[0] += dot(dot(grad_gate, gate_ref[0], 1, 1).astype(BF), take, 0, 0)
        total_ref[1] += dot(dot(grad_up, up_ref[0], 1, 1).astype(BF), take, 0, 0)

        @pl.when(j == local - 1)
        def _():
            hand_out(total_ref, sent, me, 2)

    outs = [
        shaped((local, slots, rank), BF),
        shaped((local, slots, hid), BF),
        shaped((local, slots, hid), BF),
        shaped((local, slots, 1), FL),
    ]
    chunks = [shaped((n_ex, 2 * rows, half), BF)] * n_dp
    ins = (pick, weight, mixed, act, lift, gate_factor, up_factor, down_factor)
    got = pl.pallas_call(
        kernel,
        grid=(local,),
        out_shape=outs + chunks,
        in_specs=[SCALAR] + [whole(piece) for piece in pieces] + [each(x) for x in ins],
        out_specs=[each(out) for out in outs] + [whole(chunk) for chunk in chunks],
        scratch_shapes=[pltpu.VMEM((1, rank, total), rows_kind(rows)), pltpu.VMEM((2, rank, total), FL)],
        compiler_params=params(total, True),
        cost_estimate=pl.CostEstimate(
            flops=local * slots * rank * (6 * total + 6 * hid),
            bytes_accessed=32 << 20,
            transcendentals=0,
        ),
        name="backward",
    )(dp.reshape(1), *pieces, *ins)
    return got[:4], got[4:]


def factor_grads(hg, grad_gate, hu, grad_up, hidden, back, total, first):
    local, slots, rank = hg.shape
    hid = hidden.shape[2]

    def kernel(hg_ref, gate_ref, hu_ref, up_ref, hidden_ref, back_ref, _, out_g, out_u, out_d):
        out_g[0] = dot(hg_ref[0], gate_ref[0], 0, 0)
        out_u[0] = dot(hu_ref[0], up_ref[0], 0, 0)
        out_d[0] = dot(hidden_ref[0], back_ref[0], 0, 0)

    outs = [
        shaped((local, rank, hid), FL),
        shaped((local, rank, hid), FL),
        shaped((local, hid, rank), FL),
    ]
    ins = (hg, grad_gate, hu, grad_up, hidden, back)
    return pl.pallas_call(
        kernel,
        grid=(local,),
        out_shape=outs,
        in_specs=[each(x) for x in ins] + [ANYWHERE],
        out_specs=[each(out) for out in outs],
        compiler_params=params(total),
        cost_estimate=FREE,
        name="factor_grads",
    )(*ins, first)


def body(
    tokens,
    grad_out,
    route_ids,
    route_weight,
    cluster_of,
    gate_basis,
    up_basis,
    down_basis,
    gate_factor,
    up_factor,
    down_factor,
):
    n_dp = lax.axis_size("dp")
    n_z = lax.axis_size("ez")
    n_ex = n_z * 2
    dp = lax.axis_index("dp")
    z = lax.axis_index("ez")
    core = lax.axis_index("core")
    me_e = z * 2 + core
    tok_rows, model_width = tokens.shape
    top = route_ids.shape[1]
    local = gate_factor.shape[0]
    experts = local * n_ex
    capacity = max(2, 5 * tok_rows * top // (4 * experts))
    blocks = n_dp * n_ex
    total = blocks * tok_rows
    half = total // 2
    slots = blocks * capacity
    clusters, rank_own, width = gate_basis.shape
    parts_core = n_dp // 2
    rank_part = rank_own // parts_core

    lanes = 128

    def own_columns(rows, more):
        rows = rows.reshape(tok_rows, n_dp, width).transpose(1, 0, 2)
        if more is not None:
            more = jnp.broadcast_to(more[None], (n_dp, tok_rows, lanes))
            rows = jnp.concatenate([rows, more], axis=2)
        rows = jnp.broadcast_to(rows[:, None], (n_dp, n_z) + rows.shape[1:])
        rows = rows.reshape(n_dp * n_z, tok_rows, -1)
        got = lax.all_to_all(rows, ("dp", "ez"), split_axis=0, concat_axis=0, tiled=True)
        return got.reshape(half, -1)

    routing = jnp.concatenate([route_ids.astype(BF), route_weight], axis=1)
    routing = jnp.pad(routing, ((0, 0), (0, lanes - 2 * top)))
    x_half = own_columns(tokens, routing)
    dy_half = own_columns(after(grad_out, x_half), None)
    spot = jnp.stack([dp, core]).astype(jnp.int32)

    def chip_rows(own, other):
        if rank_part % 16 == 0:
            return None
        count = len(own)
        shape = (clusters, count, parts_core, rank_part, width)
        own = jnp.stack(own, axis=1).reshape(shape)
        other = jnp.stack(other, axis=1).reshape(shape)
        result = []
        for k in range(n_dp):
            part = dp ^ k
            at = part % parts_core
            mine = lax.dynamic_index_in_dim(own, at, 2, False)
            theirs = lax.dynamic_index_in_dim(other, at, 2, False)
            rows = jnp.where(part // parts_core == core, mine, theirs)
            result.append(rows.reshape(clusters * count * rank_part, width))
        return result

    own_in, own_out = [gate_basis, up_basis], [down_basis]
    other_in = [core_swap(basis) for basis in own_in]
    other_out = [core_swap(basis) for basis in own_out]

    routing = x_half[:, width:]
    swapped = core_swap(routing)
    routing = jnp.stack(
        [jnp.where(core == 0, routing, swapped), jnp.where(core == 0, swapped, routing)]
    )
    routing = routing.reshape(blocks, tok_rows, lanes)
    ids = routing[:, :, :top].astype(jnp.int32)
    weights = routing[:, :, top : 2 * top].astype(FL)
    own_ids = me_e * local + jnp.arange(local, dtype=jnp.int32)
    hit = ids[None] == own_ids[:, None, None, None]
    named = jnp.any(hit, axis=3)
    weight_of = jnp.sum(jnp.where(hit, weights[None], 0.0), axis=3)
    order = jnp.cumsum(named.astype(jnp.int32), axis=2) - 1
    cell = jnp.arange(blocks, dtype=jnp.int32)[None, :, None] * capacity + order
    cell = jnp.where(named, cell, -1).reshape(local, 1, total)
    weight_of = weight_of.reshape(local, 1, total)
    pick, slot_weight = make_picks(cell, weight_of, slots)

    group_cluster = cluster_of.reshape(n_ex, local)[:, 0]

    def sum_parts(got):
        return sum(piece.astype(FL) for piece in got).astype(BF)

    def spread(mine):
        return lax.all_to_all(mine, ("ez", "core"), split_axis=0, concat_axis=0, tiled=True)

    rows_in, terms = project(
        x_half, chip_rows(own_in, other_in), own_in, other_in, spot, n_dp
    )
    got_in = spread(
        sum_for_groups(
            trade(lambda k: terms[k], "dp"), group_cluster, clusters, 2, [dy_half, pick]
        )
    )
    _, terms_out = project(
        dy_half, chip_rows(own_out, other_out), own_out, other_out, spot, n_dp
    )
    h_pieces = trade(lambda k: got_in, "dp")
    got_out = spread(
        sum_for_groups(
            trade(lambda k: terms_out[k], "dp"), group_cluster, clusters, 1, []
        )
    )
    (hg, hu, hidden, mixed, act, lift), mixed_chunks = forward(
        h_pieces, pick, weight_of, gate_factor, up_factor, down_factor, dp
    )
    held_out = hold(got_out, h_pieces[1:])
    d_pieces = trade(lambda k: held_out, "dp")
    (back, grad_gate, grad_up, dots), in_chunks = backward(
        d_pieces, pick, slot_weight, mixed, act, lift, gate_factor, up_factor, down_factor, dp
    )

    numbers = jnp.arange(clusters, dtype=jnp.int32)[:, None]

    def by_cluster(got, groups):
        owner = (groups[None, :] == numbers)[:, :, None, None]
        summed = jnp.sum(jnp.where(owner, got.astype(FL)[None], 0.0), axis=1)
        return summed.astype(BF).reshape(-1, half)

    mixed_mine = sum_parts(trade(lambda k: mixed_chunks[k], "dp"))
    in_mine = sum_parts(trade(lambda k: in_chunks[k], "dp"))
    grad_gate_factor, grad_up_factor, grad_down_factor = factor_grads(
        hg, grad_gate, hu, grad_up, hidden, back, total, in_mine
    )
    mine = jnp.concatenate([in_mine, mixed_mine], axis=1)
    got = spread(mine)
    in_sum = after(by_cluster(got[:, : 2 * rank_part], group_cluster), grad_gate_factor)
    mixed_sum = by_cluster(got[:, 2 * rank_part :], group_cluster)
    in_parts = trade(lambda k: in_sum, "dp")

    placed = cell == jnp.arange(slots, dtype=jnp.int32)[None, :, None]
    scores = jnp.sum(jnp.where(placed, dots, 0.0), axis=1).reshape(local, 2, half)
    mine = jnp.where(core == 0, scores[:, 0], scores[:, 1])
    theirs = core_swap(jnp.where(core == 0, scores[:, 1], scores[:, 0]))
    first = jnp.where(core == 0, mine, theirs)
    second = jnp.where(core == 0, theirs, mine)
    scores = jnp.concatenate([first, second], axis=0).T.astype(BF)
    scores = jnp.pad(scores, ((0, 0), (0, lanes - 2 * local)))

    grad_x = sum(mm("rt,rf->tf", part, rows) for part, rows in zip(in_parts, rows_in))
    leaving = jnp.concatenate([grad_x.astype(BF), scores], axis=1)
    rows = leaving.reshape(n_dp * n_z, tok_rows, width + lanes)
    rows = lax.all_to_all(rows, ("dp", "ez"), split_axis=0, concat_axis=0, tiled=True)
    rows = rows.reshape(n_dp, n_z, tok_rows, width + lanes)
    x_other = core_swap(x_half)
    dy_other = core_swap(dy_half)
    same = core == dp // parts_core

    def own_ranks(parts):
        near, far = parts[:parts_core], parts[parts_core:]
        keep = [jnp.where(same, a, b) for a, b in zip(near, far)]
        other = [core_swap(jnp.where(same, b, a)) for a, b in zip(near, far)]
        return keep, other

    shape = (clusters, rank_own, width)
    grad_gate_basis, grad_up_basis = basis_grads(
        *own_ranks(in_parts), x_half, x_other, spot, shape, n_dp, leaving
    )
    mixed_sum = after(mixed_sum, grad_gate_basis)
    mixed_parts = trade(lambda k: mixed_sum, "dp")
    (grad_down_basis,) = basis_grads(
        *own_ranks(mixed_parts), dy_half, dy_other, spot, shape, n_dp, leaving
    )

    grad_rows = jnp.sum(rows[..., :width].astype(FL), axis=1)
    grad_rows = after(grad_rows, grad_down_basis)
    grad_tokens = grad_rows.astype(BF).transpose(1, 0, 2).reshape(tok_rows, model_width)
    by_expert = jnp.sum(rows[..., width : width + 2 * local].astype(FL), axis=0)
    by_expert = by_expert.transpose(1, 0, 2).reshape(tok_rows, 1, experts)
    chosen = route_ids[:, :, None] == jnp.arange(experts, dtype=jnp.int32)[None, None, :]
    grad_route = jnp.sum(jnp.where(chosen, by_expert, 0.0), axis=2)
    return (
        grad_tokens,
        grad_route,
        grad_gate_basis,
        grad_up_basis,
        grad_down_basis,
        grad_gate_factor,
        grad_up_factor,
        grad_down_factor,
    )


def solution(mesh):
    n_dp, n_ex = mesh.shape["dp"], mesh.shape["expert"]
    split = Mesh(mesh.devices.reshape(n_dp, n_ex // 2, 2), ("dp", "ez", "core"))
    ex = ("ez", "core")
    rows = P(("dp", "ez", "core"), None)
    basis = P(None, ex, "dp")
    in_specs = (
        rows,
        rows,
        rows,
        rows,
        P(),
        basis,
        basis,
        basis,
        P(ex, None, "dp"),
        P(ex, None, "dp"),
        P(ex, "dp", None),
    )
    out_specs = (
        rows,
        rows,
        basis,
        basis,
        basis,
        P(ex, None, "dp"),
        P(ex, None, "dp"),
        P(ex, "dp", None),
    )
    return jax.shard_map(body, mesh=split, in_specs=in_specs, out_specs=out_specs, check_vma=False)
```
